32 devices in a mesh: dp: 8 (over y, x, core), seq: 4 (over z).
Axes of the slice: x: 2, y: 2, z: 4, core: 2. Of those that a mesh axis runs over, the one named last changes fastest.
Arguments:
- layer_in: bfloat16 [32, 1024, 768], P('dp', 'seq'), may hold values from -6 to 6
- out_grad: bfloat16 [32, 1024, 768], P('dp', 'seq'), may hold values from -6 to 6
- norm_gain: float32 [768], P(('dp', 'seq')), may hold values from 0.1 to 1.9
- in_weight: float32 [768, 3352], P(('dp', 'seq')), may hold values from -0.21875 to 0.21875
- conv_params: float32 [5, 1792], P(None, ('dp', 'seq')), may hold values from -3 to 3
- gate_gain: float32 [1536], P(('dp', 'seq')), may hold values from 0.1 to 1.9
- out_weight: float32 [1536, 768], P(('dp', 'seq')), may hold values from -0.15625 to 0.15625
- head_params: float32 [3, 24], replicated, may hold values from -7 to 2.5, as said below
- norm_first: float32 [768], P(('dp', 'seq')), may hold values from -384 to 384
- norm_second: float32 [768], P(('dp', 'seq')), may hold values from 39321.6 to 163840
- in_first: float32 [768, 3352], P(('dp', 'seq')), may hold values from -192 to 192
- in_second: float32 [768, 3352], P(('dp', 'seq')), may hold values from 9830.4 to 40960
- conv_first: float32 [5, 1792], P(None, ('dp', 'seq')), may hold values from -192 to 192
- conv_second: float32 [5, 1792], P(None, ('dp', 'seq')), may hold values from 9830.4 to 40960
- gate_first: float32 [1536], P(('dp', 'seq')), may hold values from -256 to 256
- gate_second: float32 [1536], P(('dp', 'seq')), may hold values from 19660.8 to 81920
- out_first: float32 [1536, 768], P(('dp', 'seq')), may hold values from -384 to 384
- out_second: float32 [1536, 768], P(('dp', 'seq')), may hold values from 39321.6 to 163840
- head_first: float32 [3, 24], replicated, may hold values from -1280 to 1280
- head_second: float32 [3, 24], replicated, may hold values from 655360 to 2621440
- step_count: int32 [1], replicated, may hold values from 1 to 3
- hyper: float32 [4], replicated, may hold values from 0.01 to 0.8, as said below
Outputs:
- layer_out: bfloat16 [32, 1024, 768], P('dp', 'seq')
- in_grad: float32 [32, 1024, 768], P('dp', 'seq')
- norm_step: float32 [768], P(('dp', 'seq'))
- norm_first_new: float32 [768], P(('dp', 'seq'))
- norm_second_new: float32 [768], P(('dp', 'seq'))
- in_new: float32 [768, 3352], P(('dp', 'seq'))
- in_first_new: float32 [768, 3352], P(('dp', 'seq'))
- in_second_new: float32 [768, 3352], P(('dp', 'seq'))
- conv_step: float32 [5, 1792], P(None, ('dp', 'seq'))
- conv_first_new: float32 [5, 1792], P(None, ('dp', 'seq'))
- conv_second_new: float32 [5, 1792], P(None, ('dp', 'seq'))
- gate_step: float32 [1536], P(('dp', 'seq'))
- gate_first_new: float32 [1536], P(('dp', 'seq'))
- gate_second_new: float32 [1536], P(('dp', 'seq'))
- out_new: float32 [1536, 768], P(('dp', 'seq'))
- out_first_new: float32 [1536, 768], P(('dp', 'seq'))
- out_second_new: float32 [1536, 768], P(('dp', 'seq'))
- head_step: float32 [3, 24], replicated
- head_first_new: float32 [3, 24], replicated
- head_second_new: float32 [3, 24], replicated
- in_copy: bfloat16 [768, 3352], P(('dp', 'seq'))
- out_copy: bfloat16 [1536, 768], P(('dp', 'seq'))
The draws below stay inside these ranges and needn't reach their ends.
Inputs may be any that keep to these rules, and one draw needn't show every extreme that they name: `head_params`: rows: step bias in -7 to -3, log of the decay rate in 0 to 2.5, skip gain in -1 to 1. `hyper`: learning rate 0.01 to 0.03, beta one 0.7 to 0.8, beta two 0.4 to 0.5, weight decay 0.05 to 0.2.
All inputs are finite; a program needn't handle non-finite values.
Results may differ from the reference program's by a relative error of at most 0.012.
The reference program's roundings to bfloat16 on the way count: a program that leaves them out, or rounds other values in their place, can miss the bound.
Values may be sent and summed in bfloat16 or wider, within the bound.
No kernel may reach another device: no remote copies, remote signals or barrier semaphores. Data moves between devices by JAX's collectives and lax.ppermute only.
A program may use at most 192 MiB of HBM per device.

```python
import math
import jax
import jax.numpy as jnp
from jax import lax

D = 768
HEADS = 24
STATE = 128
CONV = 4
GROUP = 256
INNER = 1536
CONVDIM = 1792
PROJ = 3352
LENGTH = 1024
SEQS = 32


def draw_head_params(key, part):
    key_step, key_decay, key_skip = jax.random.split(key, 3)
    step_bias = jax.random.uniform(key_step, (HEADS,), jnp.float32, -7.0, -3.0)
    decay_log = jax.random.uniform(key_decay, (HEADS,), jnp.float32, 0.0, 2.5)
    skip_gain = jax.random.uniform(key_skip, (HEADS,), jnp.float32, -1.0, 1.0)
    return jnp.stack([step_bias, decay_log, skip_gain])


def draw_hyper(key, part):
    lower_ends = jnp.array([0.01, 0.7, 0.4, 0.05], jnp.float32)
    upper_ends = jnp.array([0.03, 0.8, 0.5, 0.2], jnp.float32)
    return lower_ends + (upper_ends - lower_ends) * jax.random.uniform(key, (4,), jnp.float32)


def levels(stream_key, extent, cuts, low, high):
    gain = 1.0
    for axis_at, shards_of in cuts:
        heights = jax.random.uniform(jax.random.fold_in(jax.random.fold_in(stream_key, 6), axis_at), (shards_of,), jnp.float32, low / len(cuts), high / len(cuts))
        gain = gain * jnp.repeat(jnp.exp(heights), extent[axis_at] // shards_of).reshape((-1,) + (1,) * (len(extent) - 1 - axis_at))
    return gain


def noise(key, extent, spread, reach, cuts=(), kind=jnp.bfloat16):
    drawn = jax.random.normal(key, extent, jnp.float32) * spread
    if len(cuts) > 0:
        drawn = levels(key, extent, cuts, -0.22, 0.18) * drawn
    return jnp.clip(drawn, min=-reach, max=reach).astype(kind)


def setup_inputs(seed: int = 0) -> dict:
    splits = jax.random.split(jax.random.key(seed), 23)
    layer_in = noise(splits[0], (SEQS, LENGTH, D), 1.0, 6.0, ((0, 8), (1, 4)))
    out_grad = noise(splits[1], (SEQS, LENGTH, D), 1.0, 6.0, ((0, 8), (1, 4)))
    norm_gain = jnp.clip(1.0 + 0.18 * jax.random.normal(splits[2], (D,), jnp.float32), 0.1, 1.9)
    in_weight = noise(splits[3], (D, PROJ), D ** -0.5, 0.21875, ((0, 32),), jnp.float32)
    conv_params = noise(splits[4], (CONV + 1, CONVDIM), 0.5, 3.0, ((1, 32),), jnp.float32)
    gate_gain = jnp.clip(1.0 + 0.18 * jax.random.normal(splits[5], (INNER,), jnp.float32), 0.1, 1.9)
    out_weight = noise(splits[6], (INNER, D), INNER ** -0.5, 0.15625, ((0, 32),), jnp.float32)
    head_params = draw_head_params(jax.random.fold_in(splits[22], 71), 0)
    norm_first = noise(splits[8], (D,), (0.33 * (SEQS * LENGTH) ** 0.5), 384.0, ((0, 32),), jnp.float32)
    norm_second = jnp.clip(jnp.exp(math.log(163840.0) - 1.4271163 * jax.random.uniform(splits[9], (D,), jnp.float32) ** levels(splits[9], (D,), ((0, 32),), -0.2, 0.2)), 39321.6, 163840.0)
    in_first = noise(splits[10], (D, PROJ), (0.17 * (SEQS * LENGTH) ** 0.5), 192.0, ((0, 32),), jnp.float32)
    in_second = jnp.clip(jnp.exp(math.log(40960.0) - 1.4271163 * jax.random.uniform(splits[11], (D, PROJ), jnp.float32) ** levels(splits[11], (D, PROJ), ((0, 32),), -0.2, 0.2)), 9830.4, 40960.0)
    conv_first = noise(splits[12], (CONV + 1, CONVDIM), (0.17 * (SEQS * LENGTH) ** 0.5), 192.0, ((1, 32),), jnp.float32)
    conv_second = jnp.clip(jnp.exp(math.log(40960.0) - 1.4271163 * jax.random.uniform(splits[13], (CONV + 1, CONVDIM), jnp.float32) ** levels(splits[13], (CONV + 1, CONVDIM), ((1, 32),), -0.2, 0.2)), 9830.4, 40960.0)
    gate_first = noise(splits[14], (INNER,), (0.23 * (SEQS * LENGTH) ** 0.5), 256.0, ((0, 32),), jnp.float32)
    gate_second = jnp.clip(jnp.exp(math.log(81920.0) - 1.4271163 * jax.random.uniform(splits[15], (INNER,), jnp.float32) ** levels(splits[15], (INNER,), ((0, 32),), -0.2, 0.2)), 19660.8, 81920.0)
    out_first = noise(splits[16], (INNER, D), (0.33 * (SEQS * LENGTH) ** 0.5), 384.0, ((0, 32),), jnp.float32)
    out_second = jnp.clip(jnp.exp(math.log(163840.0) - 1.4271163 * jax.random.uniform(splits[17], (INNER, D), jnp.float32) ** levels(splits[17], (INNER, D), ((0, 32),), -0.2, 0.2)), 39321.6, 163840.0)
    head_first = noise(splits[18], (3, HEADS), (1.3 * (SEQS * LENGTH) ** 0.5), 1280.0, (), jnp.float32)
    head_second = jnp.clip(jnp.exp(jax.random.uniform(splits[19], (3, HEADS), jnp.float32, math.log(655360.0), math.log(2621440))), 655360.0, 2621440)
    step_count = jax.random.randint(splits[20], (1,), 1, 4).astype(jnp.int32)
    hyper = draw_hyper(jax.random.fold_in(splits[22], 71), 0)
    return dict(layer_in=layer_in, out_grad=out_grad, norm_gain=norm_gain, in_weight=in_weight, conv_params=conv_params, gate_gain=gate_gain, out_weight=out_weight, head_params=head_params, norm_first=norm_first, norm_second=norm_second, in_first=in_first, in_second=in_second, conv_first=conv_first, conv_second=conv_second, gate_first=gate_first, gate_second=gate_second, out_first=out_first, out_second=out_second, head_first=head_first, head_second=head_second, step_count=step_count, hyper=hyper)


@jax.custom_vjp
def low(v):
    return lax.optimization_barrier(v.astype(jnp.bfloat16)).astype(jnp.float32)

@jax.custom_vjp
def low_back(v):
    return v

def low_keep(v):
    return (low(v), None)

def low_pass(kept, grad):
    return (grad,)

def back_keep(v):
    return (v, None)

def back_low(kept, grad):
    return (low(grad),)
low.defvjp(low_keep, low_pass)
low_back.defvjp(back_keep, back_low)
norm_eps = 1e-05
adam_eps = 1e-08
highest = lax.Precision.HIGHEST

def exact_dot(left, right):
    return jnp.dot(left, right, precision=highest, preferred_element_type=jnp.float32)

def spread_heads(decay, width):
    return jnp.repeat(decay, width // decay.shape[-1], axis=-1)[..., None]

def conv_silu(extended, conv):
    tap_count = conv.shape[0] - 1
    out_rows = extended.shape[-2] - (tap_count - 1)
    summed = conv[tap_count]
    for offset in range(tap_count):
        summed = summed + conv[offset] * extended[..., offset:offset + out_rows, :]
    return jax.nn.silu(summed)

def group_local(mixed, dt_raw, head, inner_dim):
    state_dim = (mixed.shape[-1] - inner_dim) // 2
    value_rows = mixed[:, :inner_dim]
    key_rows = mixed[:, inner_dim:inner_dim + state_dim]
    query_rows = mixed[:, inner_dim + state_dim:]
    dt_steps = jax.nn.softplus(dt_raw + head[0])
    log_decay = dt_steps * -jnp.exp(head[1])
    length = mixed.shape[0]
    lower_mask = (jnp.arange(length)[:, None] >= jnp.arange(length)[None, :]).astype(mixed.dtype)
    cum_decay = exact_dot(lower_mask, log_decay)
    return (value_rows, key_rows, query_rows, dt_steps, cum_decay)

def group_state(value_rows, key_rows, dt_steps, cum_decay):
    head_size = value_rows.shape[1] // dt_steps.shape[1]
    tail_weight = jnp.exp(cum_decay[-1][None, :] - cum_decay) * dt_steps
    weighted = value_rows * jnp.repeat(tail_weight, head_size, axis=1)
    state_loc = exact_dot(weighted.T, key_rows)
    return (state_loc, jnp.exp(cum_decay[-1]))

def group_tail(value_rows, key_rows, query_rows, dt_steps, cum_decay, state_in, gate_rows, head, gate_gain):
    length, inner_dim = value_rows.shape
    head_count = dt_steps.shape[1]
    head_size = inner_dim // head_count
    scores = exact_dot(query_rows, key_rows.T)
    lower_mask = jnp.arange(length)[:, None] >= jnp.arange(length)[None, :]
    cum_heads = cum_decay.T
    decay_gaps = cum_heads[:, :, None] - cum_heads[:, None, :]
    zero_gap = jnp.zeros_like(decay_gaps)
    decays = jnp.where(lower_mask, jnp.exp(jnp.where(lower_mask, decay_gaps, zero_gap)), zero_gap)
    mixing = decays * scores[None] * dt_steps.T[:, None, :]
    per_head = value_rows.reshape(length, head_count, head_size)
    diag_out = jnp.einsum('hts,shp->thp', mixing, per_head, precision=highest).reshape(length, inner_dim)
    carried = exact_dot(query_rows, state_in.T) * jnp.repeat(jnp.exp(cum_decay), head_size, axis=1)
    skip_out = value_rows * jnp.repeat(head[2], head_size)
    mixed_out = diag_out + carried + skip_out
    gated_rows = mixed_out * jax.nn.silu(gate_rows)
    inv_rms = lax.rsqrt(lax.optimization_barrier(jnp.mean(gated_rows * gated_rows, axis=-1, keepdims=True)) + norm_eps)
    return gated_rows * inv_rms * gate_gain

def sequence_forward(seq_rows, norm_w, in_w, conv_w, gate_w, out_w, head_w):
    normed = seq_rows * lax.rsqrt(lax.optimization_barrier(jnp.mean(seq_rows * seq_rows, axis=-1, keepdims=True)) + norm_eps) * norm_w
    projected = low_back(exact_dot(low(normed), in_w))
    gate_rows = projected[:, :INNER]
    conv_input = projected[:, INNER:INNER + CONVDIM]
    dt_raw = projected[:, INNER + CONVDIM:]
    extended = jnp.concatenate([jnp.zeros((CONV - 1, CONVDIM), conv_input.dtype), conv_input], axis=0)
    mixed = conv_silu(extended, conv_w)
    group_count = LENGTH // GROUP
    blocks = (mixed.reshape(group_count, GROUP, CONVDIM), dt_raw.reshape(group_count, GROUP, HEADS), gate_rows.reshape(group_count, GROUP, INNER))

    def group_step(state_now, block):
        mixed_blk, dt_blk, gate_blk = block
        value_rows, key_rows, query_rows, dt_steps, cum_decay = group_local(mixed_blk, dt_blk, head_w, INNER)
        normed_out = group_tail(value_rows, key_rows, query_rows, dt_steps, cum_decay, state_now, gate_blk, head_w, gate_w)
        state_loc, decay_tot = group_state(value_rows, key_rows, dt_steps, cum_decay)
        return (spread_heads(decay_tot, INNER) * state_now + state_loc, normed_out)
    _, outs_all = lax.scan(jax.checkpoint(group_step), jnp.zeros((INNER, STATE), mixed.dtype), blocks)
    branch = exact_dot(low(outs_all.reshape(LENGTH, INNER)), out_w)
    return seq_rows + branch

def adam_update(master, grad_sum, first_moment, second_moment, step_count, hyper):
    learn_rate, beta_one, beta_two, decay_rate = (hyper[0], hyper[1], hyper[2], hyper[3])
    step_float = step_count[0].astype(hyper.dtype)
    new_first = beta_one * first_moment + (1.0 - beta_one) * grad_sum
    new_second = beta_two * second_moment + (1.0 - beta_two) * grad_sum * grad_sum
    first_hat = new_first / (1.0 - beta_one ** step_float)
    second_hat = new_second / (1.0 - beta_two ** step_float)
    change = -learn_rate * (first_hat / (jnp.sqrt(second_hat) + adam_eps) + decay_rate * master)
    return (master + change, change, new_first, new_second)

def reference(layer_in, out_grad, norm_gain, in_weight, conv_params, gate_gain, out_weight, head_params, norm_first, norm_second, in_first, in_second, conv_first, conv_second, gate_first, gate_second, out_first, out_second, head_first, head_second, step_count, hyper):
    masters = (norm_gain, in_weight, conv_params, gate_gain, out_weight, head_params)

    def forward(tokens, params):
        norm_w = low(params[0])
        in_w = low(params[1])
        conv_w = low(params[2])
        gate_w = low(params[3])
        out_w = low(params[4])
        head_w = params[5]

        def one_sequence(seq_rows):
            return sequence_forward(seq_rows, norm_w, in_w, conv_w, gate_w, out_w, head_w)
        return lax.map(jax.checkpoint(one_sequence), tokens)
    tokens = layer_in.astype(jnp.float32)
    result, pull = jax.vjp(forward, tokens, masters)
    d_tokens, grads = pull(out_grad.astype(jnp.float32))
    firsts = (norm_first, in_first, conv_first, gate_first, out_first, head_first)
    seconds = (norm_second, in_second, conv_second, gate_second, out_second, head_second)
    updated = [adam_update(masters[index], grads[index], firsts[index], seconds[index], step_count, hyper) for index in range(6)]
    return (result.astype(jnp.bfloat16), d_tokens, updated[0][1], updated[0][2], updated[0][3], updated[1][0], updated[1][2], updated[1][3], updated[2][1], updated[2][2], updated[2][3], updated[3][1], updated[3][2], updated[3][3], updated[4][0], updated[4][2], updated[4][3], updated[5][1], updated[5][2], updated[5][3], updated[1][0].astype(jnp.bfloat16), updated[4][0].astype(jnp.bfloat16))
```

```python
import math
from functools import partial

import jax
import jax.numpy as jnp
import numpy as np
from jax import lax
from jax.experimental import pallas as pl
from jax.experimental.pallas import tpu as pltpu
from jax.sharding import PartitionSpec as P

norm_eps = 1e-05
adam_eps = 1e-08
log2e = math.log2(math.e)
lanes = 128
vmem_bytes = 56 * 1024 * 1024
f32 = jnp.float32
bf16 = jnp.bfloat16


def dot(left, right, left_dim=1, right_dim=0):
    return lax.dot_general(
        left, right, (((left_dim,), (right_dim,)), ((), ())), preferred_element_type=f32
    )


def halves(value):
    high = value.astype(bf16)
    return high, (value - high.astype(f32)).astype(bf16)


def sigmoid(value):
    return 1.0 / (1.0 + jnp.exp(-value))


def column(ref_value, at, width):
    return jnp.broadcast_to(ref_value[:, at : at + 1], (ref_value.shape[0], width))


def pair_columns(value, pair, low_lane):
    rows = value.shape[0]
    first = column(value, 2 * pair, lanes)
    second = column(value, 2 * pair + 1, lanes)
    return jnp.where(low_lane, first, second), first, second


def tri_sum(mask, value, head_lane):
    high = value.astype(bf16).astype(f32)
    rest = value - high
    mid = rest.astype(bf16).astype(f32)
    low = rest - mid
    packed = high + pltpu.roll(mid, 32, 1) + pltpu.roll(low, 64, 1)
    summed = dot(mask, packed.astype(bf16))
    total = summed + pltpu.roll(summed, lanes - 32, 1) + pltpu.roll(summed, lanes - 64, 1)
    return jnp.where(head_lane, total, 0.0)


def conv_chunk(ext_ref, conv_ref, at, length, taps):
    summed = conv_ref[taps : taps + 1, at : at + lanes]
    base = 8 - (taps - 1)
    for tap in range(taps):
        summed = (
            summed
            + conv_ref[tap : tap + 1, at : at + lanes]
            * ext_ref[base + tap : base + tap + length, at : at + lanes]
        )
    return summed


def step_sizes(dt_raw, head_ref, head_lane):
    shifted = dt_raw + head_ref[0:1, :]
    steps = jnp.maximum(shifted, 0.0) + jnp.log1p(jnp.exp(-jnp.abs(shifted)))
    return jnp.where(head_lane, steps, 0.0), shifted


def fetch_weight(core_ref, own_ref, other_ref, whole_ref, sems):
    blocks, rows, _ = own_ref.shape
    core = core_ref[0]
    copies = []
    for block in range(blocks):
        for which, source in ((core, own_ref), (1 - core, other_ref)):
            at = pl.multiple_of((2 * block + which) * rows, rows)
            copies.append(
                pltpu.make_async_copy(
                    source.at[block], whole_ref.at[pl.ds(at, rows)], sems.at[len(copies)]
                )
            )
    for copy in copies:
        copy.start()
    return copies


def hand_out(core, total_ref, send_ref, keep_ref):
    blocks, rows, _ = send_ref.shape
    for block in range(blocks):
        at = pl.multiple_of((2 * block + 1 - core) * rows, rows)
        send_ref[block] = total_ref[pl.ds(at, rows), :].astype(bf16)
        at = pl.multiple_of((2 * block + core) * rows, rows)
        keep_ref[block] = total_ref[pl.ds(at, rows), :]


def add_product(total_ref, left_ref, right):
    for at in range(0, total_ref.shape[0], 2 * lanes):
        here = slice(at, at + 2 * lanes)
        total_ref[here, :] += dot(left_ref[:, here], right, 0, 0)


def mixer_forward_kernel(
    core_ref,
    x_ref,
    edge_ref,
    wa_own,
    wa_other,
    wb_own,
    wb_other,
    conv_ref,
    head_ref,
    skip_ref,
    start_ref,
    normed_ref,
    ext_ref,
    dtr_ref,
    cum_ref,
    y_ref,
    sin_ref,
    end_ref,
    tail_ref,
    state_ref,
    carried_ref,
    weighted_ref,
    wa_ref,
    wb_ref,
    wa_sems,
    wb_sems,
    *,
    heads,
    inner,
    taps,
    grouped,
):
    block = pl.program_id(1)
    length, width = x_ref.shape

    @pl.when(jnp.logical_and(pl.program_id(0) == 0, block == 0))
    def _():
        copies = fetch_weight(core_ref, wa_own, wa_other, wa_ref, wa_sems)
        copies += fetch_weight(core_ref, wb_own, wb_other, wb_ref, wb_sems)
        for copy in copies:
            copy.wait()

    half = length // 2
    wide_a = wa_ref.shape[1]
    conv_dim = conv_ref.shape[1]
    state_dim = (conv_dim - inner) // 2

    def norm_of(rows):
        rows = rows.astype(f32)
        scale = lax.rsqrt(jnp.mean(rows * rows, axis=-1, keepdims=True) + norm_eps)
        return (rows * scale * conv_ref[taps + 1 : taps + 2, :width]).astype(bf16)

    @pl.when(block == 0)
    def _():
        if grouped:
            state_ref[...] = start_ref[...]
            edge = norm_of(edge_ref[...])
            tail_ref[:, :wide_a] = dot(edge, wa_ref[...])
            tail_ref[:, wide_a:] = dot(edge, wb_ref[...])[:, : conv_dim - wide_a]
        else:
            state_ref[...] = jnp.zeros_like(state_ref)
            tail_ref[...] = jnp.zeros_like(tail_ref)

    normed = norm_of(x_ref[...])
    normed_ref[...] = normed
    ext_ref[0:8, :] = tail_ref[...]
    ext_ref[8 : 8 + length, :wide_a] = dot(normed, wa_ref[...])
    second = dot(normed, wb_ref[...])
    ext_ref[8 : 8 + length, wide_a:] = second[:, : conv_dim - wide_a]
    dt_raw = second[:, conv_dim - wide_a :]
    tail_ref[...] = ext_ref[length : length + 8, :]

    lane = lax.broadcasted_iota(jnp.int32, (length, lanes), 1)
    low_lane = lane < lanes // 2
    head_lane = lane < heads
    dtr_ref[...] = dt_raw
    steps, _ = step_sizes(dt_raw, head_ref, head_lane)
    log_decay = steps * (-log2e * jnp.exp(head_ref[1:2, :]))
    row = lax.broadcasted_iota(jnp.int32, (length, length), 0)
    col = lax.broadcasted_iota(jnp.int32, (length, length), 1)
    cum = tri_sum((row >= col).astype(bf16), log_decay, head_lane)
    cum_ref[...] = cum
    cum_rows = cum.T

    def mixed_chunk(at):
        summed = conv_chunk(ext_ref, conv_ref, at, length, taps)
        return summed * sigmoid(summed)

    keys = jnp.concatenate(
        [mixed_chunk(inner + at) for at in range(0, state_dim, lanes)], axis=1
    ).astype(bf16)
    queries = jnp.concatenate(
        [mixed_chunk(inner + state_dim + at) for at in range(0, state_dim, lanes)], axis=1
    ).astype(bf16)
    state_low = state_ref[...].astype(bf16)
    sin_ref[...] = state_low
    carried_ref[...] = dot(queries, state_low)
    square = (half, half)
    diag = lax.broadcasted_iota(jnp.int32, square, 0) >= lax.broadcasted_iota(
        jnp.int32, square, 1
    )
    scores_00 = jnp.where(diag, dot(queries[:half], keys[:half], 1, 1), 0.0)
    scores_10 = dot(queries[half:], keys[:half], 1, 1)
    scores_11 = jnp.where(diag, dot(queries[half:], keys[half:], 1, 1), 0.0)
    for pair in range(heads // 2):
        at = pair * lanes
        values = mixed_chunk(at)
        cum_rep, cum_0, cum_1 = pair_columns(cum, pair, low_lane)
        dt_rep, _, _ = pair_columns(steps, pair, low_lane)
        stepped = values * dt_rep
        last = cum_rep[length - 1 : length, :]
        weighted_ref[:, at : at + lanes] = (stepped * jnp.exp2(last - cum_rep)).astype(bf16)
        top = None
        bottom = None
        for which, cum_col in ((0, cum_0), (1, cum_1)):
            own = jnp.where(low_lane if which == 0 else jnp.logical_not(low_lane), stepped, 0.0)
            own = own.astype(bf16)
            head = 2 * pair + which
            early = cum_rows[head : head + 1, :half]
            late = cum_rows[head : head + 1, half:]
            mix_00 = jnp.exp2(jnp.minimum(cum_col[:half] - early, 0.0)) * scores_00
            mix_10 = jnp.exp2(jnp.minimum(cum_col[half:] - early, 0.0)) * scores_10
            mix_11 = jnp.exp2(jnp.minimum(cum_col[half:] - late, 0.0)) * scores_11
            part_top = dot(mix_00.astype(bf16), own[:half])
            part_bottom = dot(
                jnp.concatenate([mix_10.astype(bf16), mix_11.astype(bf16)], axis=1), own
            )
            top = part_top if top is None else top + part_top
            bottom = part_bottom if bottom is None else bottom + part_bottom
        rest = (
            jnp.exp2(cum_rep) * carried_ref[:, at : at + lanes]
            + skip_ref[0:1, at : at + lanes] * values
        )
        y_ref[0:half, at : at + lanes] = top + rest[:half]
        y_ref[half:length, at : at + lanes] = bottom + rest[half:]
        fresh = dot(keys, weighted_ref[:, at : at + lanes], 0, 0)
        state_ref[:, at : at + lanes] = jnp.exp2(last) * state_ref[:, at : at + lanes] + fresh

    @pl.when(block == pl.num_programs(1) - 1)
    def _():
        end_ref[...] = state_ref[...]


def gate_kernel(
    core_ref,
    normed_ref,
    x_ref,
    cot_ref,
    y_ref,
    wg_own,
    wg_other,
    wo_own,
    wo_other,
    small_ref,
    out_ref,
    dy_ref,
    dgate_ref,
    dgain_ref,
    out_send,
    out_keep,
    gate_send,
    gate_keep,
    gate_ref,
    dno_ref,
    low_ref,
    out_sum,
    gate_sum,
    wg_ref,
    wo_ref,
    wg_sems,
    wo_sems,
    *,
    gain_row,
):
    length, inner = y_ref.shape
    first = jnp.logical_and(pl.program_id(0) == 0, pl.program_id(1) == 0)

    @pl.when(first)
    def _():
        copies = fetch_weight(core_ref, wg_own, wg_other, wg_ref, wg_sems)
        copies += fetch_weight(core_ref, wo_own, wo_other, wo_ref, wo_sems)
        dgain_ref[...] = jnp.zeros_like(dgain_ref)
        out_sum[...] = jnp.zeros_like(out_sum)
        gate_sum[...] = jnp.zeros_like(gate_sum)
        for copy in copies:
            copy.wait()

    gate_ref[...] = dot(normed_ref[...], wg_ref[...])
    dno_ref[...] = dot(cot_ref[...], wo_ref[...], 1, 1)
    squares = jnp.zeros((length, lanes), f32)
    crosses = jnp.zeros((length, lanes), f32)
    for at in range(0, inner, lanes):
        here = slice(at, at + lanes)
        gate = gate_ref[:, here]
        gated = y_ref[:, here] * (gate * sigmoid(gate))
        squares = squares + gated * gated
        crosses = crosses + gated * (small_ref[gain_row : gain_row + 1, here] * dno_ref[:, here])
    scale = lax.rsqrt(jnp.sum(squares, axis=1, keepdims=True) * (1.0 / inner) + norm_eps)
    cross = scale * scale * scale * (jnp.sum(crosses, axis=1, keepdims=True) * (1.0 / inner))
    scale_b = jnp.broadcast_to(scale, (length, lanes))
    cross_b = jnp.broadcast_to(cross, (length, lanes))
    for at in range(0, inner, lanes):
        here = slice(at, at + lanes)
        gate = gate_ref[:, here]
        mixed_out = y_ref[:, here]
        sig = sigmoid(gate)
        silu = gate * sig
        gated = mixed_out * silu
        scaled = gated * scale_b
        d_out = dno_ref[:, here]
        low_ref[:, here] = (scaled * small_ref[gain_row : gain_row + 1, here]).astype(bf16)
        dgain_ref[0:1, here] += jnp.sum(scaled * d_out, axis=0, keepdims=True)
        d_gated = scale_b * (small_ref[gain_row : gain_row + 1, here] * d_out) - gated * cross_b
        dy_ref[:, here] = (d_gated * silu).astype(bf16)
        dgate_ref[:, here] = (d_gated * mixed_out * (sig * (1.0 + gate * (1.0 - sig)))).astype(
            bf16
        )
    out_ref[...] = (x_ref[...].astype(f32) + dot(low_ref[...], wo_ref[...])).astype(bf16)
    add_product(out_sum, low_ref, cot_ref[...])
    add_product(gate_sum, normed_ref, dgate_ref[...])
    last = jnp.logical_and(
        pl.program_id(0) == pl.num_programs(0) - 1, pl.program_id(1) == pl.num_programs(1) - 1
    )

    @pl.when(last)
    def _():
        hand_out(core_ref[0], out_sum, out_send, out_keep)
        hand_out(core_ref[0], gate_sum, gate_send, gate_keep)


def mixer_backward_kernel(
    ext_ref,
    dtr_ref,
    cum_ref,
    y_ref,
    sin_ref,
    dy_ref,
    conv_ref,
    head_ref,
    skip_ref,
    sum_ref,
    start_ref,
    next_ref,
    small_in_ref,
    dgain_ref,
    _,
    dproj_ref,
    dconv_ref,
    end_ref,
    lead_ref,
    grad_ref,
    dsx_ref,
    dwv_ref,
    dye_ref,
    weighted_ref,
    zhigh_ref,
    zlow_ref,
    direct_ref,
    rows_ref,
    *,
    heads,
    inner,
    taps,
    fresh,
):
    step = pl.program_id(1)
    length = dy_ref.shape[0]
    half = length // 2
    conv_dim = conv_ref.shape[1]
    state_dim = (conv_dim - inner) // 2
    first = jnp.logical_and(pl.program_id(0) == 0, step == 0)

    @pl.when(first)
    def _():
        if small_in_ref.shape == dconv_ref.shape:
            dconv_ref[...] = small_in_ref[...]
        else:
            dconv_ref[...] = jnp.zeros_like(dconv_ref)
            dconv_ref[taps + 2 : taps + 3, :inner] = dgain_ref[0:1, :]
        rows_ref[...] = jnp.zeros_like(rows_ref)

    @pl.when(step == 0)
    def _():
        if fresh:
            grad_ref[...] = jnp.zeros_like(grad_ref)
            dsx_ref[length : length + 8, :] = jnp.zeros((8, conv_dim), f32)
        else:
            grad_ref[...] = start_ref[...]
            dsx_ref[length : length + 8, :] = next_ref[...]

    @pl.when(step > 0)
    def _():
        dsx_ref[length : length + 8, :] = dsx_ref[0:8, :]

    lane = lax.broadcasted_iota(jnp.int32, (length, lanes), 1)
    low_lane = lane < lanes // 2
    head_lane = lane < heads
    steps, shifted = step_sizes(dtr_ref[...], head_ref, head_lane)
    cum = cum_ref[...]
    cum_rows = cum.T

    def slope_chunk(at):
        summed = conv_chunk(ext_ref, conv_ref, at, length, taps)
        sig = sigmoid(summed)
        return summed * sig, sig * (1.0 + summed * (1.0 - sig))

    def put_grad(at, d_summed):
        here = slice(at, at + lanes)
        dsx_ref[0:length, here] = d_summed
        total = None
        for tap in range(taps):
            base = 8 - (taps - 1) + tap
            dconv_ref[tap : tap + 1, here] += jnp.sum(
                d_summed * ext_ref[base : base + length, here], axis=0, keepdims=True
            )
            back = taps - 1 - tap
            term = conv_ref[tap : tap + 1, here] * dsx_ref[back : back + length, here]
            total = term if total is None else total + term
        dconv_ref[taps : taps + 1, here] += jnp.sum(d_summed, axis=0, keepdims=True)
        dproj_ref[:, here] = total.astype(bf16)

    parts = [slope_chunk(inner + at) for at in range(0, 2 * state_dim, lanes)]
    count = state_dim // lanes
    keys = jnp.concatenate([part[0] for part in parts[:count]], axis=1).astype(bf16)
    queries = jnp.concatenate([part[0] for part in parts[count:]], axis=1).astype(bf16)
    grad_low = grad_ref[...].astype(bf16)
    dwv_ref[...] = dot(keys, grad_low)
    square = (half, half)
    diag = lax.broadcasted_iota(jnp.int32, square, 0) <= lax.broadcasted_iota(
        jnp.int32, square, 1
    )
    scores_00 = jnp.where(diag, dot(keys[:half], queries[:half], 1, 1), 0.0)
    scores_01 = dot(keys[:half], queries[half:], 1, 1)
    scores_11 = jnp.where(diag, dot(keys[half:], queries[half:], 1, 1), 0.0)
    ds_00 = jnp.zeros(square, f32)
    ds_01 = jnp.zeros(square, f32)
    ds_11 = jnp.zeros(square, f32)
    for pair in range(heads // 2):
        at = pair * lanes
        here = slice(at, at + lanes)
        values, slope = slope_chunk(at)
        cum_rep, cum_0, cum_1 = pair_columns(cum, pair, low_lane)
        dt_rep, _, _ = pair_columns(steps, pair, low_lane)
        stepped = (values * dt_rep).astype(bf16)
        stepped_f = stepped.astype(f32)
        last = cum_rep[length - 1 : length, :]
        tail = jnp.exp2(last - cum_rep)
        d_y = dy_ref[:, here]
        d_yf = d_y.astype(f32)
        dye_ref[:, here] = (d_yf * jnp.exp2(cum_rep)).astype(bf16)
        top = None
        bottom = None
        for which, cum_col in ((0, cum_0), (1, cum_1)):
            own_lane = low_lane if which == 0 else jnp.logical_not(low_lane)
            own_dy = jnp.where(own_lane, d_yf, 0.0).astype(bf16)
            own_x = jnp.where(own_lane, stepped_f, 0.0).astype(bf16)
            head = 2 * pair + which
            early = cum_rows[head : head + 1, :half]
            late = cum_rows[head : head + 1, half:]
            decay_00 = jnp.exp2(jnp.minimum(early - cum_col[:half], 0.0))
            decay_01 = jnp.exp2(jnp.minimum(late - cum_col[:half], 0.0))
            decay_11 = jnp.exp2(jnp.minimum(late - cum_col[half:], 0.0))
            mix_0 = jnp.concatenate(
                [(decay_00 * scores_00).astype(bf16), (decay_01 * scores_01).astype(bf16)], axis=1
            )
            mix_1 = (decay_11 * scores_11).astype(bf16)
            part_top = dot(mix_0, own_dy)
            part_bottom = dot(mix_1, own_dy[half:])
            top = part_top if top is None else top + part_top
            bottom = part_bottom if bottom is None else bottom + part_bottom
            d_mix_0 = dot(own_x[:half], d_y, 1, 1)
            d_mix_1 = dot(own_x[half:], d_y[half:], 1, 1)
            ds_00 = ds_00 + decay_00 * d_mix_0[:, :half]
            ds_01 = ds_01 + decay_01 * d_mix_0[:, half:]
            ds_11 = ds_11 + decay_11 * d_mix_1
        d_diag = jnp.concatenate([top, bottom], axis=0)
        weighted = (stepped_f * tail).astype(bf16)
        weighted_ref[:, here] = weighted
        d_weighted = dwv_ref[:, here]
        through = weighted.astype(f32) * d_weighted
        d_stepped = d_diag + tail * d_weighted
        skip = skip_ref[0:1, here]
        z = d_yf * (y_ref[:, here] - skip * values) - stepped_f * d_diag - through
        z_high, z_low = halves(z)
        zhigh_ref[:, here] = z_high
        zlow_ref[:, here] = z_low
        direct_ref[:, here] = (d_stepped * values).astype(bf16)
        total_decay = jnp.exp2(last)
        rows_ref[0:1, here] = jnp.sum(through, axis=0, keepdims=True) + total_decay * jnp.sum(
            grad_ref[:, here] * sin_ref[:, here].astype(f32), axis=0, keepdims=True
        )
        rows_ref[1:2, here] = jnp.sum(d_yf * values, axis=0, keepdims=True)
        put_grad(at, (d_stepped * dt_rep + skip * d_yf) * slope)
        grad_ref[:, here] = total_decay * grad_ref[:, here] + dot(
            queries, dye_ref[:, here], 0, 0
        )

    ds_00 = jnp.where(diag, ds_00, 0.0).astype(bf16)
    ds_11 = jnp.where(diag, ds_11, 0.0).astype(bf16)
    ds_01 = ds_01.astype(bf16)
    d_queries = dot(dye_ref[...], sin_ref[...], 1, 1)
    d_keys = dot(weighted_ref[...], grad_low, 1, 1)
    d_queries = d_queries + jnp.concatenate(
        [
            dot(ds_00, keys[:half], 0, 0),
            dot(ds_01, keys[:half], 0, 0) + dot(ds_11, keys[half:], 0, 0),
        ],
        axis=0,
    )
    d_keys = d_keys + jnp.concatenate(
        [
            dot(ds_00, queries[:half]) + dot(ds_01, queries[half:]),
            dot(ds_11, queries[half:]),
        ],
        axis=0,
    )
    for at in range(0, state_dim, lanes):
        put_grad(inner + at, d_keys[:, at : at + lanes] * parts[at // lanes][1])
        put_grad(
            inner + state_dim + at,
            d_queries[:, at : at + lanes] * parts[count + at // lanes][1],
        )
    summing = sum_ref[...]
    rows_high, rows_low = halves(rows_ref[...])
    row_sums = dot(rows_high, summing) + dot(rows_low, summing)
    d_cum = dot(zhigh_ref[...], summing) + dot(zlow_ref[...], summing)
    at_last = lax.broadcasted_iota(jnp.int32, (length, lanes), 0) == length - 1
    d_cum = d_cum + jnp.where(at_last, row_sums[0:1, :], 0.0)
    row = lax.broadcasted_iota(jnp.int32, (length, length), 0)
    col = lax.broadcasted_iota(jnp.int32, (length, length), 1)
    d_log = tri_sum((row <= col).astype(bf16), d_cum, head_lane)
    rate = jnp.exp(head_ref[1:2, :])
    d_steps = dot(direct_ref[...], summing) - rate * d_log
    d_raw = jnp.where(head_lane, d_steps * sigmoid(shifted), 0.0)
    dproj_ref[:, conv_dim : conv_dim + lanes] = d_raw.astype(bf16)
    head_row = slice(taps + 3, taps + 4)
    dconv_ref[head_row, :lanes] += jnp.sum(d_raw, axis=0, keepdims=True)
    dconv_ref[head_row, lanes : 2 * lanes] += jnp.sum(d_log * steps, axis=0, keepdims=True) * (
        -rate
    )
    dconv_ref[head_row, 2 * lanes : 3 * lanes] += row_sums[1:2, :]

    @pl.when(step == pl.num_programs(1) - 1)
    def _():
        end_ref[...] = grad_ref[...]
        lead_ref[...] = dsx_ref[0:8, :]


def input_grad_kernel(
    core_ref,
    x_ref,
    dgate_ref,
    dproj_ref,
    small_ref,
    wg_own,
    wg_other,
    wa_own,
    wa_other,
    wb_own,
    wb_other,
    dx_ref,
    dsmall_ref,
    a_send,
    a_keep,
    b_send,
    b_keep,
    normed_ref,
    a_sum,
    b_sum,
    wg_ref,
    wa_ref,
    wb_ref,
    wg_sems,
    wa_sems,
    wb_sems,
    *,
    gain_row,
):
    first = jnp.logical_and(pl.program_id(0) == 0, pl.program_id(1) == 0)
    width = x_ref.shape[1]

    @pl.when(first)
    def _():
        copies = fetch_weight(core_ref, wg_own, wg_other, wg_ref, wg_sems)
        copies += fetch_weight(core_ref, wa_own, wa_other, wa_ref, wa_sems)
        copies += fetch_weight(core_ref, wb_own, wb_other, wb_ref, wb_sems)
        dsmall_ref[...] = jnp.zeros_like(dsmall_ref)
        a_sum[...] = jnp.zeros_like(a_sum)
        b_sum[...] = jnp.zeros_like(b_sum)
        for copy in copies:
            copy.wait()

    wide_a = wa_ref.shape[1]
    d_normed = (
        dot(dgate_ref[...], wg_ref[...], 1, 1)
        + dot(dproj_ref[:, :wide_a], wa_ref[...], 1, 1)
        + dot(dproj_ref[:, wide_a:], wb_ref[...], 1, 1)
    )
    rows = x_ref[...].astype(f32)
    scale = lax.rsqrt(jnp.mean(rows * rows, axis=-1, keepdims=True) + norm_eps)
    scaled = rows * scale
    dsmall_ref[0:1, :] += jnp.sum(scaled * d_normed, axis=0, keepdims=True)
    gain = small_ref[gain_row : gain_row + 1, :width]
    normed_ref[...] = (scaled * gain).astype(bf16)
    add_product(a_sum, normed_ref, dproj_ref[:, :wide_a])
    add_product(b_sum, normed_ref, dproj_ref[:, wide_a:])
    inner_grad = gain * d_normed
    cross = jnp.mean(scaled * inner_grad, axis=-1, keepdims=True)
    dx_ref[...] = (scale * (inner_grad - scaled * cross)).astype(bf16)
    last = jnp.logical_and(
        pl.program_id(0) == pl.num_programs(0) - 1, pl.program_id(1) == pl.num_programs(1) - 1
    )

    @pl.when(last)
    def _():
        hand_out(core_ref[0], a_sum, a_send, a_keep)
        hand_out(core_ref[0], b_sum, b_send, b_keep)


def adam_kernel(
    rates_ref,
    sums_ref,
    norm_ref,
    *refs,
    heads,
    taps,
    at_refs,
    arrivals,
):
    rest_refs, front_refs, refs = refs[:arrivals], refs[arrivals : 2 * arrivals], refs[2 * arrivals :]
    ins, outs = refs[:18], refs[18:]
    learn_rate, decay_rate = rates_ref[0], rates_ref[3]
    beta_one, beta_two = rates_ref[1], rates_ref[2]
    first_scale, second_scale = rates_ref[4], rates_ref[5]

    def update(which, grad, index):
        master, first, second = (ref[index] for ref in ins[3 * which : 3 * which + 3])
        new_first = beta_one * first + (1.0 - beta_one) * grad
        new_second = beta_two * second + (1.0 - beta_two) * grad * grad
        change = -learn_rate * (
            (new_first * first_scale) / (jnp.sqrt(new_second * second_scale) + adam_eps)
            + decay_rate * master
        )
        where = at_refs[which]
        outs[where][index] = master + change if which in (1, 4) else change
        outs[where + 1][index] = new_first
        outs[where + 2][index] = new_second
        if which in (1, 4):
            outs[-2 if which == 1 else -1][index] = (master + change).astype(bf16)

    everything = (slice(None), slice(None))
    rest, front = rest_refs[0][...], front_refs[0][...]
    inner = rest.shape[1] // 2
    for rest_ref, front_ref in zip(rest_refs[1:], front_refs[1:]):
        rest = rest + rest_ref[...].astype(f32)
        front = front + front_ref[...].astype(f32)
    proj = ins[3].shape[1]
    update(1, rest[:, :inner], (slice(None), slice(0, inner)))
    update(1, front[:, : proj - inner], (slice(None), slice(inner, proj)))
    rows = rest.shape[0]
    half = inner // 2
    update(4, rest[:, inner : inner + half], (slice(0, rows), slice(None)))
    update(4, rest[:, inner + half :], (slice(rows, 2 * rows), slice(None)))
    me = rates_ref[6].astype(jnp.int32)

    def own(sums, at, count):
        wide = sums.shape[1]
        shift = lax.rem(wide - me * count, wide)
        return pltpu.roll(sums[...], shift, 1)[at, :count]

    update(0, own(norm_ref, slice(0, 1), ins[0].shape[1]), everything)
    update(2, own(sums_ref, slice(0, taps + 1), ins[6].shape[1]), everything)
    update(3, own(sums_ref, slice(taps + 2, taps + 3), ins[9].shape[1]), everything)
    head_row = slice(taps + 3, taps + 4)
    for row in range(3):
        grad = sums_ref[head_row, row * lanes : row * lanes + heads]
        update(5, grad, (slice(row, row + 1), slice(None)))


def whole(shape):
    return pl.BlockSpec(shape, lambda p, b: (0,) * len(shape))


def by_block(shape, size, back=False):
    if back:
        return pl.BlockSpec(shape, lambda p, s: (p * size + (size - 1 - s), 0))
    return pl.BlockSpec(shape, lambda p, b: (p * size + b, 0))


def by_part(shape):
    return pl.BlockSpec(shape, lambda p, b: (p, 0))


def params():
    return pltpu.CompilerParams(
        dimension_semantics=("arbitrary", "arbitrary"), vmem_limit_bytes=vmem_bytes
    )


def cost(flops, moved, powers):
    return pl.CostEstimate(flops=flops, bytes_accessed=moved, transcendentals=powers)


ANY = pl.BlockSpec(memory_space=pl.ANY)
SMEM = pl.BlockSpec(memory_space=pltpu.SMEM)


def weight_scratch(*weights):
    wholes = [
        pltpu.VMEM((2 * own.shape[0] * own.shape[1], own.shape[2]), bf16) for own, _ in weights
    ]
    return wholes + [pltpu.SemaphoreType.DMA((2 * own.shape[0],)) for own, _ in weights]


def handed_out(rows, columns, blocks):
    shape = (blocks, rows // (2 * blocks), columns)
    return [jax.ShapeDtypeStruct(shape, bf16), jax.ShapeDtypeStruct(shape, f32)]


def mixer_forward(dims, core, tokens, wa, wb, small, head, skip, grouped, edge, start):
    part, size, piece, width, inner, heads, taps = dims
    conv_dim = small.shape[1]
    state_dim = (conv_dim - inner) // 2
    blocks = part * size
    rows = blocks * piece
    ext_rows = piece + 8
    return pl.pallas_call(
        partial(mixer_forward_kernel, heads=heads, inner=inner, taps=taps, grouped=grouped),
        grid=(part, size),
        in_specs=[
            SMEM,
            by_block((piece, width), size),
            by_part((8, width)) if grouped else ANY,
            ANY,
            ANY,
            ANY,
            ANY,
            whole(small.shape),
            whole(head.shape),
            whole(skip.shape),
            by_part((state_dim, inner)) if grouped else ANY,
        ],
        out_specs=[
            by_block((piece, width), size),
            by_block((ext_rows, conv_dim), size),
            by_block((piece, lanes), size),
            by_block((piece, lanes), size),
            by_block((piece, inner), size),
            by_block((state_dim, inner), size),
            by_part((state_dim, inner)),
        ],
        out_shape=[
            jax.ShapeDtypeStruct((rows, width), bf16),
            jax.ShapeDtypeStruct((blocks * ext_rows, conv_dim), f32),
            jax.ShapeDtypeStruct((rows, lanes), f32),
            jax.ShapeDtypeStruct((rows, lanes), f32),
            jax.ShapeDtypeStruct((rows, inner), f32),
            jax.ShapeDtypeStruct((blocks * state_dim, inner), bf16),
            jax.ShapeDtypeStruct((part * state_dim, inner), f32),
        ],
        scratch_shapes=[
            pltpu.VMEM((8, conv_dim), f32),
            pltpu.VMEM((state_dim, inner), f32),
            pltpu.VMEM((piece, inner), f32),
            pltpu.VMEM((piece, inner), bf16),
        ]
        + weight_scratch(wa, wb),
        compiler_params=params(),
        cost_estimate=cost(1, 1, 0),
    )(core, tokens, edge, *wa, *wb, small, head, skip, start)


def gate_step(dims, core, normed, tokens, cots, y, wg, wo, small):
    part, size, piece, width, inner, heads, taps = dims
    rows = part * size * piece
    blocks = wo[0].shape[0]
    handed = handed_out(inner, width, blocks) + handed_out(width, inner, blocks)
    return pl.pallas_call(
        partial(gate_kernel, gain_row=taps + 2),
        grid=(part, size),
        in_specs=[
            SMEM,
            by_block((piece, width), size),
            by_block((piece, width), size),
            by_block((piece, width), size),
            by_block((piece, inner), size),
            ANY,
            ANY,
            ANY,
            ANY,
            whole(small.shape),
        ],
        out_specs=[
            by_block((piece, width), size),
            by_block((piece, inner), size),
            by_block((piece, inner), size),
            whole((8, inner)),
        ]
        + [whole(array.shape) for array in handed],
        out_shape=[
            jax.ShapeDtypeStruct((rows, width), bf16),
            jax.ShapeDtypeStruct((rows, inner), bf16),
            jax.ShapeDtypeStruct((rows, inner), bf16),
            jax.ShapeDtypeStruct((8, inner), f32),
        ]
        + handed,
        scratch_shapes=[
            pltpu.VMEM((piece, inner), f32),
            pltpu.VMEM((piece, inner), f32),
            pltpu.VMEM((piece, inner), bf16),
            pltpu.VMEM((inner, width), f32),
            pltpu.VMEM((width, inner), f32),
        ]
        + weight_scratch(wg, wo),
        compiler_params=params(),
        cost_estimate=cost(1, 1, 0),
    )(core, normed, tokens, cots, y, *wg, *wo, small)


def mixer_backward(dims, saved, consts, carry, blocks, fresh):
    part, size, piece, width, inner, heads, taps = dims
    first, count = blocks
    small, head, skip, summing, dgain = consts
    conv_dim = small.shape[1]
    state_dim = (conv_dim - inner) // 2
    ext_rows = piece + 8
    wide = conv_dim + lanes
    dproj, dsmall, state, lead = carry

    def by_block(shape):
        return pl.BlockSpec(shape, lambda p, s: (p * size + (first + count - 1 - s), 0))

    return pl.pallas_call(
        partial(mixer_backward_kernel, heads=heads, inner=inner, taps=taps, fresh=fresh),
        grid=(part, count),
        in_specs=[
            by_block((ext_rows, conv_dim)),
            by_block((piece, lanes)),
            by_block((piece, lanes)),
            by_block((piece, inner)),
            by_block((state_dim, inner)),
            by_block((piece, inner)),
            whole(small.shape),
            whole(head.shape),
            whole(skip.shape),
            whole(summing.shape),
            ANY if fresh else by_part((state_dim, inner)),
            ANY if fresh else by_part((8, conv_dim)),
            whole(dsmall.shape),
            whole(dgain.shape),
            ANY,
        ],
        out_specs=[
            by_block((piece, wide)),
            whole((8, conv_dim)),
            by_part((state_dim, inner)),
            by_part((8, conv_dim)),
        ],
        out_shape=[
            jax.ShapeDtypeStruct((part * size * piece, wide), bf16),
            jax.ShapeDtypeStruct((8, conv_dim), f32),
            jax.ShapeDtypeStruct((part * state_dim, inner), f32),
            jax.ShapeDtypeStruct((part * 8, conv_dim), f32),
        ],
        scratch_shapes=[
            pltpu.VMEM((state_dim, inner), f32),
            pltpu.VMEM((piece + 8, conv_dim), f32),
            pltpu.VMEM((piece, inner), f32),
            pltpu.VMEM((piece, inner), bf16),
            pltpu.VMEM((piece, inner), bf16),
            pltpu.VMEM((piece, inner), bf16),
            pltpu.VMEM((piece, inner), bf16),
            pltpu.VMEM((piece, inner), bf16),
            pltpu.VMEM((8, inner), f32),
        ],
        input_output_aliases={14: 0} if dproj.shape[0] == part * size * piece else {},
        compiler_params=params(),
        cost_estimate=cost(1, 1, 0),
    )(*saved, small, head, skip, summing, state, lead, dsmall, dgain, dproj)


def input_grad(dims, core, tokens, dgate, dproj, small, wg, wa, wb):
    part, size, piece, width, inner, heads, taps = dims
    rows = part * size * piece
    blocks = wa[0].shape[0]
    wide_a, wide_b = wa[0].shape[2], wb[0].shape[2]
    handed = handed_out(width, wide_a, blocks) + handed_out(width, wide_b, blocks)
    return pl.pallas_call(
        partial(input_grad_kernel, gain_row=taps + 1),
        grid=(part, size),
        in_specs=[
            SMEM,
            by_block((piece, width), size),
            by_block((piece, inner), size),
            by_block((piece, dproj.shape[1]), size),
            whole(small.shape),
            ANY,
            ANY,
            ANY,
            ANY,
            ANY,
            ANY,
        ],
        out_specs=[by_block((piece, width), size), whole((8, width))]
        + [whole(array.shape) for array in handed],
        out_shape=[
            jax.ShapeDtypeStruct((rows, width), bf16),
            jax.ShapeDtypeStruct((8, width), f32),
        ]
        + handed,
        scratch_shapes=[
            pltpu.VMEM((piece, width), bf16),
            pltpu.VMEM((width, wide_a), f32),
            pltpu.VMEM((width, wide_b), f32),
        ]
        + weight_scratch(wg, wa, wb),
        compiler_params=params(),
        cost_estimate=cost(1, 1, 0),
    )(core, tokens, dgate, dproj, small, *wg, *wa, *wb)


def adam(rates, sums, norm_sums, gate_grads, front_grads, states, heads, taps):
    outs = []
    at_refs = []
    for which, (master, first, second) in enumerate(states):
        at_refs.append(len(outs))
        outs += [jax.ShapeDtypeStruct(master.shape, f32)] * 3
    outs.append(jax.ShapeDtypeStruct(states[1][0].shape, bf16))
    outs.append(jax.ShapeDtypeStruct(states[4][0].shape, bf16))
    flat = [array for state in states for array in state]
    vmem = pl.BlockSpec(memory_space=pltpu.VMEM)
    return pl.pallas_call(
        partial(
            adam_kernel, heads=heads, taps=taps, at_refs=at_refs, arrivals=len(gate_grads)
        ),
        in_specs=[SMEM] + [vmem] * (2 + 2 * len(gate_grads) + len(flat)),
        out_specs=[vmem] * len(outs),
        out_shape=outs,
        compiler_params=pltpu.CompilerParams(vmem_limit_bytes=vmem_bytes),
        cost_estimate=cost(1, 1, 0),
    )(rates, sums, norm_sums, *gate_grads, *front_grads, *flat)


def bit_count(extent):
    count = extent.bit_length() - 1
    if 1 << count != extent:
        raise ValueError(extent)
    return count


def swap(block, axis, bit):
    devices = range(lax.axis_size(axis))
    return lax.ppermute(block, axis, [(i, i ^ (1 << bit)) for i in devices])


def shifted_by(block, axis, distance):
    devices = range(lax.axis_size(axis))
    route = [(i, i + distance) for i in devices if i + distance in devices]
    return lax.ppermute(block, axis, route)


def pick(block, at, axis):
    return lax.dynamic_index_in_dim(block, at, axis, keepdims=False)


def gather_bit(block, axis, bit, at, *others):
    mine = (lax.axis_index(axis) >> bit) & 1
    other = swap(block, axis, bit)
    if others:
        other = after(other, *others)
    low = jnp.where(mine == 1, other, block)
    high = jnp.where(mine == 1, block, other)
    return jnp.stack([low, high], axis=at)


def gather_seq(shard):
    block = shard
    kept = []
    for done, bit in enumerate(reversed(range(bit_count(lax.axis_size("seq"))))):
        block = gather_bit(block, "seq", bit, done)
        kept.append(block)
    return block.reshape((-1,) + shard.shape), kept[0]


def dp_orders():
    bits = bit_count(lax.axis_size("dp"))
    return list(range(bits - 1, 0, -1)) + [0], list(range(1, bits)) + [0]


def gather_dp_bit(block, order, step, *others):
    at = sum(1 for b in order[:step] if b > order[step])
    return gather_bit(block, "dp", order[step], at, *others)


def give_half(block, axis, bit, at):
    mine = (lax.axis_index(axis) >> bit) & 1
    other = swap(pick(block, 1 - mine, at).astype(bf16), axis, bit)
    return pick(block, mine, at) + other.astype(f32)


def core_sums(send, keep):
    extent = lax.axis_size("seq")
    total = keep + swap(send, "dp", 0).astype(f32)
    bits = bit_count(lax.axis_size("dp")) - 1
    return total.reshape((2,) * bits + (extent, -1, send.shape[2]))


def scatter_dp_bit(block, order, step):
    bit = order[-1 - step]
    return give_half(block, "dp", bit, sum(1 for b in order[: len(order) - 1 - step] if b > bit))


def scatter_seq(block):
    extent = lax.axis_size("seq")
    place = lax.axis_index("seq")
    arrivals = [pick(block, place, 0)]
    for distance in range(1, extent):
        sent = pick(block, lax.rem(place + distance, extent), 0).astype(bf16)
        route = [(i, (i + distance) % extent) for i in range(extent)]
        arrivals.append(lax.ppermute(sent, "seq", route))
    return arrivals


def sum_over(block, axis):
    for bit in range(bit_count(lax.axis_size(axis))):
        block = block + swap(block, axis, bit)
    return block


def seq_groups(size):
    extent = lax.axis_size("seq")
    if size == extent:
        return None
    return [list(range(at, at + size)) for at in range(0, extent, size)]


def to_sequences(block, part, size):
    if size > 1:
        block = lax.all_to_all(
            block, "seq", 0, 0, axis_index_groups=seq_groups(size), tiled=True
        )
    piece, width = block.shape[1:]
    block = block.reshape(size, part, piece, width)
    if part > 1:
        block = block.transpose(1, 0, 2, 3)
    return block.reshape(-1, width)


def to_pieces(rows, part, size, piece):
    block = rows.reshape(part, size, piece, -1)
    if part > 1:
        block = block.transpose(1, 0, 2, 3)
    block = block.reshape(part * size, piece, -1)
    if size > 1:
        block = lax.all_to_all(
            block, "seq", 0, 0, axis_index_groups=seq_groups(size), tiled=True
        )
    return block


def after(value, *others):
    return lax.optimization_barrier((value,) + others)[0]


def padded(block, rows, columns):
    return jnp.pad(block, ((0, rows - block.shape[0]), (0, columns - block.shape[1])))


def summing_matrix(inner, heads):
    columns = np.zeros((inner, lanes), np.float32)
    columns[np.arange(inner), np.arange(inner) // (inner // heads)] = 1.0
    return jnp.asarray(columns, bf16)


def local(
    layer_in,
    out_grad,
    norm_gain,
    in_weight,
    conv_params,
    gate_gain,
    out_weight,
    head_params,
    norm_first,
    norm_second,
    in_first,
    in_second,
    conv_first,
    conv_second,
    gate_first,
    gate_second,
    out_first,
    out_second,
    head_first,
    head_second,
    step_count,
    hyper,
):
    seq_count, piece, width = layer_in.shape
    seq_extent = lax.axis_size("seq")
    me = lax.axis_index("dp") * seq_extent + lax.axis_index("seq")
    step_float = step_count[0].astype(f32)
    scales = 1.0 / (1.0 - hyper[1:3] ** step_float)
    rates = jnp.concatenate([hyper, scales, jnp.stack([me.astype(f32), jnp.zeros((), f32)])])
    core = (lax.axis_index("dp") & 1).astype(jnp.int32)[None]
    owners = lax.axis_size("dp") * seq_extent
    size = math.gcd(seq_extent, seq_count)
    part = seq_count // size
    groups = seq_extent // size
    inner = out_weight.shape[0] * owners
    heads = head_params.shape[1]
    tap_rows, conv_own = conv_params.shape
    taps = tap_rows - 1
    conv_dim = conv_own * owners
    state_dim = (conv_dim - inner) // 2
    own_rows = in_weight.shape[0]
    gate_own = gate_gain.shape[0]
    wide_a = min(1024, inner)
    dims = (part, size, piece, width, inner, heads, taps)

    small = jnp.zeros((8, conv_dim), bf16)
    for at, row, count in (
        (0, conv_params, conv_own),
        (tap_rows, norm_gain[None, :], own_rows),
        (tap_rows + 1, gate_gain[None, :], gate_own),
    ):
        small = lax.dynamic_update_slice(small, row.astype(bf16), (at, me * count))
    head = padded(head_params, 8, lanes)
    skip = jnp.repeat(head_params[2], inner // heads)[None, :]
    summing = summing_matrix(inner, heads)

    in_low = padded(in_weight.astype(bf16), own_rows, inner + conv_dim + lanes)
    out_low_own = out_weight.astype(bf16).reshape(2, own_rows, width)
    shard = jnp.concatenate([in_low, out_low_own[0], out_low_own[1]], axis=1)
    gathered, half_gathered = gather_seq(shard)
    small = sum_over(after(small, half_gathered), "seq")
    front_end = inner + conv_dim + lanes
    wg = gathered[:, :, :inner]
    wa = gathered[:, :, inner : inner + wide_a]
    wb = gathered[:, :, inner + wide_a : front_end]
    wo = jnp.stack(
        [gathered[:, :, front_end : front_end + width], gathered[:, :, front_end + width :]],
        axis=1,
    ).reshape(-1, 2 * own_rows, width)
    tokens = to_sequences(after(layer_in, head, skip, shard, rates), part, size)
    order_a, order_b = dp_orders()
    last = len(order_a) - 1
    for step in range(last):
        wa = gather_dp_bit(wa, order_a, step)
        wb = gather_dp_bit(wb, order_b, step)
    small = sum_over(small, "dp").astype(f32)
    wg, wo = after((wg, wo), wa, wb, small)

    def core_halves(block):
        block = block.reshape(owners // 2 // seq_extent, -1, block.shape[-1])
        return block, swap(block, "dp", 0)

    wb = core_halves(wb)
    wa = core_halves(wa)
    for step in range(last - 1):
        wg = gather_dp_bit(wg, order_a, step)
        wo = gather_dp_bit(wo, order_b, step)
    wg, wo, tokens = lax.optimization_barrier((wg, wo, after(tokens, wa, wb)))
    cots = to_sequences(after(out_grad, tokens), part, size)

    edge = core
    if groups > 1:
        edge = tokens.reshape(part, size * piece, width)[:, size * piece - 8 :, :]
        edge = shifted_by(edge, "seq", size).reshape(part * 8, width)

    def forward(start):
        return mixer_forward(
            dims, core, tokens, wa, wb, small, head, skip, groups > 1, edge, start
        )

    if groups > 1:
        first_out = forward(jnp.zeros((part * state_dim, inner), f32))
        cum_last = first_out[3].reshape(part, size, piece, lanes)[:, :, piece - 1, :heads]
        decay = jnp.exp2(jnp.sum(cum_last, axis=1))
        decay = jnp.repeat(decay, inner // heads, axis=1)[:, None, :]

        def relay(ends, distance):
            ends = ends.reshape(part, state_dim, inner)
            carried = jnp.zeros_like(ends)
            for _ in range(groups - 1):
                sent = (decay * carried + ends).astype(bf16)
                carried = shifted_by(sent, "seq", distance).astype(f32)
            return carried.reshape(part * state_dim, inner)

        start = relay(first_out[6], size)
    else:
        start = core
    normed, ext, dtr, cum, y, sin, _ = forward(start)

    wg = core_halves(gather_dp_bit(wg, order_a, last - 1, normed))
    wo = core_halves(gather_dp_bit(wo, order_b, last - 1, normed))
    layer_rows, dy, dgate, dgain, *handed = gate_step(
        dims, core, normed, tokens, cots, y, wg, wo, small
    )
    layer_out = to_pieces(layer_rows, part, size, piece)
    g_out = core_sums(*handed[:2])
    g_gate = core_sums(*handed[2:])
    dy = after(dy, g_out, g_gate)
    cut = size // 2
    saved = (ext, dtr, cum, y, sin, dy)
    consts = (small, head, skip, summing, dgain)

    def backward(state, lead):
        carry = (core, head, state, lead)
        return list(
            mixer_backward(dims, saved, consts, carry, (cut, size - cut), groups == 1)
        )

    if groups > 1:
        zeros = (jnp.zeros((part * state_dim, inner), f32), jnp.zeros((part * 8, conv_dim), f32))
        first_out = backward(*zeros)
        first_out = mixer_backward(dims, saved, consts, first_out, (0, cut), False)
        backward_out = backward(relay(first_out[2], -size), zeros[1])
    else:
        backward_out = backward(core, core)
    for step in range(1, last):
        g_out = scatter_dp_bit(g_out, order_a, step)
        g_gate = scatter_dp_bit(g_gate, order_b, step)
    backward_out[2], g_out, g_gate = lax.optimization_barrier((backward_out[2], g_out, g_gate))
    dproj, dsmall, _, lead = mixer_backward(dims, saved, consts, backward_out, (0, cut), False)
    g_out = scatter_dp_bit(g_out, order_a, last)
    g_gate = scatter_dp_bit(g_gate, order_b, last)
    if groups > 1:
        lead = shifted_by(lead.astype(bf16), "seq", -size).astype(f32)
        lead = lead.reshape(part, 8, conv_dim)
        fixes = []
        for row in range(taps - 1):
            terms = [small[tap] * lead[:, row - tap] for tap in range(row + 1)]
            fixes.append(sum(terms[1:], terms[0]))
        fix = jnp.pad(jnp.stack(fixes, axis=1), ((0, 0), (0, 0), (0, lanes)))
        dproj = dproj.reshape(part, size * piece, conv_dim + lanes)
        ends = dproj[:, size * piece - (taps - 1) :].astype(f32) + fix
        dproj = dproj.at[:, size * piece - (taps - 1) :].set(ends.astype(bf16))
        dproj = dproj.reshape(-1, conv_dim + lanes)
    g_rest = scatter_seq(
        jnp.concatenate([g_gate, g_out[:, :own_rows], g_out[:, own_rows:]], axis=2)
    )
    sums = sum_over(dsmall, "seq")
    tokens = after(tokens, layer_out, g_gate, g_out)
    dx, d_gain, *handed = input_grad(dims, core, tokens, dgate, dproj, small, wg, wa, wb)
    handed, dx, sums = after((handed, dx, sums), g_rest)
    g_a = core_sums(*handed[:2])
    g_b = core_sums(*handed[2:])
    sums, d_gain = after((sums, d_gain), g_a, g_b)
    for step in range(1, last + 1):
        g_a = scatter_dp_bit(g_a, order_a, step)
        g_b = scatter_dp_bit(g_b, order_b, step)
    g_front = scatter_seq(jnp.concatenate([g_a, g_b], axis=2))
    in_grad = out_grad.astype(f32) + to_pieces(dx, part, size, piece).astype(f32)
    sums = sum_over(sums, "dp")
    norm_sums = sum_over(sum_over(d_gain, "dp"), "seq")

    states = (
        (norm_gain[None, :], norm_first[None, :], norm_second[None, :]),
        (in_weight, in_first, in_second),
        (conv_params, conv_first, conv_second),
        (gate_gain[None, :], gate_first[None, :], gate_second[None, :]),
        (out_weight, out_first, out_second),
        (head_params, head_first, head_second),
    )
    new = adam(rates, sums, norm_sums, g_rest, g_front, states, heads, taps)
    new = [array[0] if array.shape[0] == 1 else array for array in new]
    return (layer_out, in_grad, *new)


def solution(mesh):
    in_specs = (
        P("dp", "seq", None),
        P("dp", "seq", None),
        P(("dp", "seq")),
        P(("dp", "seq"), None),
        P(None, ("dp", "seq")),
        P(("dp", "seq")),
        P(("dp", "seq"), None),
        P(),
        P(("dp", "seq")),
        P(("dp", "seq")),
        P(("dp", "seq"), None),
        P(("dp", "seq"), None),
        P(None, ("dp", "seq")),
        P(None, ("dp", "seq")),
        P(("dp", "seq")),
        P(("dp", "seq")),
        P(("dp", "seq"), None),
        P(("dp", "seq"), None),
        P(),
        P(),
        P(),
        P(),
    )
    out_specs = (
        P("dp", "seq", None),
        P("dp", "seq", None),
        P(("dp", "seq")),
        P(("dp", "seq")),
        P(("dp", "seq")),
        P(("dp", "seq"), None),
        P(("dp", "seq"), None),
        P(("dp", "seq"), None),
        P(None, ("dp", "seq")),
        P(None, ("dp", "seq")),
        P(None, ("dp", "seq")),
        P(("dp", "seq")),
        P(("dp", "seq")),
        P(("dp", "seq")),
        P(("dp", "seq"), None),
        P(("dp", "seq"), None),
        P(("dp", "seq"), None),
        P(),
        P(),
        P(),
        P(("dp", "seq"), None),
        P(("dp", "seq"), None),
    )
    return jax.shard_map(local, mesh=mesh, in_specs=in_specs, out_specs=out_specs, check_vma=False)
```

```python
import math
from functools import partial

import jax
import jax.numpy as jnp
import numpy as np
from jax import lax
from jax.experimental import pallas as pl
from jax.experimental.pallas import tpu as pltpu
from jax.sharding import PartitionSpec as P

norm_eps = 1e-05
adam_eps = 1e-08
log2e = math.log2(math.e)
lanes = 128
vmem_bytes = 56 * 1024 * 1024
f32 = jnp.float32
bf16 = jnp.bfloat16


def dot(left, right, left_dim=1, right_dim=0):
    return lax.dot_general(
        left, right, (((left_dim,), (right_dim,)), ((), ())), preferred_element_type=f32
    )


def halves(value):
    high = value.astype(bf16)
    return high, (value - high.astype(f32)).astype(bf16)


def sigmoid(value):
    return 0.5 * jnp.tanh(0.5 * value) + 0.5


def column(ref_value, at, width):
    return jnp.broadcast_to(ref_value[:, at : at + 1], (ref_value.shape[0], width))


def pair_columns(value, pair, low_lane):
    rows = value.shape[0]
    first = column(value, 2 * pair, lanes)
    second = column(value, 2 * pair + 1, lanes)
    return jnp.where(low_lane, first, second), first, second


def tri_sum(mask, value, head_lane):
    high = value.astype(bf16).astype(f32)
    rest = value - high
    mid = rest.astype(bf16).astype(f32)
    low = rest - mid
    packed = high + pltpu.roll(mid, 32, 1) + pltpu.roll(low, 64, 1)
    summed = dot(mask, packed.astype(bf16))
    total = summed + pltpu.roll(summed, lanes - 32, 1) + pltpu.roll(summed, lanes - 64, 1)
    return jnp.where(head_lane, total, 0.0)


def conv_chunk(ext_ref, conv_ref, at, length, taps):
    summed = conv_ref[taps : taps + 1, at : at + lanes]
    base = 8 - (taps - 1)
    for tap in range(taps):
        summed = (
            summed
            + conv_ref[tap : tap + 1, at : at + lanes]
            * ext_ref[at // lanes, base + tap : base + tap + length, :]
        )
    return summed


def put_columns(ext_ref, rows, values, chunk):
    for at in range(0, values.shape[1], lanes):
        ext_ref[chunk + at // lanes, rows, :] = values[:, at : at + lanes]


def step_sizes(dt_raw, head_ref, head_lane):
    shifted = dt_raw + head_ref[0:1, :]
    steps = jnp.maximum(shifted, 0.0) + jnp.log1p(jnp.exp(-jnp.abs(shifted)))
    return jnp.where(head_lane, steps, 0.0), shifted


def fetch_weight(core_ref, own_ref, other_ref, whole_ref, sems):
    blocks, rows, _ = own_ref.shape
    core = core_ref[0]
    copies = []
    for block in range(blocks):
        for which, source in ((core, own_ref), (1 - core, other_ref)):
            at = pl.multiple_of((2 * block + which) * rows, rows)
            copies.append(
                pltpu.make_async_copy(
                    source.at[block], whole_ref.at[pl.ds(at, rows)], sems.at[len(copies)]
                )
            )
    for copy in copies:
        copy.start()
    return copies


def hand_out(core, total_ref, send_ref, keep_ref):
    blocks, rows, _ = send_ref.shape
    for block in range(blocks):
        at = pl.multiple_of((2 * block + 1 - core) * rows, rows)
        send_ref[block] = total_ref[pl.ds(at, rows), :].astype(bf16)
        at = pl.multiple_of((2 * block + core) * rows, rows)
        keep_ref[block] = total_ref[pl.ds(at, rows), :]


def add_product(total_ref, left_ref, right):
    for at in range(0, total_ref.shape[0], 2 * lanes):
        here = slice(at, at + 2 * lanes)
        total_ref[here, :] += dot(left_ref[:, here], right, 0, 0)


def mixer_forward_kernel(
    core_ref,
    x_ref,
    edge_ref,
    wa_own,
    wa_other,
    wb_own,
    wb_other,
    conv_ref,
    head_ref,
    skip_ref,
    start_ref,
    before_ref,
    *refs,
    heads,
    inner,
    taps,
    grouped,
    resumed,
):
    (
        normed_ref,
        ext_ref,
        dtr_ref,
        cum_ref,
        y_ref,
        sin_ref,
        end_ref,
        after_ref,
        tail_ref,
        state_ref,
        carried_ref,
        weighted_ref,
        wa_ref,
        wb_ref,
        wa_sems,
        wb_sems,
    ) = refs[6:] if resumed else refs
    block = pl.program_id(1)
    length, width = x_ref.shape

    @pl.when(jnp.logical_and(pl.program_id(0) == 0, block == 0))
    def _():
        copies = fetch_weight(core_ref, wa_own, wa_other, wa_ref, wa_sems)
        copies += fetch_weight(core_ref, wb_own, wb_other, wb_ref, wb_sems)
        for copy in copies:
            copy.wait()

    half = length // 2
    wide_a = wa_ref.shape[1]
    conv_dim = conv_ref.shape[1]
    state_dim = (conv_dim - inner) // 2

    def norm_of(rows):
        rows = rows.astype(f32)
        scale = lax.rsqrt(jnp.mean(rows * rows, axis=-1, keepdims=True) + norm_eps)
        return (rows * scale * conv_ref[taps + 1 : taps + 2, :width]).astype(bf16)

    @pl.when(block == 0)
    def _():
        if resumed:
            state_ref[...] = start_ref[...]
            tail_ref[...] = before_ref[...]
        elif grouped:
            state_ref[...] = start_ref[...]
            edge = norm_of(edge_ref[...])
            put_columns(tail_ref, slice(0, 8), dot(edge, wa_ref[...]), 0)
            edge_b = dot(edge, wb_ref[...])[:, : conv_dim - wide_a]
            put_columns(tail_ref, slice(0, 8), edge_b, wide_a // lanes)
        else:
            state_ref[...] = jnp.zeros_like(state_ref)
            tail_ref[...] = jnp.zeros_like(tail_ref)

    normed = norm_of(x_ref[...])
    normed_ref[...] = normed
    ext_ref[:, 0:8, :] = tail_ref[...]
    own_rows = slice(8, 8 + length)
    for at in range(0, wide_a, 2 * lanes):
        product = dot(normed, wa_ref[:, at : at + 2 * lanes])
        put_columns(ext_ref, own_rows, product, at // lanes)
    second = dot(normed, wb_ref[...])
    put_columns(ext_ref, own_rows, second[:, : conv_dim - wide_a], wide_a // lanes)
    dt_raw = second[:, conv_dim - wide_a :]
    tail_ref[...] = ext_ref[:, length : length + 8, :]

    lane = lax.broadcasted_iota(jnp.int32, (length, lanes), 1)
    low_lane = lane < lanes // 2
    head_lane = lane < heads
    dtr_ref[...] = dt_raw
    steps, _ = step_sizes(dt_raw, head_ref, head_lane)
    log_decay = steps * (-log2e * jnp.exp(head_ref[1:2, :]))
    row = lax.broadcasted_iota(jnp.int32, (length, length), 0)
    col = lax.broadcasted_iota(jnp.int32, (length, length), 1)
    cum = tri_sum((row >= col).astype(bf16), log_decay, head_lane)
    cum_ref[...] = cum
    cum_rows = cum.T

    def mixed_chunk(at):
        summed = conv_chunk(ext_ref, conv_ref, at, length, taps)
        return summed * sigmoid(summed)

    keys = jnp.concatenate(
        [mixed_chunk(inner + at) for at in range(0, state_dim, lanes)], axis=1
    ).astype(bf16)
    queries = jnp.concatenate(
        [mixed_chunk(inner + state_dim + at) for at in range(0, state_dim, lanes)], axis=1
    ).astype(bf16)
    state_low = state_ref[...].astype(bf16)
    sin_ref[...] = state_low
    carried_ref[...] = dot(queries, state_low)
    square = (half, half)
    diag = lax.broadcasted_iota(jnp.int32, square, 0) >= lax.broadcasted_iota(
        jnp.int32, square, 1
    )
    scores_00 = jnp.where(diag, dot(queries[:half], keys[:half], 1, 1), 0.0)
    scores_10 = dot(queries[half:], keys[:half], 1, 1)
    scores_11 = jnp.where(diag, dot(queries[half:], keys[half:], 1, 1), 0.0)
    for pair in range(heads // 2):
        at = pair * lanes
        values = mixed_chunk(at)
        cum_rep, cum_0, cum_1 = pair_columns(cum, pair, low_lane)
        dt_rep, _, _ = pair_columns(steps, pair, low_lane)
        stepped = values * dt_rep
        last = cum_rep[length - 1 : length, :]
        weighted_ref[:, at : at + lanes] = (stepped * jnp.exp2(last - cum_rep)).astype(bf16)
        top = None
        bottom = None
        for which, cum_col in ((0, cum_0), (1, cum_1)):
            own = jnp.where(low_lane if which == 0 else jnp.logical_not(low_lane), stepped, 0.0)
            own = own.astype(bf16)
            head = 2 * pair + which
            early = cum_rows[head : head + 1, :half]
            late = cum_rows[head : head + 1, half:]
            mix_00 = jnp.exp2(jnp.minimum(cum_col[:half] - early, 0.0)) * scores_00
            mix_10 = jnp.exp2(cum_col[half:] - early) * scores_10
            mix_11 = jnp.exp2(jnp.minimum(cum_col[half:] - late, 0.0)) * scores_11
            part_top = dot(mix_00.astype(bf16), own[:half])
            part_bottom = dot(
                jnp.concatenate([mix_10.astype(bf16), mix_11.astype(bf16)], axis=1), own
            )
            top = part_top if top is None else top + part_top
            bottom = part_bottom if bottom is None else bottom + part_bottom
        rest = (
            jnp.exp2(cum_rep) * carried_ref[:, at : at + lanes]
            + skip_ref[0:1, at : at + lanes] * values
        )
        y_ref[0:half, at : at + lanes] = top + rest[:half]
        y_ref[half:length, at : at + lanes] = bottom + rest[half:]
        state_ref[:, at : at + lanes] = jnp.exp2(last) * state_ref[:, at : at + lanes]

    state_ref[...] += dot(keys, weighted_ref[...], 0, 0)

    @pl.when(block == pl.num_programs(1) - 1)
    def _():
        end_ref[...] = state_ref[...]
        after_ref[...] = tail_ref[...]


def gate_kernel(
    core_ref,
    normed_ref,
    x_ref,
    cot_a_ref,
    cot_b_ref,
    y_ref,
    wg_own,
    wg_other,
    wo_own,
    wo_other,
    small_ref,
    out_ref,
    dy_ref,
    dgate_ref,
    dgain_ref,
    out_send,
    out_keep,
    gate_send,
    gate_keep,
    gate_ref,
    dno_ref,
    low_ref,
    cot_ref,
    out_sum,
    gate_sum,
    wg_ref,
    wo_ref,
    wg_sems,
    wo_sems,
    *,
    gain_row,
):
    length, inner = y_ref.shape
    first = jnp.logical_and(pl.program_id(0) == 0, pl.program_id(1) == 0)

    @pl.when(first)
    def _():
        copies = fetch_weight(core_ref, wg_own, wg_other, wg_ref, wg_sems)
        copies += fetch_weight(core_ref, wo_own, wo_other, wo_ref, wo_sems)
        dgain_ref[...] = jnp.zeros_like(dgain_ref)
        out_sum[...] = jnp.zeros_like(out_sum)
        gate_sum[...] = jnp.zeros_like(gate_sum)
        for copy in copies:
            copy.wait()

    gate_ref[...] = dot(normed_ref[...], wg_ref[...])
    cot_ref[:, : cot_a_ref.shape[1]] = cot_a_ref[...]
    cot_ref[:, cot_a_ref.shape[1] :] = cot_b_ref[...]
    dno_ref[...] = dot(cot_ref[...], wo_ref[...], 1, 1)
    squares = jnp.zeros((length, lanes), f32)
    crosses = jnp.zeros((length, lanes), f32)
    for at in range(0, inner, lanes):
        here = slice(at, at + lanes)
        gate = gate_ref[:, here]
        gated = y_ref[:, here] * (gate * sigmoid(gate))
        squares = squares + gated * gated
        crosses = crosses + gated * (small_ref[gain_row : gain_row + 1, here] * dno_ref[:, here])
    scale = lax.rsqrt(jnp.sum(squares, axis=1, keepdims=True) * (1.0 / inner) + norm_eps)
    cross = scale * scale * scale * (jnp.sum(crosses, axis=1, keepdims=True) * (1.0 / inner))
    scale_b = jnp.broadcast_to(scale, (length, lanes))
    cross_b = jnp.broadcast_to(cross, (length, lanes))
    for at in range(0, inner, lanes):
        here = slice(at, at + lanes)
        gate = gate_ref[:, here]
        mixed_out = y_ref[:, here]
        sig = sigmoid(gate)
        silu = gate * sig
        gated = mixed_out * silu
        scaled = gated * scale_b
        d_out = dno_ref[:, here]
        low_ref[:, here] = (scaled * small_ref[gain_row : gain_row + 1, here]).astype(bf16)
        dgain_ref[0:1, here] += jnp.sum(scaled * d_out, axis=0, keepdims=True)
        d_gated = scale_b * (small_ref[gain_row : gain_row + 1, here] * d_out) - gated * cross_b
        dy_ref[:, here] = (d_gated * silu).astype(bf16)
        dgate_ref[:, here] = (d_gated * mixed_out * (sig * (1.0 + gate * (1.0 - sig)))).astype(
            bf16
        )
    out_ref[...] = (x_ref[...].astype(f32) + dot(low_ref[...], wo_ref[...])).astype(bf16)
    add_product(out_sum, low_ref, cot_ref[...])
    add_product(gate_sum, normed_ref, dgate_ref[...])
    last = jnp.logical_and(
        pl.program_id(0) == pl.num_programs(0) - 1, pl.program_id(1) == pl.num_programs(1) - 1
    )

    @pl.when(last)
    def _():
        hand_out(core_ref[0], out_sum, out_send, out_keep)
        hand_out(core_ref[0], gate_sum, gate_send, gate_keep)


def mixer_backward_kernel(
    ext_ref,
    dtr_ref,
    cum_ref,
    y_ref,
    sin_ref,
    dy_ref,
    conv_ref,
    head_ref,
    skip_ref,
    sum_ref,
    start_ref,
    next_ref,
    small_in_ref,
    dgain_ref,
    _,
    dproj_ref,
    dconv_ref,
    end_ref,
    lead_ref,
    grad_ref,
    dsx_ref,
    dwv_ref,
    dye_ref,
    weighted_ref,
    zhigh_ref,
    zlow_ref,
    direct_ref,
    rows_ref,
    *,
    heads,
    inner,
    taps,
    fresh,
):
    step = pl.program_id(1)
    length = dy_ref.shape[0]
    half = length // 2
    conv_dim = conv_ref.shape[1]
    state_dim = (conv_dim - inner) // 2
    first = jnp.logical_and(pl.program_id(0) == 0, step == 0)

    @pl.when(first)
    def _():
        if small_in_ref.shape == dconv_ref.shape:
            dconv_ref[...] = small_in_ref[...]
        else:
            dconv_ref[...] = jnp.zeros_like(dconv_ref)
            dconv_ref[taps + 2 : taps + 3, :inner] = dgain_ref[0:1, :]
        rows_ref[...] = jnp.zeros_like(rows_ref)

    @pl.when(step == 0)
    def _():
        if fresh:
            grad_ref[...] = jnp.zeros_like(grad_ref)
            dsx_ref[:, length : length + 8, :] = jnp.zeros((conv_dim // lanes, 8, lanes), f32)
        else:
            grad_ref[...] = start_ref[...]
            dsx_ref[:, length : length + 8, :] = next_ref[...]

    @pl.when(step > 0)
    def _():
        dsx_ref[:, length : length + 8, :] = dsx_ref[:, 0:8, :]

    lane = lax.broadcasted_iota(jnp.int32, (length, lanes), 1)
    low_lane = lane < lanes // 2
    head_lane = lane < heads
    steps, shifted = step_sizes(dtr_ref[...], head_ref, head_lane)
    cum = cum_ref[...]
    cum_rows = cum.T

    def slope_chunk(at):
        summed = conv_chunk(ext_ref, conv_ref, at, length, taps)
        sig = sigmoid(summed)
        return summed * sig, sig * (1.0 + summed * (1.0 - sig))

    def put_grad(at, d_summed):
        here = slice(at, at + lanes)
        chunk = at // lanes
        dsx_ref[chunk, 0:length, :] = d_summed
        total = None
        for tap in range(taps):
            base = 8 - (taps - 1) + tap
            dconv_ref[tap : tap + 1, here] += jnp.sum(
                d_summed * ext_ref[chunk, base : base + length, :], axis=0, keepdims=True
            )
            back = taps - 1 - tap
            term = conv_ref[tap : tap + 1, here] * dsx_ref[chunk, back : back + length, :]
            total = term if total is None else total + term
        dconv_ref[taps : taps + 1, here] += jnp.sum(d_summed, axis=0, keepdims=True)
        dproj_ref[:, here] = total.astype(bf16)

    parts = [slope_chunk(inner + at) for at in range(0, 2 * state_dim, lanes)]
    count = state_dim // lanes
    keys = jnp.concatenate([part[0] for part in parts[:count]], axis=1).astype(bf16)
    queries = jnp.concatenate([part[0] for part in parts[count:]], axis=1).astype(bf16)
    grad_low = grad_ref[...].astype(bf16)
    dwv_ref[...] = dot(keys, grad_low)
    square = (half, half)
    diag = lax.broadcasted_iota(jnp.int32, square, 0) <= lax.broadcasted_iota(
        jnp.int32, square, 1
    )
    scores_00 = jnp.where(diag, dot(keys[:half], queries[:half], 1, 1), 0.0)
    scores_01 = dot(keys[:half], queries[half:], 1, 1)
    scores_11 = jnp.where(diag, dot(keys[half:], queries[half:], 1, 1), 0.0)
    ds_00 = jnp.zeros(square, f32)
    ds_01 = jnp.zeros(square, f32)
    ds_11 = jnp.zeros(square, f32)
    for pair in range(heads // 2):
        at = pair * lanes
        here = slice(at, at + lanes)
        values, slope = slope_chunk(at)
        cum_rep, cum_0, cum_1 = pair_columns(cum, pair, low_lane)
        dt_rep, _, _ = pair_columns(steps, pair, low_lane)
        stepped = (values * dt_rep).astype(bf16)
        stepped_f = stepped.astype(f32)
        last = cum_rep[length - 1 : length, :]
        tail = jnp.exp2(last - cum_rep)
        d_y = dy_ref[:, here]
        d_yf = d_y.astype(f32)
        d_y_t = d_yf.T.astype(bf16)
        dye_ref[:, here] = (d_yf * jnp.exp2(cum_rep)).astype(bf16)
        top = None
        bottom = None
        for which, cum_col in ((0, cum_0), (1, cum_1)):
            own_lane = low_lane if which == 0 else jnp.logical_not(low_lane)
            own_dy = jnp.where(own_lane, d_yf, 0.0).astype(bf16)
            own_x = jnp.where(own_lane, stepped_f, 0.0).astype(bf16)
            head = 2 * pair + which
            early = cum_rows[head : head + 1, :half]
            late = cum_rows[head : head + 1, half:]
            decay_00 = jnp.exp2(jnp.minimum(early - cum_col[:half], 0.0))
            decay_01 = jnp.exp2(late - cum_col[:half])
            decay_11 = jnp.exp2(jnp.minimum(late - cum_col[half:], 0.0))
            mix_0 = jnp.concatenate(
                [(decay_00 * scores_00).astype(bf16), (decay_01 * scores_01).astype(bf16)], axis=1
            )
            mix_1 = (decay_11 * scores_11).astype(bf16)
            part_top = dot(mix_0, own_dy)
            part_bottom = dot(mix_1, own_dy[half:])
            top = part_top if top is None else top + part_top
            bottom = part_bottom if bottom is None else bottom + part_bottom
            d_mix_0 = dot(own_x[:half], d_y_t)
            d_mix_1 = dot(own_x[half:], d_y_t[:, half:])
            ds_00 = ds_00 + decay_00 * d_mix_0[:, :half]
            ds_01 = ds_01 + decay_01 * d_mix_0[:, half:]
            ds_11 = ds_11 + decay_11 * d_mix_1
        d_diag = jnp.concatenate([top, bottom], axis=0)
        weighted = (stepped_f * tail).astype(bf16)
        weighted_ref[:, here] = weighted
        d_weighted = dwv_ref[:, here]
        through = weighted.astype(f32) * d_weighted
        d_stepped = d_diag + tail * d_weighted
        skip = skip_ref[0:1, here]
        z = d_yf * (y_ref[:, here] - skip * values) - stepped_f * d_diag - through
        z_high, z_low = halves(z)
        zhigh_ref[:, here] = z_high
        zlow_ref[:, here] = z_low
        direct_ref[:, here] = (d_stepped * values).astype(bf16)
        total_decay = jnp.exp2(last)
        rows_ref[0:1, here] = jnp.sum(through, axis=0, keepdims=True) + total_decay * jnp.sum(
            grad_ref[:, here] * sin_ref[:, here].astype(f32), axis=0, keepdims=True
        )
        rows_ref[1:2, here] = jnp.sum(d_yf * values, axis=0, keepdims=True)
        put_grad(at, (d_stepped * dt_rep + skip * d_yf) * slope)
        grad_ref[:, here] = total_decay * grad_ref[:, here]

    grad_ref[...] += dot(queries, dye_ref[...], 0, 0)
    ds_00 = jnp.where(diag, ds_00, 0.0).astype(bf16)
    ds_11 = jnp.where(diag, ds_11, 0.0).astype(bf16)
    ds_01 = ds_01.astype(bf16)
    d_queries = dot(dye_ref[...], sin_ref[...], 1, 1)
    d_keys = dot(weighted_ref[...], grad_low, 1, 1)
    d_queries = d_queries + jnp.concatenate(
        [
            dot(ds_00, keys[:half], 0, 0),
            dot(ds_01, keys[:half], 0, 0) + dot(ds_11, keys[half:], 0, 0),
        ],
        axis=0,
    )
    d_keys = d_keys + jnp.concatenate(
        [
            dot(ds_00, queries[:half]) + dot(ds_01, queries[half:]),
            dot(ds_11, queries[half:]),
        ],
        axis=0,
    )
    for at in range(0, state_dim, lanes):
        put_grad(inner + at, d_keys[:, at : at + lanes] * parts[at // lanes][1])
        put_grad(
            inner + state_dim + at,
            d_queries[:, at : at + lanes] * parts[count + at // lanes][1],
        )
    summing = sum_ref[...]
    rows_high, rows_low = halves(rows_ref[...])
    row_sums = dot(rows_high, summing) + dot(rows_low, summing)
    d_cum = dot(zhigh_ref[...], summing) + dot(zlow_ref[...], summing)
    at_last = lax.broadcasted_iota(jnp.int32, (length, lanes), 0) == length - 1
    d_cum = d_cum + jnp.where(at_last, row_sums[0:1, :], 0.0)
    row = lax.broadcasted_iota(jnp.int32, (length, length), 0)
    col = lax.broadcasted_iota(jnp.int32, (length, length), 1)
    d_log = tri_sum((row <= col).astype(bf16), d_cum, head_lane)
    rate = jnp.exp(head_ref[1:2, :])
    d_steps = dot(direct_ref[...], summing) - rate * d_log
    d_raw = jnp.where(head_lane, d_steps * sigmoid(shifted), 0.0)
    dproj_ref[:, conv_dim : conv_dim + lanes] = d_raw.astype(bf16)
    head_row = slice(taps + 3, taps + 4)
    dconv_ref[head_row, :lanes] += jnp.sum(d_raw, axis=0, keepdims=True)
    dconv_ref[head_row, lanes : 2 * lanes] += jnp.sum(d_log * steps, axis=0, keepdims=True) * (
        -rate
    )
    dconv_ref[head_row, 2 * lanes : 3 * lanes] += row_sums[1:2, :]

    @pl.when(step == pl.num_programs(1) - 1)
    def _():
        end_ref[...] = grad_ref[...]
        lead_ref[...] = dsx_ref[:, 0:8, :]


def input_grad_kernel(
    core_ref,
    x_ref,
    dgate_ref,
    dproj_ref,
    small_ref,
    dsmall_in_ref,
    wg_own,
    wg_other,
    wa_own,
    wa_other,
    wb_own,
    wb_other,
    dx_ref,
    dsmall_ref,
    a_send,
    a_keep,
    b_send,
    b_keep,
    normed_ref,
    a_sum,
    b_sum,
    wg_ref,
    wa_ref,
    wb_ref,
    wg_sems,
    wa_sems,
    wb_sems,
    *,
    gain_row,
):
    first = jnp.logical_and(pl.program_id(0) == 0, pl.program_id(1) == 0)
    width = x_ref.shape[1]

    @pl.when(first)
    def _():
        copies = fetch_weight(core_ref, wg_own, wg_other, wg_ref, wg_sems)
        copies += fetch_weight(core_ref, wa_own, wa_other, wa_ref, wa_sems)
        copies += fetch_weight(core_ref, wb_own, wb_other, wb_ref, wb_sems)
        dsmall_ref[...] = dsmall_in_ref[...]
        a_sum[...] = jnp.zeros_like(a_sum)
        b_sum[...] = jnp.zeros_like(b_sum)
        for copy in copies:
            copy.wait()

    wide_a = wa_ref.shape[1]
    d_normed = (
        dot(dgate_ref[...], wg_ref[...], 1, 1)
        + dot(dproj_ref[:, :wide_a], wa_ref[...], 1, 1)
        + dot(dproj_ref[:, wide_a:], wb_ref[...], 1, 1)
    )
    rows = x_ref[...].astype(f32)
    scale = lax.rsqrt(jnp.mean(rows * rows, axis=-1, keepdims=True) + norm_eps)
    scaled = rows * scale
    dsmall_ref[gain_row : gain_row + 1, :width] += jnp.sum(
        scaled * d_normed, axis=0, keepdims=True
    )
    gain = small_ref[gain_row : gain_row + 1, :width]
    normed_ref[...] = (scaled * gain).astype(bf16)
    add_product(a_sum, normed_ref, dproj_ref[:, :wide_a])
    add_product(b_sum, normed_ref, dproj_ref[:, wide_a:])
    inner_grad = gain * d_normed
    cross = jnp.mean(scaled * inner_grad, axis=-1, keepdims=True)
    dx_ref[...] = (scale * (inner_grad - scaled * cross)).astype(bf16)
    last = jnp.logical_and(
        pl.program_id(0) == pl.num_programs(0) - 1, pl.program_id(1) == pl.num_programs(1) - 1
    )

    @pl.when(last)
    def _():
        hand_out(core_ref[0], a_sum, a_send, a_keep)
        hand_out(core_ref[0], b_sum, b_send, b_keep)


def adam_kernel(
    rates_ref,
    *refs,
    heads,
    taps,
    at_refs,
    arrivals,
):
    sum_refs, refs = refs[:arrivals], refs[arrivals:]
    rest_refs, front_refs, refs = refs[:arrivals], refs[arrivals : 2 * arrivals], refs[2 * arrivals :]
    ins, outs = refs[:18], refs[18:]
    learn_rate, decay_rate = rates_ref[0], rates_ref[3]
    beta_one, beta_two = rates_ref[1], rates_ref[2]
    first_scale, second_scale = rates_ref[4], rates_ref[5]

    def update(which, grad, index):
        master, first, second = (ref[index] for ref in ins[3 * which : 3 * which + 3])
        new_first = beta_one * first + (1.0 - beta_one) * grad
        new_second = beta_two * second + (1.0 - beta_two) * grad * grad
        change = -learn_rate * (
            (new_first * first_scale) / (jnp.sqrt(new_second * second_scale) + adam_eps)
            + decay_rate * master
        )
        where = at_refs[which]
        outs[where][index] = master + change if which in (1, 4) else change
        outs[where + 1][index] = new_first
        outs[where + 2][index] = new_second
        if which in (1, 4):
            outs[-2 if which == 1 else -1][index] = (master + change).astype(bf16)

    everything = (slice(None), slice(None))
    rest, front = rest_refs[0][...], front_refs[0][...]
    inner = rest.shape[1] // 2
    for rest_ref, front_ref in zip(rest_refs[1:], front_refs[1:]):
        rest = rest + rest_ref[...].astype(f32)
        front = front + front_ref[...].astype(f32)
    proj = ins[3].shape[1]
    update(1, rest[:, :inner], (slice(None), slice(0, inner)))
    update(1, front[:, : proj - inner], (slice(None), slice(inner, proj)))
    rows = rest.shape[0]
    half = inner // 2
    update(4, rest[:, inner : inner + half], (slice(0, rows), slice(None)))
    update(4, rest[:, inner + half :], (slice(rows, 2 * rows), slice(None)))
    me = rates_ref[6].astype(jnp.int32)

    place = rates_ref[7].astype(jnp.int32)
    terms = [ref[...] for ref in sum_refs]
    sums = terms[0]
    for term in terms[1:]:
        sums = sums + term

    def own(at, count):
        wide = sums.shape[1]
        shift = lax.rem(wide - me * count, wide)
        return pltpu.roll(sums, shift, 1)[at, :count]

    update(0, own(slice(taps + 1, taps + 2), ins[0].shape[1]), everything)
    update(2, own(slice(0, taps + 1), ins[6].shape[1]), everything)
    update(3, own(slice(taps + 2, taps + 3), ins[9].shape[1]), everything)
    sums = jnp.zeros_like(sums)
    for source in range(arrivals):
        distance = lax.rem(place + arrivals - source, arrivals)
        term = terms[0]
        for which in range(1, arrivals):
            term = jnp.where(distance == which, terms[which], term)
        sums = sums + term
    head_row = slice(taps + 3, taps + 4)
    for row in range(3):
        grad = sums[head_row, row * lanes : row * lanes + heads]
        update(5, grad, (slice(row, row + 1), slice(None)))


def whole(shape):
    return pl.BlockSpec(shape, lambda p, b: (0,) * len(shape))


def by_block(shape, size, back=False):
    if back:
        return pl.BlockSpec(shape, lambda p, s: (p * size + (size - 1 - s), 0))
    return pl.BlockSpec(shape, lambda p, b: (p * size + b, 0))


def by_part(shape):
    return pl.BlockSpec(shape, lambda p, b: (p, 0))


def params():
    return pltpu.CompilerParams(
        dimension_semantics=("arbitrary", "arbitrary"), vmem_limit_bytes=vmem_bytes
    )


def cost(flops, moved, powers):
    return pl.CostEstimate(flops=flops, bytes_accessed=moved, transcendentals=powers)


ANY = pl.BlockSpec(memory_space=pl.ANY)
SMEM = pl.BlockSpec(memory_space=pltpu.SMEM)


def weight_scratch(*weights):
    wholes = [
        pltpu.VMEM((2 * own.shape[0] * own.shape[1], own.shape[2]), bf16) for own, _ in weights
    ]
    return wholes + [pltpu.SemaphoreType.DMA((2 * own.shape[0],)) for own, _ in weights]


def handed_out(rows, columns, blocks):
    shape = (blocks, rows // (2 * blocks), columns)
    return [jax.ShapeDtypeStruct(shape, bf16), jax.ShapeDtypeStruct(shape, f32)]


def mixer_forward(dims, core, tokens, wa, wb, small, head, skip, edge, start, grouped, kept, blocks):
    part, size, piece, width, inner, heads, taps = dims
    first, count = blocks
    conv_dim = small.shape[1]
    state_dim = (conv_dim - inner) // 2
    all_blocks = part * size
    rows = all_blocks * piece
    ext_rows = piece + 8
    chunks = conv_dim // lanes
    resumed = kept is not None

    def by_block(shape):
        return pl.BlockSpec(shape, lambda p, b: (p * size + first + b, 0))

    tail_block = pl.BlockSpec((chunks, 8, lanes), lambda p, b: (p, 0, 0))
    before = core
    if resumed:
        *arrays, start, before = kept
    else:
        arrays = []
    return pl.pallas_call(
        partial(
            mixer_forward_kernel,
            heads=heads,
            inner=inner,
            taps=taps,
            grouped=grouped,
            resumed=resumed,
        ),
        grid=(part, count),
        in_specs=[
            SMEM,
            by_block((piece, width)),
            by_part((8, width)) if grouped else ANY,
            ANY,
            ANY,
            ANY,
            ANY,
            whole(small.shape),
            whole(head.shape),
            whole(skip.shape),
            by_part((state_dim, inner)) if grouped or resumed else ANY,
            tail_block if resumed else ANY,
        ]
        + [ANY] * len(arrays),
        out_specs=[
            by_block((piece, width)),
            pl.BlockSpec((chunks, ext_rows, lanes), lambda p, b: (p * size + first + b, 0, 0)),
            by_block((piece, lanes)),
            by_block((piece, lanes)),
            by_block((piece, inner)),
            by_block((state_dim, inner)),
            by_part((state_dim, inner)),
            tail_block,
        ],
        out_shape=[
            jax.ShapeDtypeStruct((rows, width), bf16),
            jax.ShapeDtypeStruct((all_blocks * chunks, ext_rows, lanes), f32),
            jax.ShapeDtypeStruct((rows, lanes), f32),
            jax.ShapeDtypeStruct((rows, lanes), f32),
            jax.ShapeDtypeStruct((rows, inner), f32),
            jax.ShapeDtypeStruct((all_blocks * state_dim, inner), bf16),
            jax.ShapeDtypeStruct((part * state_dim, inner), f32),
            jax.ShapeDtypeStruct((part * chunks, 8, lanes), f32),
        ],
        scratch_shapes=[
            pltpu.VMEM((chunks, 8, lanes), f32),
            pltpu.VMEM((state_dim, inner), f32),
            pltpu.VMEM((piece, inner), f32),
            pltpu.VMEM((piece, inner), bf16),
        ]
        + weight_scratch(wa, wb),
        input_output_aliases={12 + at: at for at in range(len(arrays))},
        compiler_params=params(),
        cost_estimate=cost(1, 1, 0),
    )(core, tokens, edge, *wa, *wb, small, head, skip, start, before, *arrays)


def gate_step(dims, core, normed, tokens, cots_b, y, wg, wo, small):
    part, size, piece, width, inner, heads, taps = dims
    rows = part * size * piece
    blocks = wo[0].shape[0]
    handed = handed_out(inner, width, blocks) + handed_out(width, inner, blocks)
    wide_b = cots_b.shape[1]
    at_a = width // (width - wide_b)
    return pl.pallas_call(
        partial(gate_kernel, gain_row=taps + 2),
        grid=(part, size),
        in_specs=[
            SMEM,
            by_block((piece, width), size),
            by_block((piece, width), size),
            pl.BlockSpec((piece, width - wide_b), lambda p, b: (p * size + b, at_a)),
            by_block((piece, wide_b), size),
            by_block((piece, inner), size),
            ANY,
            ANY,
            ANY,
            ANY,
            whole(small.shape),
        ],
        out_specs=[
            by_block((piece, width), size),
            by_block((piece, inner), size),
            by_block((piece, inner), size),
            whole((8, inner)),
        ]
        + [whole(array.shape) for array in handed],
        out_shape=[
            jax.ShapeDtypeStruct((rows, width), bf16),
            jax.ShapeDtypeStruct((rows, inner), bf16),
            jax.ShapeDtypeStruct((rows, inner), bf16),
            jax.ShapeDtypeStruct((8, inner), f32),
        ]
        + handed,
        scratch_shapes=[
            pltpu.VMEM((piece, inner), f32),
            pltpu.VMEM((piece, inner), f32),
            pltpu.VMEM((piece, inner), bf16),
            pltpu.VMEM((piece, width), bf16),
            pltpu.VMEM((inner, width), f32),
            pltpu.VMEM((width, inner), f32),
        ]
        + weight_scratch(wg, wo),
        compiler_params=params(),
        cost_estimate=cost(1, 1, 0),
    )(core, normed, tokens, tokens, cots_b, y, *wg, *wo, small)


def mixer_backward(dims, saved, consts, carry, blocks, fresh):
    part, size, piece, width, inner, heads, taps = dims
    first, count = blocks
    small, head, skip, summing, dgain = consts
    conv_dim = small.shape[1]
    state_dim = (conv_dim - inner) // 2
    ext_rows = piece + 8
    chunks = conv_dim // lanes
    wide = conv_dim + lanes
    dproj, dsmall, state, lead = carry
    lead_block = pl.BlockSpec((chunks, 8, lanes), lambda p, s: (p, 0, 0))

    def by_block(shape):
        return pl.BlockSpec(shape, lambda p, s: (p * size + (first + count - 1 - s), 0))

    return pl.pallas_call(
        partial(mixer_backward_kernel, heads=heads, inner=inner, taps=taps, fresh=fresh),
        grid=(part, count),
        in_specs=[
            pl.BlockSpec(
                (chunks, ext_rows, lanes), lambda p, s: (p * size + (first + count - 1 - s), 0, 0)
            ),
            by_block((piece, lanes)),
            by_block((piece, lanes)),
            by_block((piece, inner)),
            by_block((state_dim, inner)),
            by_block((piece, inner)),
            whole(small.shape),
            whole(head.shape),
            whole(skip.shape),
            whole(summing.shape),
            ANY if fresh else by_part((state_dim, inner)),
            ANY if fresh else lead_block,
            whole(dsmall.shape),
            whole(dgain.shape),
            ANY,
        ],
        out_specs=[
            by_block((piece, wide)),
            whole((8, conv_dim)),
            by_part((state_dim, inner)),
            lead_block,
        ],
        out_shape=[
            jax.ShapeDtypeStruct((part * size * piece, wide), bf16),
            jax.ShapeDtypeStruct((8, conv_dim), f32),
            jax.ShapeDtypeStruct((part * state_dim, inner), f32),
            jax.ShapeDtypeStruct((part * chunks, 8, lanes), f32),
        ],
        scratch_shapes=[
            pltpu.VMEM((state_dim, inner), f32),
            pltpu.VMEM((chunks, ext_rows, lanes), f32),
            pltpu.VMEM((piece, inner), f32),
            pltpu.VMEM((piece, inner), bf16),
            pltpu.VMEM((piece, inner), bf16),
            pltpu.VMEM((piece, inner), bf16),
            pltpu.VMEM((piece, inner), bf16),
            pltpu.VMEM((piece, inner), bf16),
            pltpu.VMEM((8, inner), f32),
        ],
        input_output_aliases={14: 0} if dproj.shape[0] == part * size * piece else {},
        compiler_params=params(),
        cost_estimate=cost(1, 1, 0),
    )(*saved, small, head, skip, summing, state, lead, dsmall, dgain, dproj)


def input_grad(dims, core, tokens, dgate, dproj, small, dsmall, wg, wa, wb):
    part, size, piece, width, inner, heads, taps = dims
    rows = part * size * piece
    blocks = wa[0].shape[0]
    wide_a, wide_b = wa[0].shape[2], wb[0].shape[2]
    handed = handed_out(width, wide_a, blocks) + handed_out(width, wide_b, blocks)
    return pl.pallas_call(
        partial(input_grad_kernel, gain_row=taps + 1),
        grid=(part, size),
        in_specs=[
            SMEM,
            by_block((piece, width), size),
            by_block((piece, inner), size),
            by_block((piece, dproj.shape[1]), size),
            whole(small.shape),
            whole(dsmall.shape),
            ANY,
            ANY,
            ANY,
            ANY,
            ANY,
            ANY,
        ],
        out_specs=[by_block((piece, width), size), whole(dsmall.shape)]
        + [whole(array.shape) for array in handed],
        out_shape=[
            jax.ShapeDtypeStruct((rows, width), bf16),
            jax.ShapeDtypeStruct(dsmall.shape, f32),
        ]
        + handed,
        scratch_shapes=[
            pltpu.VMEM((piece, width), bf16),
            pltpu.VMEM((width, wide_a), f32),
            pltpu.VMEM((width, wide_b), f32),
        ]
        + weight_scratch(wg, wa, wb),
        compiler_params=params(),
        cost_estimate=cost(1, 1, 0),
    )(core, tokens, dgate, dproj, small, dsmall, *wg, *wa, *wb)


def adam(rates, sums, gate_grads, front_grads, states, heads, taps):
    outs = []
    at_refs = []
    for which, (master, first, second) in enumerate(states):
        at_refs.append(len(outs))
        outs += [jax.ShapeDtypeStruct(master.shape, f32)] * 3
    outs.append(jax.ShapeDtypeStruct(states[1][0].shape, bf16))
    outs.append(jax.ShapeDtypeStruct(states[4][0].shape, bf16))
    flat = [array for state in states for array in state]
    vmem = pl.BlockSpec(memory_space=pltpu.VMEM)
    return pl.pallas_call(
        partial(
            adam_kernel, heads=heads, taps=taps, at_refs=at_refs, arrivals=len(gate_grads)
        ),
        in_specs=[SMEM] + [vmem] * (3 * len(gate_grads) + len(flat)),
        out_specs=[vmem] * len(outs),
        out_shape=outs,
        compiler_params=pltpu.CompilerParams(vmem_limit_bytes=vmem_bytes),
        cost_estimate=cost(1, 1, 0),
    )(rates, *sums, *gate_grads, *front_grads, *flat)


def bit_count(extent):
    count = extent.bit_length() - 1
    if 1 << count != extent:
        raise ValueError(extent)
    return count


def swap(block, axis, bit):
    devices = range(lax.axis_size(axis))
    return lax.ppermute(block, axis, [(i, i ^ (1 << bit)) for i in devices])


def shifted_by(block, axis, distance):
    devices = range(lax.axis_size(axis))
    route = [(i, i + distance) for i in devices if i + distance in devices]
    return lax.ppermute(block, axis, route)


def pick(block, at, axis):
    return lax.dynamic_index_in_dim(block, at, axis, keepdims=False)


def gather_bit(block, axis, bit, at, *others):
    mine = (lax.axis_index(axis) >> bit) & 1
    other = swap(block, axis, bit)
    if others:
        other = after(other, *others)
    low = jnp.where(mine == 1, other, block)
    high = jnp.where(mine == 1, block, other)
    return jnp.stack([low, high], axis=at)


def gather_seq(shard):
    block = shard
    for done, bit in enumerate(reversed(range(bit_count(lax.axis_size("seq"))))):
        block = gather_bit(block, "seq", bit, done)
    return block.reshape((-1,) + shard.shape)


def dp_orders():
    bits = bit_count(lax.axis_size("dp"))
    return list(range(bits - 1, 0, -1)) + [0], list(range(1, bits)) + [0]


def gather_dp_bit(block, order, step, *others):
    at = sum(1 for b in order[:step] if b > order[step])
    return gather_bit(block, "dp", order[step], at, *others)


def give_half(block, axis, bit, at):
    mine = (lax.axis_index(axis) >> bit) & 1
    other = swap(pick(block, 1 - mine, at).astype(bf16), axis, bit)
    return pick(block, mine, at) + other.astype(f32)


def core_sums(send, keep):
    extent = lax.axis_size("seq")
    bits = bit_count(lax.axis_size("dp")) - 1
    shape = (2,) * bits + (extent, -1, send.shape[2])
    other = swap(send, "dp", 0)
    return keep.reshape(shape), other.reshape(shape)


def core_and_next(keep, other, order):
    bit = order[-2]
    at = sum(1 for b in order[:-2] if b > bit)
    mine = (lax.axis_index("dp") >> bit) & 1
    sent = pick(keep, 1 - mine, at) + pick(other, 1 - mine, at).astype(f32)
    arrived = swap(sent.astype(bf16), "dp", bit)
    return pick(keep, mine, at) + pick(other, mine, at).astype(f32), arrived


def scatter_dp_bit(block, order, step):
    bit = order[-1 - step]
    return give_half(block, "dp", bit, sum(1 for b in order[: len(order) - 1 - step] if b > bit))


def scatter_seq(block):
    extent = lax.axis_size("seq")
    place = lax.axis_index("seq")
    arrivals = [pick(block, place, 0)]
    for distance in range(1, extent):
        sent = pick(block, lax.rem(place + distance, extent), 0).astype(bf16)
        route = [(i, (i + distance) % extent) for i in range(extent)]
        arrivals.append(lax.ppermute(sent, "seq", route))
    return arrivals


def sum_over(block, axis, *others):
    for bit in reversed(range(bit_count(lax.axis_size(axis)))):
        if bit == 0 and others:
            block = after(block, *others)
        block = block + swap(block, axis, bit)
    return block


def seq_groups(size):
    extent = lax.axis_size("seq")
    if size == extent:
        return None
    return [list(range(at, at + size)) for at in range(0, extent, size)]


def to_sequences(block, part, size):
    if size > 1:
        block = lax.all_to_all(
            block, "seq", 0, 0, axis_index_groups=seq_groups(size), tiled=True
        )
    piece, width = block.shape[1:]
    block = block.reshape(size, part, piece, width)
    if part > 1:
        block = block.transpose(1, 0, 2, 3)
    return block.reshape(-1, width)


def to_pieces(rows, part, size, piece):
    block = rows.reshape(part, size, piece, -1)
    if part > 1:
        block = block.transpose(1, 0, 2, 3)
    block = block.reshape(part * size, piece, -1)
    if size > 1:
        block = lax.all_to_all(
            block, "seq", 0, 0, axis_index_groups=seq_groups(size), tiled=True
        )
    return block


def after(value, *others):
    return lax.optimization_barrier((value,) + others)[0]


def padded(block, rows, columns):
    return jnp.pad(block, ((0, rows - block.shape[0]), (0, columns - block.shape[1])))


def summing_matrix(inner, heads):
    columns = np.zeros((inner, lanes), np.float32)
    columns[np.arange(inner), np.arange(inner) // (inner // heads)] = 1.0
    return jnp.asarray(columns, bf16)


def local(
    layer_in,
    out_grad,
    norm_gain,
    in_weight,
    conv_params,
    gate_gain,
    out_weight,
    head_params,
    norm_first,
    norm_second,
    in_first,
    in_second,
    conv_first,
    conv_second,
    gate_first,
    gate_second,
    out_first,
    out_second,
    head_first,
    head_second,
    step_count,
    hyper,
):
    seq_count, piece, width = layer_in.shape
    seq_extent = lax.axis_size("seq")
    me = lax.axis_index("dp") * seq_extent + lax.axis_index("seq")
    step_float = step_count[0].astype(f32)
    scales = 1.0 / (1.0 - hyper[1:3] ** step_float)
    place = lax.axis_index("seq")
    rates = jnp.concatenate([hyper, scales, jnp.stack([me.astype(f32), place.astype(f32)])])
    core = (lax.axis_index("dp") & 1).astype(jnp.int32)[None]
    owners = lax.axis_size("dp") * seq_extent
    size = math.gcd(seq_extent, seq_count)
    part = seq_count // size
    groups = seq_extent // size
    inner = out_weight.shape[0] * owners
    heads = head_params.shape[1]
    tap_rows, conv_own = conv_params.shape
    taps = tap_rows - 1
    conv_dim = conv_own * owners
    state_dim = (conv_dim - inner) // 2
    own_rows = in_weight.shape[0]
    gate_own = gate_gain.shape[0]
    wide_a = min(1024, inner)
    dims = (part, size, piece, width, inner, heads, taps)

    head = padded(head_params, 8, lanes)
    skip = jnp.repeat(head_params[2], inner // heads)[None, :]
    summing = summing_matrix(inner, heads)

    in_low = padded(in_weight.astype(bf16), own_rows, inner + conv_dim + lanes)
    out_low_own = out_weight.astype(bf16).reshape(2, own_rows, width)
    own_small = jnp.concatenate(
        [
            padded(conv_params.astype(bf16), tap_rows, lanes),
            padded(norm_gain.astype(bf16)[None, :], 1, lanes),
            padded(gate_gain.astype(bf16)[None, :], 1, lanes),
        ]
    )
    shard = jnp.concatenate([in_low, out_low_own[0], out_low_own[1]], axis=1)
    half = width // 2
    both = jnp.concatenate([layer_in, out_grad[:, :, :half]], axis=2)
    if own_rows >= tap_rows + 2:
        shard = jnp.concatenate([shard, padded(own_small, own_rows, lanes)], axis=1)
        gathered = gather_seq(shard)
        seq_small = gathered[:, : tap_rows + 2, -lanes:]
    else:
        gathered = gather_seq(shard)
        seq_small = gather_seq(padded(own_small, 8, lanes))[:, : tap_rows + 2]
    tokens = to_sequences(after(both, shard), part, size)
    small = jnp.zeros((8, conv_dim), bf16)
    group = lax.axis_index("dp")
    for at, rows, count in (
        (0, tap_rows, conv_own),
        (tap_rows, 1, own_rows),
        (tap_rows + 1, 1, gate_own),
    ):
        piece_rows = jnp.concatenate(
            [seq_small[z, at : at + rows, :count] for z in range(seq_extent)], axis=1
        )
        small = lax.dynamic_update_slice(small, piece_rows, (at, group * seq_extent * count))
    front_end = inner + conv_dim + lanes
    wg = gathered[:, :, :inner]
    wa = gathered[:, :, inner : inner + wide_a]
    wb = gathered[:, :, inner + wide_a : front_end]
    wo = jnp.stack(
        [
            gathered[:, :, front_end : front_end + width],
            gathered[:, :, front_end + width : front_end + 2 * width],
        ],
        axis=1,
    ).reshape(-1, 2 * own_rows, width)
    order_a, order_b = dp_orders()
    last = len(order_a) - 1
    for step in range(last):
        wa = gather_dp_bit(wa, order_a, step)
        wb = gather_dp_bit(wb, order_b, step)
    wg, wo = after((wg, wo), wa, wb)

    def core_halves(block):
        block = block.reshape(owners // 2 // seq_extent, -1, block.shape[-1])
        return block, swap(block, "dp", 0)

    wb = core_halves(wb)
    wa = core_halves(wa)
    small = sum_over(small, "dp", tokens, wa, wb, head, skip).astype(f32)
    for step in range(last - 1):
        wg = gather_dp_bit(wg, order_a, step)
        wo = gather_dp_bit(wo, order_b, step)
    cots_b = to_sequences(after(out_grad, tokens)[:, :, half:], part, size)

    edge = core
    if groups > 1:
        edge = tokens.reshape(part, size * piece, -1)[:, size * piece - 8 :, :width]
        edge = shifted_by(edge, "seq", size).reshape(part * 8, width)

    def forward(start, kept, blocks):
        weights = (wa, wb, small, head, skip)
        grouped = groups > 1
        return mixer_forward(dims, core, tokens, *weights, edge, start, grouped, kept, blocks)

    start = core
    if groups > 1:
        first_out = forward(jnp.zeros((part * state_dim, inner), f32), None, (0, size))
        cum_last = first_out[3].reshape(part, size, piece, lanes)[:, :, piece - 1, :heads]
        decay = jnp.exp2(jnp.sum(cum_last, axis=1))
        decay = jnp.repeat(decay, inner // heads, axis=1)[:, None, :]

        def relay(ends, distance):
            ends = ends.reshape(part, state_dim, inner)
            carried = jnp.zeros_like(ends)
            for _ in range(groups - 1):
                sent = (decay * carried + ends).astype(bf16)
                carried = shifted_by(sent, "seq", distance).astype(f32)
            return carried.reshape(part * state_dim, inner)

        start = relay(first_out[6], size)
    normed, ext, dtr, cum, y, sin, _, _ = forward(start, None, (0, size))
    wg = core_halves(gather_dp_bit(wg, order_a, last - 1, normed))
    wo = core_halves(gather_dp_bit(wo, order_b, last - 1, normed))
    layer_rows, dy, dgate, dgain, *handed = gate_step(
        dims, core, normed, tokens, cots_b, y, wg, wo, small
    )
    layer_out = to_pieces(layer_rows, part, size, piece)
    consts = (small, head, skip, summing, dgain)
    saved = (ext, dtr, cum, y, sin, dy)

    def backward(carry, block, fresh=False):
        return list(mixer_backward(dims, saved, consts, carry, (block, 1), fresh))

    def fresh_carry():
        if groups == 1:
            return (core, head, core, core)
        lead = jnp.zeros((part * (conv_dim // lanes), 8, lanes), f32)
        first_out = (core, head, jnp.zeros((part * state_dim, inner), f32), lead)
        for block in reversed(range(size)):
            first_out = backward(first_out, block)
        return (core, head, relay(first_out[2], -size), lead)

    g_out = core_sums(*handed[:2])
    g_gate = core_sums(*handed[2:])
    carry = backward(fresh_carry(), size - 1, groups == 1)
    for block in reversed(range(size - 1)):
        carry[2], g_out, g_gate = lax.optimization_barrier((carry[2], g_out, g_gate))
        step = size - 2 - block
        if step == 0:
            g_out = core_and_next(*g_out, order_a)
            g_gate = core_and_next(*g_gate, order_b)
        elif step == 1:
            g_out = g_out[0] + g_out[1].astype(f32)
            g_gate = g_gate[0] + g_gate[1].astype(f32)
            for bit_step in range(2, last + 1):
                g_out = scatter_dp_bit(g_out, order_a, bit_step)
                g_gate = scatter_dp_bit(g_gate, order_b, bit_step)
        elif step == 2:
            g_rest = scatter_seq(
                jnp.concatenate([g_gate, g_out[:, :own_rows], g_out[:, own_rows:]], axis=2)
            )
        carry = backward(carry, block)
    dproj, dsmall, _, lead = carry
    if groups > 1:
        lead = shifted_by(lead.astype(bf16), "seq", -size).astype(f32)
        lead = lead.reshape(part, -1, 8, lanes).transpose(0, 2, 1, 3).reshape(part, 8, conv_dim)
        fixes = []
        for row in range(taps - 1):
            terms = [small[tap] * lead[:, row - tap] for tap in range(row + 1)]
            fixes.append(sum(terms[1:], terms[0]))
        fix = jnp.pad(jnp.stack(fixes, axis=1), ((0, 0), (0, 0), (0, lanes)))
        dproj = dproj.reshape(part, size * piece, conv_dim + lanes)
        ends = dproj[:, size * piece - (taps - 1) :].astype(f32) + fix
        dproj = dproj.at[:, size * piece - (taps - 1) :].set(ends.astype(bf16))
        dproj = dproj.reshape(-1, conv_dim + lanes)
    tokens, g_rest = lax.optimization_barrier((after(tokens, layer_out, dproj), g_rest))
    dx, dsmall, *handed = input_grad(dims, core, tokens, dgate, dproj, small, dsmall, wg, wa, wb)
    g_a = core_sums(*handed[:2])
    g_b = core_sums(*handed[2:])
    g_a = core_and_next(*g_a, order_a)
    g_b = core_and_next(*g_b, order_b)
    g_a = g_a[0] + g_a[1].astype(f32)
    g_b = g_b[0] + g_b[1].astype(f32)
    for step in range(2, last + 1):
        g_a = scatter_dp_bit(g_a, order_a, step)
        g_b = scatter_dp_bit(g_b, order_b, step)
    g_front = scatter_seq(jnp.concatenate([g_a, g_b], axis=2))
    in_grad = out_grad.astype(f32) + to_pieces(dx, part, size, piece).astype(f32)
    dsmall = sum_over(dsmall, "dp")
    sums = [dsmall]
    for distance in range(1, seq_extent):
        route = [(i, (i + distance) % seq_extent) for i in range(seq_extent)]
        sums.append(lax.ppermute(dsmall, "seq", route))

    states = (
        (norm_gain[None, :], norm_first[None, :], norm_second[None, :]),
        (in_weight, in_first, in_second),
        (conv_params, conv_first, conv_second),
        (gate_gain[None, :], gate_first[None, :], gate_second[None, :]),
        (out_weight, out_first, out_second),
        (head_params, head_first, head_second),
    )
    new = adam(rates, sums, g_rest, g_front, states, heads, taps)
    new = [array[0] if array.shape[0] == 1 else array for array in new]
    return (layer_out, in_grad, *new)


def solution(mesh):
    in_specs = (
        P("dp", "seq", None),
        P("dp", "seq", None),
        P(("dp", "seq")),
        P(("dp", "seq"), None),
        P(None, ("dp", "seq")),
        P(("dp", "seq")),
        P(("dp", "seq"), None),
        P(),
        P(("dp", "seq")),
        P(("dp", "seq")),
        P(("dp", "seq"), None),
        P(("dp", "seq"), None),
        P(None, ("dp", "seq")),
        P(None, ("dp", "seq")),
        P(("dp", "seq")),
        P(("dp", "seq")),
        P(("dp", "seq"), None),
        P(("dp", "seq"), None),
        P(),
        P(),
        P(),
        P(),
    )
    out_specs = (
        P("dp", "seq", None),
        P("dp", "seq", None),
        P(("dp", "seq")),
        P(("dp", "seq")),
        P(("dp", "seq")),
        P(("dp", "seq"), None),
        P(("dp", "seq"), None),
        P(("dp", "seq"), None),
        P(None, ("dp", "seq")),
        P(None, ("dp", "seq")),
        P(None, ("dp", "seq")),
        P(("dp", "seq")),
        P(("dp", "seq")),
        P(("dp", "seq")),
        P(("dp", "seq"), None),
        P(("dp", "seq"), None),
        P(("dp", "seq"), None),
        P(),
        P(),
        P(),
        P(("dp", "seq"), None),
        P(("dp", "seq"), None),
    )
    return jax.shard_map(local, mesh=mesh, in_specs=in_specs, out_specs=out_specs, check_vma=False)
```

```python
import math
from functools import partial

import jax
import jax.numpy as jnp
import numpy as np
from jax import lax
from jax.experimental import pallas as pl
from jax.experimental.pallas import tpu as pltpu
from jax.sharding import PartitionSpec as P

norm_eps = 1e-05
adam_eps = 1e-08
log2e = math.log2(math.e)
lanes = 128
vmem_bytes = 56 * 1024 * 1024
f32 = jnp.float32
bf16 = jnp.bfloat16


def dot(left, right, left_dim=1, right_dim=0):
    return lax.dot_general(
        left, right, (((left_dim,), (right_dim,)), ((), ())), preferred_element_type=f32
    )


def halves(value):
    high = value.astype(bf16)
    return high, (value - high.astype(f32)).astype(bf16)


def sigmoid(value):
    return 0.5 * jnp.tanh(0.5 * value) + 0.5


def column(ref_value, at, width):
    return jnp.broadcast_to(ref_value[:, at : at + 1], (ref_value.shape[0], width))


def pair_columns(value, pair, low_lane):
    rows = value.shape[0]
    first = column(value, 2 * pair, lanes)
    second = column(value, 2 * pair + 1, lanes)
    return jnp.where(low_lane, first, second), first, second


def tri_sum(mask, value, head_lane):
    high = value.astype(bf16).astype(f32)
    rest = value - high
    mid = rest.astype(bf16).astype(f32)
    low = rest - mid
    packed = high + pltpu.roll(mid, 32, 1) + pltpu.roll(low, 64, 1)
    summed = dot(mask, packed.astype(bf16))
    total = summed + pltpu.roll(summed, lanes - 32, 1) + pltpu.roll(summed, lanes - 64, 1)
    return jnp.where(head_lane, total, 0.0)


def conv_chunk(ext_ref, conv_ref, at, length, taps):
    summed = conv_ref[taps : taps + 1, at : at + lanes]
    base = 8 - (taps - 1)
    for tap in range(taps):
        summed = (
            summed
            + conv_ref[tap : tap + 1, at : at + lanes]
            * ext_ref[at // lanes, base + tap : base + tap + length, :]
        )
    return summed


def put_columns(ext_ref, rows, values, chunk):
    for at in range(0, values.shape[1], lanes):
        ext_ref[chunk + at // lanes, rows, :] = values[:, at : at + lanes]


def step_sizes(dt_raw, head_ref, head_lane):
    shifted = dt_raw + head_ref[0:1, :]
    steps = jnp.maximum(shifted, 0.0) + jnp.log1p(jnp.exp(-jnp.abs(shifted)))
    return jnp.where(head_lane, steps, 0.0), shifted


def fetch_weight(core_ref, own_ref, other_ref, whole_ref, sems):
    blocks, rows, _ = own_ref.shape
    core = core_ref[0]
    copies = []
    for block in range(blocks):
        for which, source in ((core, own_ref), (1 - core, other_ref)):
            at = pl.multiple_of((2 * block + which) * rows, rows)
            copies.append(
                pltpu.make_async_copy(
                    source.at[block], whole_ref.at[pl.ds(at, rows)], sems.at[len(copies)]
                )
            )
    for copy in copies:
        copy.start()
    return copies


def hand_out(core, total_ref, send_ref, keep_ref):
    blocks, rows, _ = send_ref.shape
    for block in range(blocks):
        at = pl.multiple_of((2 * block + 1 - core) * rows, rows)
        send_ref[block] = total_ref[pl.ds(at, rows), :].astype(bf16)
        at = pl.multiple_of((2 * block + core) * rows, rows)
        keep_ref[block] = total_ref[pl.ds(at, rows), :]


def add_product(total_ref, left_ref, right):
    for at in range(0, total_ref.shape[0], 2 * lanes):
        here = slice(at, at + 2 * lanes)
        total_ref[here, :] += dot(left_ref[:, here], right, 0, 0)


def mixer_forward_kernel(
    core_ref,
    x_ref,
    edge_ref,
    wa_own,
    wa_other,
    wb_own,
    wb_other,
    conv_ref,
    head_ref,
    skip_ref,
    start_ref,
    before_ref,
    *refs,
    heads,
    inner,
    taps,
    grouped,
    resumed,
):
    (
        normed_ref,
        ext_ref,
        dtr_ref,
        cum_ref,
        y_ref,
        sin_ref,
        end_ref,
        after_ref,
        tail_ref,
        state_ref,
        carried_ref,
        weighted_ref,
        wa_ref,
        wb_ref,
        wa_sems,
        wb_sems,
    ) = refs[6:] if resumed else refs
    block = pl.program_id(1)
    length, width = x_ref.shape

    @pl.when(jnp.logical_and(pl.program_id(0) == 0, block == 0))
    def _():
        copies = fetch_weight(core_ref, wa_own, wa_other, wa_ref, wa_sems)
        copies += fetch_weight(core_ref, wb_own, wb_other, wb_ref, wb_sems)
        for copy in copies:
            copy.wait()

    half = length // 2
    wide_a = wa_ref.shape[1]
    conv_dim = conv_ref.shape[1]
    state_dim = (conv_dim - inner) // 2

    def norm_of(rows):
        rows = rows.astype(f32)
        scale = lax.rsqrt(jnp.mean(rows * rows, axis=-1, keepdims=True) + norm_eps)
        return (rows * scale * conv_ref[taps + 1 : taps + 2, :width]).astype(bf16)

    @pl.when(block == 0)
    def _():
        if resumed:
            state_ref[...] = start_ref[...]
            tail_ref[...] = before_ref[...]
        elif grouped:
            state_ref[...] = start_ref[...]
            edge = norm_of(edge_ref[...])
            put_columns(tail_ref, slice(0, 8), dot(edge, wa_ref[...]), 0)
            edge_b = dot(edge, wb_ref[...])[:, : conv_dim - wide_a]
            put_columns(tail_ref, slice(0, 8), edge_b, wide_a // lanes)
        else:
            state_ref[...] = jnp.zeros_like(state_ref)
            tail_ref[...] = jnp.zeros_like(tail_ref)

    normed = norm_of(x_ref[...])
    normed_ref[...] = normed
    ext_ref[:, 0:8, :] = tail_ref[...]
    own_rows = slice(8, 8 + length)
    for at in range(0, wide_a, 2 * lanes):
        product = dot(normed, wa_ref[:, at : at + 2 * lanes])
        put_columns(ext_ref, own_rows, product, at // lanes)
    second = dot(normed, wb_ref[...])
    put_columns(ext_ref, own_rows, second[:, : conv_dim - wide_a], wide_a // lanes)
    dt_raw = second[:, conv_dim - wide_a :]
    tail_ref[...] = ext_ref[:, length : length + 8, :]

    lane = lax.broadcasted_iota(jnp.int32, (length, lanes), 1)
    low_lane = lane < lanes // 2
    head_lane = lane < heads
    dtr_ref[...] = dt_raw
    steps, _ = step_sizes(dt_raw, head_ref, head_lane)
    log_decay = steps * (-log2e * jnp.exp(head_ref[1:2, :]))
    row = lax.broadcasted_iota(jnp.int32, (length, length), 0)
    col = lax.broadcasted_iota(jnp.int32, (length, length), 1)
    cum = tri_sum((row >= col).astype(bf16), log_decay, head_lane)
    cum_ref[...] = cum
    cum_rows = cum.T

    def mixed_chunk(at):
        summed = conv_chunk(ext_ref, conv_ref, at, length, taps)
        return summed * sigmoid(summed)

    keys = jnp.concatenate(
        [mixed_chunk(inner + at) for at in range(0, state_dim, lanes)], axis=1
    ).astype(bf16)
    queries = jnp.concatenate(
        [mixed_chunk(inner + state_dim + at) for at in range(0, state_dim, lanes)], axis=1
    ).astype(bf16)
    state_low = state_ref[...].astype(bf16)
    sin_ref[...] = state_low
    carried_ref[...] = dot(queries, state_low)
    square = (half, half)
    diag = lax.broadcasted_iota(jnp.int32, square, 0) >= lax.broadcasted_iota(
        jnp.int32, square, 1
    )
    scores_00 = jnp.where(diag, dot(queries[:half], keys[:half], 1, 1), 0.0)
    scores_10 = dot(queries[half:], keys[:half], 1, 1)
    scores_11 = jnp.where(diag, dot(queries[half:], keys[half:], 1, 1), 0.0)
    for pair in range(heads // 2):
        at = pair * lanes
        values = mixed_chunk(at)
        cum_rep, cum_0, cum_1 = pair_columns(cum, pair, low_lane)
        dt_rep, _, _ = pair_columns(steps, pair, low_lane)
        stepped = values * dt_rep
        last = cum_rep[length - 1 : length, :]
        weighted_ref[:, at : at + lanes] = (stepped * jnp.exp2(last - cum_rep)).astype(bf16)
        top = None
        bottom = None
        for which, cum_col in ((0, cum_0), (1, cum_1)):
            own = jnp.where(low_lane if which == 0 else jnp.logical_not(low_lane), stepped, 0.0)
            own = own.astype(bf16)
            head = 2 * pair + which
            early = cum_rows[head : head + 1, :half]
            late = cum_rows[head : head + 1, half:]
            mix_00 = jnp.exp2(jnp.minimum(cum_col[:half] - early, 0.0)) * scores_00
            mix_10 = jnp.exp2(cum_col[half:] - early) * scores_10
            mix_11 = jnp.exp2(jnp.minimum(cum_col[half:] - late, 0.0)) * scores_11
            part_top = dot(mix_00.astype(bf16), own[:half])
            part_bottom = dot(
                jnp.concatenate([mix_10.astype(bf16), mix_11.astype(bf16)], axis=1), own
            )
            top = part_top if top is None else top + part_top
            bottom = part_bottom if bottom is None else bottom + part_bottom
        rest = (
            jnp.exp2(cum_rep) * carried_ref[:, at : at + lanes]
            + skip_ref[0:1, at : at + lanes] * values
        )
        y_ref[0:half, at : at + lanes] = top + rest[:half]
        y_ref[half:length, at : at + lanes] = bottom + rest[half:]
        state_ref[:, at : at + lanes] = jnp.exp2(last) * state_ref[:, at : at + lanes]

    state_ref[...] += dot(keys, weighted_ref[...], 0, 0)

    @pl.when(block == pl.num_programs(1) - 1)
    def _():
        end_ref[...] = state_ref[...]
        after_ref[...] = tail_ref[...]


def gate_kernel(
    core_ref,
    normed_ref,
    x_ref,
    cot_a_ref,
    cot_b_ref,
    y_ref,
    wg_own,
    wg_other,
    wo_own,
    wo_other,
    small_ref,
    out_ref,
    dy_ref,
    dgate_ref,
    dgain_ref,
    out_send,
    out_keep,
    gate_send,
    gate_keep,
    gate_ref,
    dno_ref,
    low_ref,
    cot_ref,
    out_sum,
    gate_sum,
    wg_ref,
    wo_ref,
    wg_sems,
    wo_sems,
    *,
    gain_row,
):
    length, inner = y_ref.shape
    first = jnp.logical_and(pl.program_id(0) == 0, pl.program_id(1) == 0)

    @pl.when(first)
    def _():
        copies = fetch_weight(core_ref, wg_own, wg_other, wg_ref, wg_sems)
        copies += fetch_weight(core_ref, wo_own, wo_other, wo_ref, wo_sems)
        dgain_ref[...] = jnp.zeros_like(dgain_ref)
        out_sum[...] = jnp.zeros_like(out_sum)
        gate_sum[...] = jnp.zeros_like(gate_sum)
        for copy in copies:
            copy.wait()

    gate_ref[...] = dot(normed_ref[...], wg_ref[...])
    cot_ref[:, : cot_a_ref.shape[1]] = cot_a_ref[...]
    cot_ref[:, cot_a_ref.shape[1] :] = cot_b_ref[...]
    dno_ref[...] = dot(cot_ref[...], wo_ref[...], 1, 1)
    squares = jnp.zeros((length, lanes), f32)
    crosses = jnp.zeros((length, lanes), f32)
    for at in range(0, inner, lanes):
        here = slice(at, at + lanes)
        gate = gate_ref[:, here]
        gated = y_ref[:, here] * (gate * sigmoid(gate))
        squares = squares + gated * gated
        crosses = crosses + gated * (small_ref[gain_row : gain_row + 1, here] * dno_ref[:, here])
    scale = lax.rsqrt(jnp.sum(squares, axis=1, keepdims=True) * (1.0 / inner) + norm_eps)
    cross = scale * scale * scale * (jnp.sum(crosses, axis=1, keepdims=True) * (1.0 / inner))
    scale_b = jnp.broadcast_to(scale, (length, lanes))
    cross_b = jnp.broadcast_to(cross, (length, lanes))
    for at in range(0, inner, lanes):
        here = slice(at, at + lanes)
        gate = gate_ref[:, here]
        mixed_out = y_ref[:, here]
        sig = sigmoid(gate)
        silu = gate * sig
        gated = mixed_out * silu
        scaled = gated * scale_b
        d_out = dno_ref[:, here]
        low_ref[:, here] = (scaled * small_ref[gain_row : gain_row + 1, here]).astype(bf16)
        dgain_ref[0:1, here] += jnp.sum(scaled * d_out, axis=0, keepdims=True)
        d_gated = scale_b * (small_ref[gain_row : gain_row + 1, here] * d_out) - gated * cross_b
        dy_ref[:, here] = (d_gated * silu).astype(bf16)
        dgate_ref[:, here] = (d_gated * mixed_out * (sig * (1.0 + gate * (1.0 - sig)))).astype(
            bf16
        )
    out_ref[...] = (x_ref[...].astype(f32) + dot(low_ref[...], wo_ref[...])).astype(bf16)
    add_product(out_sum, low_ref, cot_ref[...])
    add_product(gate_sum, normed_ref, dgate_ref[...])
    last = jnp.logical_and(
        pl.program_id(0) == pl.num_programs(0) - 1, pl.program_id(1) == pl.num_programs(1) - 1
    )

    @pl.when(last)
    def _():
        hand_out(core_ref[0], out_sum, out_send, out_keep)
        hand_out(core_ref[0], gate_sum, gate_send, gate_keep)


def mixer_backward_kernel(
    ext_ref,
    dtr_ref,
    cum_ref,
    y_ref,
    sin_ref,
    dy_ref,
    conv_ref,
    head_ref,
    skip_ref,
    sum_ref,
    start_ref,
    next_ref,
    small_in_ref,
    dgain_ref,
    _,
    dproj_ref,
    dconv_ref,
    end_ref,
    lead_ref,
    grad_ref,
    dsx_ref,
    dwv_ref,
    dye_ref,
    weighted_ref,
    zhigh_ref,
    zlow_ref,
    direct_ref,
    rows_ref,
    *,
    heads,
    inner,
    taps,
    fresh,
):
    step = pl.program_id(1)
    length = dy_ref.shape[0]
    half = length // 2
    conv_dim = conv_ref.shape[1]
    state_dim = (conv_dim - inner) // 2
    first = jnp.logical_and(pl.program_id(0) == 0, step == 0)

    @pl.when(first)
    def _():
        if small_in_ref.shape == dconv_ref.shape:
            dconv_ref[...] = small_in_ref[...]
        else:
            dconv_ref[...] = jnp.zeros_like(dconv_ref)
            dconv_ref[taps + 2 : taps + 3, :inner] = dgain_ref[0:1, :]
        rows_ref[...] = jnp.zeros_like(rows_ref)

    @pl.when(step == 0)
    def _():
        if fresh:
            grad_ref[...] = jnp.zeros_like(grad_ref)
            dsx_ref[:, length : length + 8, :] = jnp.zeros((conv_dim // lanes, 8, lanes), f32)
        else:
            grad_ref[...] = start_ref[...]
            dsx_ref[:, length : length + 8, :] = next_ref[...]

    @pl.when(step > 0)
    def _():
        dsx_ref[:, length : length + 8, :] = dsx_ref[:, 0:8, :]

    lane = lax.broadcasted_iota(jnp.int32, (length, lanes), 1)
    low_lane = lane < lanes // 2
    head_lane = lane < heads
    steps, shifted = step_sizes(dtr_ref[...], head_ref, head_lane)
    cum = cum_ref[...]
    cum_rows = cum.T

    def slope_chunk(at):
        summed = conv_chunk(ext_ref, conv_ref, at, length, taps)
        sig = sigmoid(summed)
        return summed * sig, sig * (1.0 + summed * (1.0 - sig))

    def put_grad(at, d_summed):
        here = slice(at, at + lanes)
        chunk = at // lanes
        dsx_ref[chunk, 0:length, :] = d_summed
        total = None
        for tap in range(taps):
            base = 8 - (taps - 1) + tap
            dconv_ref[tap : tap + 1, here] += jnp.sum(
                d_summed * ext_ref[chunk, base : base + length, :], axis=0, keepdims=True
            )
            back = taps - 1 - tap
            term = conv_ref[tap : tap + 1, here] * dsx_ref[chunk, back : back + length, :]
            total = term if total is None else total + term
        dconv_ref[taps : taps + 1, here] += jnp.sum(d_summed, axis=0, keepdims=True)
        dproj_ref[:, here] = total.astype(bf16)

    parts = [slope_chunk(inner + at) for at in range(0, 2 * state_dim, lanes)]
    count = state_dim // lanes
    keys = jnp.concatenate([part[0] for part in parts[:count]], axis=1).astype(bf16)
    queries = jnp.concatenate([part[0] for part in parts[count:]], axis=1).astype(bf16)
    grad_low = grad_ref[...].astype(bf16)
    dwv_ref[...] = dot(keys, grad_low)
    square = (half, half)
    diag = lax.broadcasted_iota(jnp.int32, square, 0) <= lax.broadcasted_iota(
        jnp.int32, square, 1
    )
    scores_00 = jnp.where(diag, dot(keys[:half], queries[:half], 1, 1), 0.0)
    scores_01 = dot(keys[:half], queries[half:], 1, 1)
    scores_11 = jnp.where(diag, dot(keys[half:], queries[half:], 1, 1), 0.0)
    ds_00 = jnp.zeros(square, f32)
    ds_01 = jnp.zeros(square, f32)
    ds_11 = jnp.zeros(square, f32)
    for pair in range(heads // 2):
        at = pair * lanes
        here = slice(at, at + lanes)
        values, slope = slope_chunk(at)
        cum_rep, cum_0, cum_1 = pair_columns(cum, pair, low_lane)
        dt_rep, _, _ = pair_columns(steps, pair, low_lane)
        stepped = (values * dt_rep).astype(bf16)
        stepped_f = stepped.astype(f32)
        last = cum_rep[length - 1 : length, :]
        tail = jnp.exp2(last - cum_rep)
        d_y = dy_ref[:, here]
        d_yf = d_y.astype(f32)
        d_y_t = d_yf.T.astype(bf16)
        dye_ref[:, here] = (d_yf * jnp.exp2(cum_rep)).astype(bf16)
        top = None
        bottom = None
        for which, cum_col in ((0, cum_0), (1, cum_1)):
            own_lane = low_lane if which == 0 else jnp.logical_not(low_lane)
            own_dy = jnp.where(own_lane, d_yf, 0.0).astype(bf16)
            own_x = jnp.where(own_lane, stepped_f, 0.0).astype(bf16)
            head = 2 * pair + which
            early = cum_rows[head : head + 1, :half]
            late = cum_rows[head : head + 1, half:]
            decay_00 = jnp.exp2(jnp.minimum(early - cum_col[:half], 0.0))
            decay_01 = jnp.exp2(late - cum_col[:half])
            decay_11 = jnp.exp2(jnp.minimum(late - cum_col[half:], 0.0))
            mix_0 = jnp.concatenate(
                [(decay_00 * scores_00).astype(bf16), (decay_01 * scores_01).astype(bf16)], axis=1
            )
            mix_1 = (decay_11 * scores_11).astype(bf16)
            part_top = dot(mix_0, own_dy)
            part_bottom = dot(mix_1, own_dy[half:])
            top = part_top if top is None else top + part_top
            bottom = part_bottom if bottom is None else bottom + part_bottom
            d_mix_0 = dot(own_x[:half], d_y_t)
            d_mix_1 = dot(own_x[half:], d_y_t[:, half:])
            ds_00 = ds_00 + decay_00 * d_mix_0[:, :half]
            ds_01 = ds_01 + decay_01 * d_mix_0[:, half:]
            ds_11 = ds_11 + decay_11 * d_mix_1
        d_diag = jnp.concatenate([top, bottom], axis=0)
        weighted = (stepped_f * tail).astype(bf16)
        weighted_ref[:, here] = weighted
        d_weighted = dwv_ref[:, here]
        through = weighted.astype(f32) * d_weighted
        d_stepped = d_diag + tail * d_weighted
        skip = skip_ref[0:1, here]
        z = d_yf * (y_ref[:, here] - skip * values) - stepped_f * d_diag - through
        z_high, z_low = halves(z)
        zhigh_ref[:, here] = z_high
        zlow_ref[:, here] = z_low
        direct_ref[:, here] = (d_stepped * values).astype(bf16)
        total_decay = jnp.exp2(last)
        rows_ref[0:1, here] = jnp.sum(through, axis=0, keepdims=True) + total_decay * jnp.sum(
            grad_ref[:, here] * sin_ref[:, here].astype(f32), axis=0, keepdims=True
        )
        rows_ref[1:2, here] = jnp.sum(d_yf * values, axis=0, keepdims=True)
        put_grad(at, (d_stepped * dt_rep + skip * d_yf) * slope)
        grad_ref[:, here] = total_decay * grad_ref[:, here]

    grad_ref[...] += dot(queries, dye_ref[...], 0, 0)
    ds_00 = jnp.where(diag, ds_00, 0.0).astype(bf16)
    ds_11 = jnp.where(diag, ds_11, 0.0).astype(bf16)
    ds_01 = ds_01.astype(bf16)
    d_queries = dot(dye_ref[...], sin_ref[...], 1, 1)
    d_keys = dot(weighted_ref[...], grad_low, 1, 1)
    d_queries = d_queries + jnp.concatenate(
        [
            dot(ds_00, keys[:half], 0, 0),
            dot(ds_01, keys[:half], 0, 0) + dot(ds_11, keys[half:], 0, 0),
        ],
        axis=0,
    )
    d_keys = d_keys + jnp.concatenate(
        [
            dot(ds_00, queries[:half]) + dot(ds_01, queries[half:]),
            dot(ds_11, queries[half:]),
        ],
        axis=0,
    )
    for at in range(0, state_dim, lanes):
        put_grad(inner + at, d_keys[:, at : at + lanes] * parts[at // lanes][1])
        put_grad(
            inner + state_dim + at,
            d_queries[:, at : at + lanes] * parts[count + at // lanes][1],
        )
    summing = sum_ref[...]
    rows_high, rows_low = halves(rows_ref[...])
    row_sums = dot(rows_high, summing) + dot(rows_low, summing)
    d_cum = dot(zhigh_ref[...], summing) + dot(zlow_ref[...], summing)
    at_last = lax.broadcasted_iota(jnp.int32, (length, lanes), 0) == length - 1
    d_cum = d_cum + jnp.where(at_last, row_sums[0:1, :], 0.0)
    row = lax.broadcasted_iota(jnp.int32, (length, length), 0)
    col = lax.broadcasted_iota(jnp.int32, (length, length), 1)
    d_log = tri_sum((row <= col).astype(bf16), d_cum, head_lane)
    rate = jnp.exp(head_ref[1:2, :])
    d_steps = dot(direct_ref[...], summing) - rate * d_log
    d_raw = jnp.where(head_lane, d_steps * sigmoid(shifted), 0.0)
    dproj_ref[:, conv_dim : conv_dim + lanes] = d_raw.astype(bf16)
    head_row = slice(taps + 3, taps + 4)
    dconv_ref[head_row, :lanes] += jnp.sum(d_raw, axis=0, keepdims=True)
    dconv_ref[head_row, lanes : 2 * lanes] += jnp.sum(d_log * steps, axis=0, keepdims=True) * (
        -rate
    )
    dconv_ref[head_row, 2 * lanes : 3 * lanes] += row_sums[1:2, :]

    @pl.when(step == pl.num_programs(1) - 1)
    def _():
        end_ref[...] = grad_ref[...]
        lead_ref[...] = dsx_ref[:, 0:8, :]


def input_grad_kernel(
    core_ref,
    x_ref,
    dgate_ref,
    dproj_ref,
    small_ref,
    dsmall_in_ref,
    wg_own,
    wg_other,
    wa_own,
    wa_other,
    wb_own,
    wb_other,
    dx_ref,
    dsmall_ref,
    wg_ref,
    wa_ref,
    wb_ref,
    wg_sems,
    wa_sems,
    wb_sems,
    *,
    gain_row,
):
    first = jnp.logical_and(pl.program_id(0) == 0, pl.program_id(1) == 0)
    width = x_ref.shape[1]

    @pl.when(first)
    def _():
        copies = fetch_weight(core_ref, wg_own, wg_other, wg_ref, wg_sems)
        copies += fetch_weight(core_ref, wa_own, wa_other, wa_ref, wa_sems)
        copies += fetch_weight(core_ref, wb_own, wb_other, wb_ref, wb_sems)
        dsmall_ref[...] = dsmall_in_ref[...]
        for copy in copies:
            copy.wait()

    wide_a = wa_ref.shape[1]
    d_normed = (
        dot(dgate_ref[...], wg_ref[...], 1, 1)
        + dot(dproj_ref[:, :wide_a], wa_ref[...], 1, 1)
        + dot(dproj_ref[:, wide_a:], wb_ref[...], 1, 1)
    )
    rows = x_ref[...].astype(f32)
    scale = lax.rsqrt(jnp.mean(rows * rows, axis=-1, keepdims=True) + norm_eps)
    scaled = rows * scale
    dsmall_ref[gain_row : gain_row + 1, :width] += jnp.sum(
        scaled * d_normed, axis=0, keepdims=True
    )
    gain = small_ref[gain_row : gain_row + 1, :width]
    inner_grad = gain * d_normed
    cross = jnp.mean(scaled * inner_grad, axis=-1, keepdims=True)
    dx_ref[...] = (scale * (inner_grad - scaled * cross)).astype(bf16)


def front_grad_kernel(
    core_ref, normed_ref, dproj_ref, a_send, a_keep, b_send, b_keep, a_sum, b_sum
):
    turned = normed_ref[...].T
    at = 0
    for total, send, keep in ((a_sum, a_send, a_keep), (b_sum, b_send, b_keep)):
        for column in range(0, total.shape[1], lanes):
            here = slice(column, column + lanes)
            if column % (2 * lanes) == 0 and column + 2 * lanes <= total.shape[1]:
                here = slice(column, column + 2 * lanes)
            elif column % (2 * lanes) != 0:
                continue
            total[:, here] = dot(turned, dproj_ref[:, at + here.start : at + here.stop])
        at += total.shape[1]
        hand_out(core_ref[0], total, send, keep)


def adam_kernel(
    rates_ref,
    *refs,
    heads,
    taps,
    at_refs,
    arrivals,
):
    sum_refs, refs = refs[:arrivals], refs[arrivals:]
    rest_refs, front_refs, refs = refs[:arrivals], refs[arrivals : 2 * arrivals], refs[2 * arrivals :]
    ins, outs = refs[:18], refs[18:]
    learn_rate, decay_rate = rates_ref[0], rates_ref[3]
    beta_one, beta_two = rates_ref[1], rates_ref[2]
    first_scale, second_scale = rates_ref[4], rates_ref[5]

    def update(which, grad, index):
        master, first, second = (ref[index] for ref in ins[3 * which : 3 * which + 3])
        new_first = beta_one * first + (1.0 - beta_one) * grad
        new_second = beta_two * second + (1.0 - beta_two) * grad * grad
        change = -learn_rate * (
            (new_first * first_scale) / (jnp.sqrt(new_second * second_scale) + adam_eps)
            + decay_rate * master
        )
        where = at_refs[which]
        outs[where][index] = master + change if which in (1, 4) else change
        outs[where + 1][index] = new_first
        outs[where + 2][index] = new_second
        if which in (1, 4):
            outs[-2 if which == 1 else -1][index] = (master + change).astype(bf16)

    everything = (slice(None), slice(None))
    rest, front = rest_refs[0][...], front_refs[0][...]
    inner = rest.shape[1] // 2
    for rest_ref, front_ref in zip(rest_refs[1:], front_refs[1:]):
        rest = rest + rest_ref[...].astype(f32)
        front = front + front_ref[...].astype(f32)
    proj = ins[3].shape[1]
    update(1, rest[:, :inner], (slice(None), slice(0, inner)))
    update(1, front[:, : proj - inner], (slice(None), slice(inner, proj)))
    rows = rest.shape[0]
    half = inner // 2
    update(4, rest[:, inner : inner + half], (slice(0, rows), slice(None)))
    update(4, rest[:, inner + half :], (slice(rows, 2 * rows), slice(None)))

    place = rates_ref[7].astype(jnp.int32)
    terms = [ref[...] for ref in sum_refs]
    sums = terms[0]
    for term in terms[1:]:
        sums = sums + term

    def own(at, count):
        wide = sums.shape[1]
        shift = lax.rem(wide - place * count, wide)
        return pltpu.roll(sums, shift, 1)[at, :count]

    update(0, own(slice(taps + 1, taps + 2), ins[0].shape[1]), everything)
    update(2, own(slice(0, taps + 1), ins[6].shape[1]), everything)
    update(3, own(slice(taps + 2, taps + 3), ins[9].shape[1]), everything)
    sums = jnp.zeros_like(sums)
    for source in range(arrivals):
        distance = lax.rem(place + arrivals - source, arrivals)
        term = terms[0]
        for which in range(1, arrivals):
            term = jnp.where(distance == which, terms[which], term)
        sums = sums + term
    head_row = slice(taps + 3, taps + 4)
    for row in range(3):
        grad = sums[head_row, row * lanes : row * lanes + heads]
        update(5, grad, (slice(row, row + 1), slice(None)))


def whole(shape):
    return pl.BlockSpec(shape, lambda p, b: (0,) * len(shape))


def by_block(shape, size, back=False):
    if back:
        return pl.BlockSpec(shape, lambda p, s: (p * size + (size - 1 - s), 0))
    return pl.BlockSpec(shape, lambda p, b: (p * size + b, 0))


def by_part(shape):
    return pl.BlockSpec(shape, lambda p, b: (p, 0))


def params():
    return pltpu.CompilerParams(
        dimension_semantics=("arbitrary", "arbitrary"), vmem_limit_bytes=vmem_bytes
    )


def cost(flops, moved, powers):
    return pl.CostEstimate(flops=flops, bytes_accessed=moved, transcendentals=powers)


ANY = pl.BlockSpec(memory_space=pl.ANY)
SMEM = pl.BlockSpec(memory_space=pltpu.SMEM)


def weight_scratch(*weights):
    wholes = [
        pltpu.VMEM((2 * own.shape[0] * own.shape[1], own.shape[2]), bf16) for own, _ in weights
    ]
    return wholes + [pltpu.SemaphoreType.DMA((2 * own.shape[0],)) for own, _ in weights]


def handed_out(rows, columns, blocks):
    shape = (blocks, rows // (2 * blocks), columns)
    return [jax.ShapeDtypeStruct(shape, bf16), jax.ShapeDtypeStruct(shape, f32)]


def mixer_forward(dims, core, tokens, wa, wb, small, head, skip, edge, start, grouped, kept, blocks):
    part, size, piece, width, inner, heads, taps = dims
    first, count = blocks
    conv_dim = small.shape[1]
    state_dim = (conv_dim - inner) // 2
    all_blocks = part * size
    rows = all_blocks * piece
    ext_rows = piece + 8
    chunks = conv_dim // lanes
    resumed = kept is not None

    def by_block(shape):
        return pl.BlockSpec(shape, lambda p, b: (p * size + first + b, 0))

    tail_block = pl.BlockSpec((chunks, 8, lanes), lambda p, b: (p, 0, 0))
    before = core
    if resumed:
        *arrays, start, before = kept
    else:
        arrays = []
    return pl.pallas_call(
        partial(
            mixer_forward_kernel,
            heads=heads,
            inner=inner,
            taps=taps,
            grouped=grouped,
            resumed=resumed,
        ),
        grid=(part, count),
        in_specs=[
            SMEM,
            by_block((piece, width)),
            by_part((8, width)) if grouped else ANY,
            ANY,
            ANY,
            ANY,
            ANY,
            whole(small.shape),
            whole(head.shape),
            whole(skip.shape),
            by_part((state_dim, inner)) if grouped or resumed else ANY,
            tail_block if resumed else ANY,
        ]
        + [ANY] * len(arrays),
        out_specs=[
            by_block((piece, width)),
            pl.BlockSpec((chunks, ext_rows, lanes), lambda p, b: (p * size + first + b, 0, 0)),
            by_block((piece, lanes)),
            by_block((piece, lanes)),
            by_block((piece, inner)),
            by_block((state_dim, inner)),
            by_part((state_dim, inner)),
            tail_block,
        ],
        out_shape=[
            jax.ShapeDtypeStruct((rows, width), bf16),
            jax.ShapeDtypeStruct((all_blocks * chunks, ext_rows, lanes), f32),
            jax.ShapeDtypeStruct((rows, lanes), f32),
            jax.ShapeDtypeStruct((rows, lanes), f32),
            jax.ShapeDtypeStruct((rows, inner), f32),
            jax.ShapeDtypeStruct((all_blocks * state_dim, inner), bf16),
            jax.ShapeDtypeStruct((part * state_dim, inner), f32),
            jax.ShapeDtypeStruct((part * chunks, 8, lanes), f32),
        ],
        scratch_shapes=[
            pltpu.VMEM((chunks, 8, lanes), f32),
            pltpu.VMEM((state_dim, inner), f32),
            pltpu.VMEM((piece, inner), f32),
            pltpu.VMEM((piece, inner), bf16),
        ]
        + weight_scratch(wa, wb),
        input_output_aliases={12 + at: at for at in range(len(arrays))},
        compiler_params=params(),
        cost_estimate=cost(1, 1, 0),
    )(core, tokens, edge, *wa, *wb, small, head, skip, start, before, *arrays)


def gate_step(dims, core, normed, tokens, cots_b, y, wg, wo, small):
    part, size, piece, width, inner, heads, taps = dims
    rows = part * size * piece
    blocks = wo[0].shape[0]
    handed = handed_out(inner, width, blocks) + handed_out(width, inner, blocks)
    wide_b = cots_b.shape[1]
    at_a = width // (width - wide_b)
    return pl.pallas_call(
        partial(gate_kernel, gain_row=taps + 2),
        grid=(part, size),
        in_specs=[
            SMEM,
            by_block((piece, width), size),
            by_block((piece, width), size),
            pl.BlockSpec((piece, width - wide_b), lambda p, b: (p * size + b, at_a)),
            by_block((piece, wide_b), size),
            by_block((piece, inner), size),
            ANY,
            ANY,
            ANY,
            ANY,
            whole(small.shape),
        ],
        out_specs=[
            by_block((piece, width), size),
            by_block((piece, inner), size),
            by_block((piece, inner), size),
            whole((8, inner)),
        ]
        + [whole(array.shape) for array in handed],
        out_shape=[
            jax.ShapeDtypeStruct((rows, width), bf16),
            jax.ShapeDtypeStruct((rows, inner), bf16),
            jax.ShapeDtypeStruct((rows, inner), bf16),
            jax.ShapeDtypeStruct((8, inner), f32),
        ]
        + handed,
        scratch_shapes=[
            pltpu.VMEM((piece, inner), f32),
            pltpu.VMEM((piece, inner), f32),
            pltpu.VMEM((piece, inner), bf16),
            pltpu.VMEM((piece, width), bf16),
            pltpu.VMEM((inner, width), f32),
            pltpu.VMEM((width, inner), f32),
        ]
        + weight_scratch(wg, wo),
        compiler_params=params(),
        cost_estimate=cost(1, 1, 0),
    )(core, normed, tokens, tokens, cots_b, y, *wg, *wo, small)


def mixer_backward(dims, saved, consts, carry, blocks, fresh):
    part, size, piece, width, inner, heads, taps = dims
    first, count = blocks
    small, head, skip, summing, dgain = consts
    conv_dim = small.shape[1]
    state_dim = (conv_dim - inner) // 2
    ext_rows = piece + 8
    chunks = conv_dim // lanes
    wide = conv_dim + lanes
    dproj, dsmall, state, lead = carry
    lead_block = pl.BlockSpec((chunks, 8, lanes), lambda p, s: (p, 0, 0))

    def by_block(shape):
        return pl.BlockSpec(shape, lambda p, s: (p * size + (first + count - 1 - s), 0))

    return pl.pallas_call(
        partial(mixer_backward_kernel, heads=heads, inner=inner, taps=taps, fresh=fresh),
        grid=(part, count),
        in_specs=[
            pl.BlockSpec(
                (chunks, ext_rows, lanes), lambda p, s: (p * size + (first + count - 1 - s), 0, 0)
            ),
            by_block((piece, lanes)),
            by_block((piece, lanes)),
            by_block((piece, inner)),
            by_block((state_dim, inner)),
            by_block((piece, inner)),
            whole(small.shape),
            whole(head.shape),
            whole(skip.shape),
            whole(summing.shape),
            ANY if fresh else by_part((state_dim, inner)),
            ANY if fresh else lead_block,
            whole(dsmall.shape),
            whole(dgain.shape),
            ANY,
        ],
        out_specs=[
            by_block((piece, wide)),
            whole((8, conv_dim)),
            by_part((state_dim, inner)),
            lead_block,
        ],
        out_shape=[
            jax.ShapeDtypeStruct((part * size * piece, wide), bf16),
            jax.ShapeDtypeStruct((8, conv_dim), f32),
            jax.ShapeDtypeStruct((part * state_dim, inner), f32),
            jax.ShapeDtypeStruct((part * chunks, 8, lanes), f32),
        ],
        scratch_shapes=[
            pltpu.VMEM((state_dim, inner), f32),
            pltpu.VMEM((chunks, ext_rows, lanes), f32),
            pltpu.VMEM((piece, inner), f32),
            pltpu.VMEM((piece, inner), bf16),
            pltpu.VMEM((piece, inner), bf16),
            pltpu.VMEM((piece, inner), bf16),
            pltpu.VMEM((piece, inner), bf16),
            pltpu.VMEM((piece, inner), bf16),
            pltpu.VMEM((8, inner), f32),
        ],
        input_output_aliases={14: 0} if dproj.shape[0] == part * size * piece else {},
        compiler_params=params(),
        cost_estimate=cost(1, 1, 0),
    )(*saved, small, head, skip, summing, state, lead, dsmall, dgain, dproj)


def input_grad(dims, core, tokens, dgate, dproj, small, dsmall, wg, wa, wb):
    part, size, piece, width, inner, heads, taps = dims
    rows = part * size * piece
    return pl.pallas_call(
        partial(input_grad_kernel, gain_row=taps + 1),
        grid=(part, size),
        in_specs=[
            SMEM,
            by_block((piece, width), size),
            by_block((piece, inner), size),
            by_block((piece, dproj.shape[1]), size),
            whole(small.shape),
            whole(dsmall.shape),
            ANY,
            ANY,
            ANY,
            ANY,
            ANY,
            ANY,
        ],
        out_specs=[by_block((piece, width), size), whole(dsmall.shape)],
        out_shape=[
            jax.ShapeDtypeStruct((rows, width), bf16),
            jax.ShapeDtypeStruct(dsmall.shape, f32),
        ],
        scratch_shapes=weight_scratch(wg, wa, wb),
        compiler_params=params(),
        cost_estimate=cost(1, 1, 0),
    )(core, tokens, dgate, dproj, small, dsmall, *wg, *wa, *wb)


def front_grad(core, normed, dproj, wide_a, blocks):
    width = normed.shape[1]
    wide_b = dproj.shape[1] - wide_a
    handed = handed_out(width, wide_a, blocks) + handed_out(width, wide_b, blocks)
    vmem = pl.BlockSpec(memory_space=pltpu.VMEM)
    return pl.pallas_call(
        front_grad_kernel,
        in_specs=[SMEM, vmem, vmem],
        out_specs=[vmem] * 4,
        out_shape=handed,
        scratch_shapes=[pltpu.VMEM((width, wide_a), f32), pltpu.VMEM((width, wide_b), f32)],
        compiler_params=pltpu.CompilerParams(vmem_limit_bytes=vmem_bytes),
        cost_estimate=cost(6_000_000_000, 20_000_000, 0),
    )(core, normed, dproj)


def adam(rates, sums, gate_grads, front_grads, states, heads, taps):
    outs = []
    at_refs = []
    for which, (master, first, second) in enumerate(states):
        at_refs.append(len(outs))
        outs += [jax.ShapeDtypeStruct(master.shape, f32)] * 3
    outs.append(jax.ShapeDtypeStruct(states[1][0].shape, bf16))
    outs.append(jax.ShapeDtypeStruct(states[4][0].shape, bf16))
    flat = [array for state in states for array in state]
    vmem = pl.BlockSpec(memory_space=pltpu.VMEM)
    return pl.pallas_call(
        partial(
            adam_kernel, heads=heads, taps=taps, at_refs=at_refs, arrivals=len(gate_grads)
        ),
        in_specs=[SMEM] + [vmem] * (3 * len(gate_grads) + len(flat)),
        out_specs=[vmem] * len(outs),
        out_shape=outs,
        compiler_params=pltpu.CompilerParams(vmem_limit_bytes=vmem_bytes),
        cost_estimate=cost(1, 1, 0),
    )(rates, *sums, *gate_grads, *front_grads, *flat)


def bit_count(extent):
    count = extent.bit_length() - 1
    if 1 << count != extent:
        raise ValueError(extent)
    return count


def swap(block, axis, bit):
    devices = range(lax.axis_size(axis))
    return lax.ppermute(block, axis, [(i, i ^ (1 << bit)) for i in devices])


def shifted_by(block, axis, distance):
    devices = range(lax.axis_size(axis))
    route = [(i, i + distance) for i in devices if i + distance in devices]
    return lax.ppermute(block, axis, route)


def pick(block, at, axis):
    return lax.dynamic_index_in_dim(block, at, axis, keepdims=False)


def gather_bit(block, axis, bit, at, *others):
    mine = (lax.axis_index(axis) >> bit) & 1
    other = swap(block, axis, bit)
    if others:
        other = after(other, *others)
    low = jnp.where(mine == 1, other, block)
    high = jnp.where(mine == 1, block, other)
    return jnp.stack([low, high], axis=at)


def gather_seq(shard, *others):
    block = shard
    for done, bit in enumerate(reversed(range(bit_count(lax.axis_size("seq"))))):
        block = gather_bit(block, "seq", bit, done, *(others if done == 0 else ()))
    return block.reshape((-1,) + shard.shape)


def dp_orders():
    bits = bit_count(lax.axis_size("dp"))
    return list(range(bits - 1, 0, -1)) + [0], list(range(1, bits)) + [0]


def gather_dp_bit(block, order, step, *others):
    at = sum(1 for b in order[:step] if b > order[step])
    return gather_bit(block, "dp", order[step], at, *others)


def give_half(block, axis, bit, at):
    mine = (lax.axis_index(axis) >> bit) & 1
    other = swap(pick(block, 1 - mine, at).astype(bf16), axis, bit)
    return pick(block, mine, at) + other.astype(f32)


def core_sums(send, keep):
    extent = lax.axis_size("seq")
    bits = bit_count(lax.axis_size("dp")) - 1
    shape = (2,) * bits + (extent, -1, send.shape[2])
    other = swap(send, "dp", 0)
    return keep.reshape(shape), other.reshape(shape)


def core_and_next(keep, other, order):
    bit = order[-2]
    at = sum(1 for b in order[:-2] if b > bit)
    mine = (lax.axis_index("dp") >> bit) & 1
    sent = pick(keep, 1 - mine, at) + pick(other, 1 - mine, at).astype(f32)
    arrived = swap(sent.astype(bf16), "dp", bit)
    return pick(keep, mine, at) + pick(other, mine, at).astype(f32), arrived


def scatter_dp_bit(block, order, step):
    bit = order[-1 - step]
    return give_half(block, "dp", bit, sum(1 for b in order[: len(order) - 1 - step] if b > bit))


def scatter_seq(block):
    extent = lax.axis_size("seq")
    place = lax.axis_index("seq")
    arrivals = [pick(block, place, 0)]
    for distance in range(1, extent):
        sent = pick(block, lax.rem(place + distance, extent), 0).astype(bf16)
        route = [(i, (i + distance) % extent) for i in range(extent)]
        arrivals.append(lax.ppermute(sent, "seq", route))
    return arrivals


def sum_bits(block, axis, bits):
    for bit in bits:
        block = block + swap(block, axis, bit)
    return block


def seq_groups(size):
    extent = lax.axis_size("seq")
    if size == extent:
        return None
    return [list(range(at, at + size)) for at in range(0, extent, size)]


def to_sequences(block, part, size):
    if size > 1:
        block = lax.all_to_all(
            block, "seq", 0, 0, axis_index_groups=seq_groups(size), tiled=True
        )
    piece, width = block.shape[1:]
    block = block.reshape(size, part, piece, width)
    if part > 1:
        block = block.transpose(1, 0, 2, 3)
    return block.reshape(-1, width)


def to_pieces(rows, part, size, piece):
    block = rows.reshape(part, size, piece, -1)
    if part > 1:
        block = block.transpose(1, 0, 2, 3)
    block = block.reshape(part * size, piece, -1)
    if size > 1:
        block = lax.all_to_all(
            block, "seq", 0, 0, axis_index_groups=seq_groups(size), tiled=True
        )
    return block


def after(value, *others):
    return lax.optimization_barrier((value,) + others)[0]


def padded(block, rows, columns):
    return jnp.pad(block, ((0, rows - block.shape[0]), (0, columns - block.shape[1])))


def summing_matrix(inner, heads):
    columns = np.zeros((inner, lanes), np.float32)
    columns[np.arange(inner), np.arange(inner) // (inner // heads)] = 1.0
    return jnp.asarray(columns, bf16)


def local(
    layer_in,
    out_grad,
    norm_gain,
    in_weight,
    conv_params,
    gate_gain,
    out_weight,
    head_params,
    norm_first,
    norm_second,
    in_first,
    in_second,
    conv_first,
    conv_second,
    gate_first,
    gate_second,
    out_first,
    out_second,
    head_first,
    head_second,
    step_count,
    hyper,
):
    seq_count, piece, width = layer_in.shape
    seq_extent = lax.axis_size("seq")
    me = lax.axis_index("dp") * seq_extent + lax.axis_index("seq")
    step_float = step_count[0].astype(f32)
    scales = 1.0 / (1.0 - hyper[1:3] ** step_float)
    place = lax.axis_index("seq")
    rates = jnp.concatenate([hyper, scales, jnp.stack([me.astype(f32), place.astype(f32)])])
    core = (lax.axis_index("dp") & 1).astype(jnp.int32)[None]
    owners = lax.axis_size("dp") * seq_extent
    size = math.gcd(seq_extent, seq_count)
    part = seq_count // size
    groups = seq_extent // size
    inner = out_weight.shape[0] * owners
    heads = head_params.shape[1]
    tap_rows, conv_own = conv_params.shape
    taps = tap_rows - 1
    conv_dim = conv_own * owners
    state_dim = (conv_dim - inner) // 2
    own_rows = in_weight.shape[0]
    gate_own = gate_gain.shape[0]
    wide_a = min(1024, inner)
    dims = (part, size, piece, width, inner, heads, taps)

    head = padded(head_params, 8, lanes)
    skip = jnp.repeat(head_params[2], inner // heads)[None, :]
    summing = summing_matrix(inner, heads)

    in_low = padded(in_weight.astype(bf16), own_rows, inner + conv_dim + lanes)
    out_low_own = out_weight.astype(bf16).reshape(2, own_rows, width)
    own_small = jnp.concatenate(
        [
            padded(conv_params.astype(bf16), tap_rows, lanes),
            padded(norm_gain.astype(bf16)[None, :], 1, lanes),
            padded(gate_gain.astype(bf16)[None, :], 1, lanes),
        ]
    )
    shard = jnp.concatenate([in_low, out_low_own[0], out_low_own[1]], axis=1)
    half = width // 6
    both = jnp.concatenate([layer_in, out_grad[:, :, :half]], axis=2)
    second = lax.optimization_barrier(out_grad[:, :, half:])
    if own_rows >= tap_rows + 2:
        shard = jnp.concatenate([shard, padded(own_small, own_rows, lanes)], axis=1)
        gathered = gather_seq(shard, both, second, head, skip)
        seq_small = gathered[:, : tap_rows + 2, -lanes:]
    else:
        gathered = gather_seq(shard)
        seq_small = gather_seq(padded(own_small, 8, lanes))[:, : tap_rows + 2]
    tokens = to_sequences(after(both, shard), part, size)
    small = jnp.zeros((8, conv_dim), bf16)
    group = lax.axis_index("dp")
    for at, rows, count in (
        (0, tap_rows, conv_own),
        (tap_rows, 1, own_rows),
        (tap_rows + 1, 1, gate_own),
    ):
        piece_rows = jnp.concatenate(
            [seq_small[z, at : at + rows, :count] for z in range(seq_extent)], axis=1
        )
        small = lax.dynamic_update_slice(small, piece_rows, (at, group * seq_extent * count))
    front_end = inner + conv_dim + lanes
    wg = gathered[:, :, :inner]
    wa = gathered[:, :, inner : inner + wide_a]
    wb = gathered[:, :, inner + wide_a : front_end]
    wo = jnp.stack(
        [
            gathered[:, :, front_end : front_end + width],
            gathered[:, :, front_end + width : front_end + 2 * width],
        ],
        axis=1,
    ).reshape(-1, 2 * own_rows, width)
    order_a, order_b = dp_orders()
    last = len(order_a) - 1
    for step in range(last):
        wa = gather_dp_bit(wa, order_a, step)
        wb = gather_dp_bit(wb, order_b, step)
    small = sum_bits(small, "dp", order_a[:-1])
    for step in range(last):
        if step == 1:
            wg, wo = after((wg, wo), wa, wb, small)
        if step < last - 1:
            wg = gather_dp_bit(wg, order_a, step)
            wo = gather_dp_bit(wo, order_b, step)

    def core_halves(block):
        block = block.reshape(owners // 2 // seq_extent, -1, block.shape[-1])
        return block, swap(block, "dp", 0)

    wb = core_halves(wb)
    wa = core_halves(wa)
    small = sum_bits(after(small, tokens, wa, wb, head, skip), "dp", [0]).astype(f32)
    cots_b = to_sequences(after(second, tokens), part, size)

    edge = core
    if groups > 1:
        edge = tokens.reshape(part, size * piece, -1)[:, size * piece - 8 :, :width]
        edge = shifted_by(edge, "seq", size).reshape(part * 8, width)

    def forward(start, kept, blocks):
        weights = (wa, wb, small, head, skip)
        grouped = groups > 1
        return mixer_forward(dims, core, tokens, *weights, edge, start, grouped, kept, blocks)

    start = core
    if groups > 1:
        first_out = forward(jnp.zeros((part * state_dim, inner), f32), None, (0, size))
        cum_last = first_out[3].reshape(part, size, piece, lanes)[:, :, piece - 1, :heads]
        decay = jnp.exp2(jnp.sum(cum_last, axis=1))
        decay = jnp.repeat(decay, inner // heads, axis=1)[:, None, :]

        def relay(ends, distance):
            ends = ends.reshape(part, state_dim, inner)
            carried = jnp.zeros_like(ends)
            for _ in range(groups - 1):
                sent = (decay * carried + ends).astype(bf16)
                carried = shifted_by(sent, "seq", distance).astype(f32)
            return carried.reshape(part * state_dim, inner)

        start = relay(first_out[6], size)
    normed, ext, dtr, cum, y, sin, _, _ = forward(start, None, (0, size))
    wg = core_halves(gather_dp_bit(wg, order_a, last - 1, normed))
    wo = core_halves(gather_dp_bit(wo, order_b, last - 1, normed))
    layer_rows, dy, dgate, dgain, *handed = gate_step(
        dims, core, normed, tokens, cots_b, y, wg, wo, small
    )
    layer_out = to_pieces(layer_rows, part, size, piece)
    consts = (small, head, skip, summing, dgain)
    saved = (ext, dtr, cum, y, sin, dy)

    def backward(carry, block, fresh=False):
        return list(mixer_backward(dims, saved, consts, carry, (block, 1), fresh))

    def fresh_carry():
        if groups == 1:
            return (core, head, core, core)
        lead = jnp.zeros((part * (conv_dim // lanes), 8, lanes), f32)
        first_out = (core, head, jnp.zeros((part * state_dim, inner), f32), lead)
        for block in reversed(range(size)):
            first_out = backward(first_out, block)
        return (core, head, relay(first_out[2], -size), lead)

    g_out = core_sums(*handed[:2])
    g_gate = core_sums(*handed[2:])
    carry = backward(fresh_carry(), size - 1, groups == 1)
    for block in reversed(range(size - 1)):
        carry[2], g_out, g_gate = lax.optimization_barrier((carry[2], g_out, g_gate))
        step = size - 2 - block
        if step == 0:
            g_out = core_and_next(*g_out, order_a)
            g_gate = core_and_next(*g_gate, order_b)
        elif step == 1:
            g_out = g_out[0] + g_out[1].astype(f32)
            g_gate = g_gate[0] + g_gate[1].astype(f32)
            for bit_step in range(2, last + 1):
                g_out = scatter_dp_bit(g_out, order_a, bit_step)
                g_gate = scatter_dp_bit(g_gate, order_b, bit_step)
        elif step == 2:
            g_rest = scatter_seq(
                jnp.concatenate([g_gate, g_out[:, :own_rows], g_out[:, own_rows:]], axis=2)
            )
        carry = backward(carry, block)
    dproj, dsmall, _, lead = carry
    if groups > 1:
        lead = shifted_by(lead.astype(bf16), "seq", -size).astype(f32)
        lead = lead.reshape(part, -1, 8, lanes).transpose(0, 2, 1, 3).reshape(part, 8, conv_dim)
        fixes = []
        for row in range(taps - 1):
            terms = [small[tap] * lead[:, row - tap] for tap in range(row + 1)]
            fixes.append(sum(terms[1:], terms[0]))
        fix = jnp.pad(jnp.stack(fixes, axis=1), ((0, 0), (0, 0), (0, lanes)))
        dproj = dproj.reshape(part, size * piece, conv_dim + lanes)
        ends = dproj[:, size * piece - (taps - 1) :].astype(f32) + fix
        dproj = dproj.at[:, size * piece - (taps - 1) :].set(ends.astype(bf16))
        dproj = dproj.reshape(-1, conv_dim + lanes)
    tokens, g_rest = lax.optimization_barrier((after(tokens, layer_out, dproj), g_rest))
    dx, dsmall = input_grad(dims, core, tokens, dgate, dproj, small, dsmall, wg, wa, wb)
    dsmall = sum_bits(dsmall, "dp", [0])
    handed = front_grad(core, after(normed, dsmall), dproj, wide_a, owners // 2 // seq_extent)
    g_a = core_sums(*handed[:2])
    g_b = core_sums(*handed[2:])
    g_a = core_and_next(*g_a, order_a)
    g_b = core_and_next(*g_b, order_b)
    g_a = g_a[0] + g_a[1].astype(f32)
    g_b = g_b[0] + g_b[1].astype(f32)
    for step in range(2, last + 1):
        g_a = scatter_dp_bit(g_a, order_a, step)
        g_b = scatter_dp_bit(g_b, order_b, step)
    pieces = to_pieces(dx, part, size, piece)
    in_grad = out_grad.astype(f32) + pieces.astype(f32)
    g_front = scatter_seq(after(jnp.concatenate([g_a, g_b], axis=2), pieces))
    dsmall = sum_bits(dsmall, "dp", order_a[-2::-1])
    slab_wide = -(-max(3 * lanes, seq_extent * max(conv_own, own_rows, gate_own)) // lanes) * lanes
    slab = [
        padded(
            lax.dynamic_slice(
                dsmall, (at, group * seq_extent * count), (rows, seq_extent * count)
            ),
            rows,
            slab_wide,
        )
        for at, rows, count in (
            (0, tap_rows, conv_own),
            (tap_rows, 1, own_rows),
            (tap_rows + 1, 1, gate_own),
        )
    ]
    dsmall = jnp.concatenate(slab + [dsmall[tap_rows + 2 :, :slab_wide]])
    sums = [dsmall]
    for distance in range(1, seq_extent):
        route = [(i, (i + distance) % seq_extent) for i in range(seq_extent)]
        sums.append(lax.ppermute(dsmall, "seq", route))

    states = (
        (norm_gain[None, :], norm_first[None, :], norm_second[None, :]),
        (in_weight, in_first, in_second),
        (conv_params, conv_first, conv_second),
        (gate_gain[None, :], gate_first[None, :], gate_second[None, :]),
        (out_weight, out_first, out_second),
        (head_params, head_first, head_second),
    )
    new = adam(rates, sums, g_rest, g_front, states, heads, taps)
    new = [array[0] if array.shape[0] == 1 else array for array in new]
    return (layer_out, in_grad, *new)


def solution(mesh):
    in_specs = (
        P("dp", "seq", None),
        P("dp", "seq", None),
        P(("dp", "seq")),
        P(("dp", "seq"), None),
        P(None, ("dp", "seq")),
        P(("dp", "seq")),
        P(("dp", "seq"), None),
        P(),
        P(("dp", "seq")),
        P(("dp", "seq")),
        P(("dp", "seq"), None),
        P(("dp", "seq"), None),
        P(None, ("dp", "seq")),
        P(None, ("dp", "seq")),
        P(("dp", "seq")),
        P(("dp", "seq")),
        P(("dp", "seq"), None),
        P(("dp", "seq"), None),
        P(),
        P(),
        P(),
        P(),
    )
    out_specs = (
        P("dp", "seq", None),
        P("dp", "seq", None),
        P(("dp", "seq")),
        P(("dp", "seq")),
        P(("dp", "seq")),
        P(("dp", "seq"), None),
        P(("dp", "seq"), None),
        P(("dp", "seq"), None),
        P(None, ("dp", "seq")),
        P(None, ("dp", "seq")),
        P(None, ("dp", "seq")),
        P(("dp", "seq")),
        P(("dp", "seq")),
        P(("dp", "seq")),
        P(("dp", "seq"), None),
        P(("dp", "seq"), None),
        P(("dp", "seq"), None),
        P(),
        P(),
        P(),
        P(("dp", "seq"), None),
        P(("dp", "seq"), None),
    )
    return jax.shard_map(local, mesh=mesh, in_specs=in_specs, out_specs=out_specs, check_vma=False)
```

```python
import math
from functools import partial

import jax
import jax.numpy as jnp
import numpy as np
from jax import lax
from jax.experimental import pallas as pl
from jax.experimental.pallas import tpu as pltpu
from jax.sharding import PartitionSpec as P

norm_eps = 1e-05
adam_eps = 1e-08
log2e = math.log2(math.e)
lanes = 128
vmem_bytes = 56 * 1024 * 1024
f32 = jnp.float32
bf16 = jnp.bfloat16


def dot(left, right, left_dim=1, right_dim=0):
    return lax.dot_general(
        left, right, (((left_dim,), (right_dim,)), ((), ())), preferred_element_type=f32
    )


def halves(value):
    high = value.astype(bf16)
    return high, (value - high.astype(f32)).astype(bf16)


def sigmoid(value):
    return 0.5 * jnp.tanh(0.5 * value) + 0.5


def column(ref_value, at, width):
    return jnp.broadcast_to(ref_value[:, at : at + 1], (ref_value.shape[0], width))


def pair_columns(value, pair, low_lane):
    rows = value.shape[0]
    first = column(value, 2 * pair, lanes)
    second = column(value, 2 * pair + 1, lanes)
    return jnp.where(low_lane, first, second), first, second


def tri_sum(mask, value, head_lane):
    high = value.astype(bf16).astype(f32)
    rest = value - high
    mid = rest.astype(bf16).astype(f32)
    low = rest - mid
    packed = high + pltpu.roll(mid, 32, 1) + pltpu.roll(low, 64, 1)
    summed = dot(mask, packed.astype(bf16))
    total = summed + pltpu.roll(summed, lanes - 32, 1) + pltpu.roll(summed, lanes - 64, 1)
    return jnp.where(head_lane, total, 0.0)


def conv_chunk(ext_ref, conv_ref, at, length, taps):
    summed = conv_ref[taps : taps + 1, at : at + lanes]
    base = 8 - (taps - 1)
    for tap in range(taps):
        summed = (
            summed
            + conv_ref[tap : tap + 1, at : at + lanes]
            * ext_ref[at // lanes, base + tap : base + tap + length, :]
        )
    return summed


def put_columns(ext_ref, rows, values, chunk):
    for at in range(0, values.shape[1], lanes):
        ext_ref[chunk + at // lanes, rows, :] = values[:, at : at + lanes]


def step_sizes(dt_raw, head_ref, head_lane):
    shifted = dt_raw + head_ref[0:1, :]
    steps = jnp.maximum(shifted, 0.0) + jnp.log1p(jnp.exp(-jnp.abs(shifted)))
    return jnp.where(head_lane, steps, 0.0), shifted


def fetch_weight(core_ref, own_ref, other_ref, whole_ref, sems):
    blocks, rows, _ = own_ref.shape
    core = core_ref[0]
    copies = []
    for block in range(blocks):
        for which, source in ((core, own_ref), (1 - core, other_ref)):
            at = pl.multiple_of((2 * block + which) * rows, rows)
            copies.append(
                pltpu.make_async_copy(
                    source.at[block], whole_ref.at[pl.ds(at, rows)], sems.at[len(copies)]
                )
            )
    for copy in copies:
        copy.start()
    return copies


def hand_out(core, total_ref, send_ref, keep_ref):
    blocks, rows, _ = send_ref.shape
    for block in range(blocks):
        at = pl.multiple_of((2 * block + 1 - core) * rows, rows)
        send_ref[block] = total_ref[pl.ds(at, rows), :].astype(bf16)
        at = pl.multiple_of((2 * block + core) * rows, rows)
        keep_ref[block] = total_ref[pl.ds(at, rows), :]


def add_product(total_ref, left_ref, right):
    for at in range(0, total_ref.shape[0], 2 * lanes):
        here = slice(at, at + 2 * lanes)
        total_ref[here, :] += dot(left_ref[:, here], right, 0, 0)


def mixer_forward_kernel(
    core_ref,
    x_ref,
    edge_ref,
    wa_own,
    wa_other,
    wb_own,
    wb_other,
    conv_ref,
    head_ref,
    skip_ref,
    start_ref,
    before_ref,
    *refs,
    heads,
    inner,
    taps,
    grouped,
    resumed,
):
    (
        normed_ref,
        ext_ref,
        dtr_ref,
        cum_ref,
        y_ref,
        sin_ref,
        end_ref,
        after_ref,
        tail_ref,
        state_ref,
        carried_ref,
        weighted_ref,
        wa_ref,
        wb_ref,
        wa_sems,
        wb_sems,
    ) = refs[6:] if resumed else refs
    block = pl.program_id(1)
    length, width = x_ref.shape

    @pl.when(jnp.logical_and(pl.program_id(0) == 0, block == 0))
    def _():
        copies = fetch_weight(core_ref, wa_own, wa_other, wa_ref, wa_sems)
        copies += fetch_weight(core_ref, wb_own, wb_other, wb_ref, wb_sems)
        for copy in copies:
            copy.wait()

    half = length // 2
    wide_a = wa_ref.shape[1]
    conv_dim = conv_ref.shape[1]
    state_dim = (conv_dim - inner) // 2

    def norm_of(rows):
        rows = rows.astype(f32)
        scale = lax.rsqrt(jnp.mean(rows * rows, axis=-1, keepdims=True) + norm_eps)
        return (rows * scale * conv_ref[taps + 1 : taps + 2, :width]).astype(bf16)

    @pl.when(block == 0)
    def _():
        if resumed:
            state_ref[...] = start_ref[...]
            tail_ref[...] = before_ref[...]
        elif grouped:
            state_ref[...] = start_ref[...]
            edge = norm_of(edge_ref[...])
            put_columns(tail_ref, slice(0, 8), dot(edge, wa_ref[...]), 0)
            edge_b = dot(edge, wb_ref[...])[:, : conv_dim - wide_a]
            put_columns(tail_ref, slice(0, 8), edge_b, wide_a // lanes)
        else:
            state_ref[...] = jnp.zeros_like(state_ref)
            tail_ref[...] = jnp.zeros_like(tail_ref)

    normed = norm_of(x_ref[...])
    normed_ref[...] = normed
    ext_ref[:, 0:8, :] = tail_ref[...]
    own_rows = slice(8, 8 + length)
    for at in range(0, wide_a, 2 * lanes):
        product = dot(normed, wa_ref[:, at : at + 2 * lanes])
        put_columns(ext_ref, own_rows, product, at // lanes)
    second = dot(normed, wb_ref[...])
    put_columns(ext_ref, own_rows, second[:, : conv_dim - wide_a], wide_a // lanes)
    dt_raw = second[:, conv_dim - wide_a :]
    tail_ref[...] = ext_ref[:, length : length + 8, :]

    lane = lax.broadcasted_iota(jnp.int32, (length, lanes), 1)
    low_lane = lane < lanes // 2
    head_lane = lane < heads
    dtr_ref[...] = dt_raw
    steps, _ = step_sizes(dt_raw, head_ref, head_lane)
    log_decay = steps * (-log2e * jnp.exp(head_ref[1:2, :]))
    row = lax.broadcasted_iota(jnp.int32, (length, length), 0)
    col = lax.broadcasted_iota(jnp.int32, (length, length), 1)
    cum = tri_sum((row >= col).astype(bf16), log_decay, head_lane)
    cum_ref[...] = cum
    cum_rows = cum.T

    def mixed_chunk(at):
        summed = conv_chunk(ext_ref, conv_ref, at, length, taps)
        return summed * sigmoid(summed)

    keys = jnp.concatenate(
        [mixed_chunk(inner + at) for at in range(0, state_dim, lanes)], axis=1
    ).astype(bf16)
    queries = jnp.concatenate(
        [mixed_chunk(inner + state_dim + at) for at in range(0, state_dim, lanes)], axis=1
    ).astype(bf16)
    state_low = state_ref[...].astype(bf16)
    sin_ref[...] = state_low
    carried_ref[...] = dot(queries, state_low)
    square = (half, half)
    diag = lax.broadcasted_iota(jnp.int32, square, 0) >= lax.broadcasted_iota(
        jnp.int32, square, 1
    )
    scores_00 = jnp.where(diag, dot(queries[:half], keys[:half], 1, 1), 0.0)
    scores_10 = dot(queries[half:], keys[:half], 1, 1)
    scores_11 = jnp.where(diag, dot(queries[half:], keys[half:], 1, 1), 0.0)
    for pair in range(heads // 2):
        at = pair * lanes
        values = mixed_chunk(at)
        cum_rep, cum_0, cum_1 = pair_columns(cum, pair, low_lane)
        dt_rep, _, _ = pair_columns(steps, pair, low_lane)
        stepped = values * dt_rep
        last = cum_rep[length - 1 : length, :]
        weighted_ref[:, at : at + lanes] = (stepped * jnp.exp2(last - cum_rep)).astype(bf16)
        top = None
        bottom = None
        for which, cum_col in ((0, cum_0), (1, cum_1)):
            own = jnp.where(low_lane if which == 0 else jnp.logical_not(low_lane), stepped, 0.0)
            own = own.astype(bf16)
            head = 2 * pair + which
            early = cum_rows[head : head + 1, :half]
            late = cum_rows[head : head + 1, half:]
            mix_00 = jnp.exp2(jnp.minimum(cum_col[:half] - early, 0.0)) * scores_00
            mix_10 = jnp.exp2(cum_col[half:] - early) * scores_10
            mix_11 = jnp.exp2(jnp.minimum(cum_col[half:] - late, 0.0)) * scores_11
            part_top = dot(mix_00.astype(bf16), own[:half])
            part_bottom = dot(
                jnp.concatenate([mix_10.astype(bf16), mix_11.astype(bf16)], axis=1), own
            )
            top = part_top if top is None else top + part_top
            bottom = part_bottom if bottom is None else bottom + part_bottom
        rest = (
            jnp.exp2(cum_rep) * carried_ref[:, at : at + lanes]
            + skip_ref[0:1, at : at + lanes] * values
        )
        y_ref[0:half, at : at + lanes] = top + rest[:half]
        y_ref[half:length, at : at + lanes] = bottom + rest[half:]
        state_ref[:, at : at + lanes] = jnp.exp2(last) * state_ref[:, at : at + lanes]

    state_ref[...] += dot(keys, weighted_ref[...], 0, 0)

    @pl.when(block == pl.num_programs(1) - 1)
    def _():
        end_ref[...] = state_ref[...]
        after_ref[...] = tail_ref[...]


def gate_kernel(
    core_ref,
    normed_ref,
    x_ref,
    cot_a_ref,
    cot_b_ref,
    y_ref,
    wg_own,
    wg_other,
    wo_own,
    wo_other,
    small_ref,
    out_ref,
    dy_ref,
    dgate_ref,
    dgain_ref,
    out_send,
    out_keep,
    gate_send,
    gate_keep,
    gate_ref,
    dno_ref,
    low_ref,
    cot_ref,
    out_sum,
    gate_sum,
    wg_ref,
    wo_ref,
    wg_sems,
    wo_sems,
    *,
    gain_row,
):
    length, inner = y_ref.shape
    first = jnp.logical_and(pl.program_id(0) == 0, pl.program_id(1) == 0)

    @pl.when(first)
    def _():
        copies = fetch_weight(core_ref, wg_own, wg_other, wg_ref, wg_sems)
        copies += fetch_weight(core_ref, wo_own, wo_other, wo_ref, wo_sems)
        dgain_ref[...] = jnp.zeros_like(dgain_ref)
        out_sum[...] = jnp.zeros_like(out_sum)
        gate_sum[...] = jnp.zeros_like(gate_sum)
        for copy in copies:
            copy.wait()

    gate_ref[...] = dot(normed_ref[...], wg_ref[...])
    cot_ref[:, : cot_a_ref.shape[1]] = cot_a_ref[...]
    cot_ref[:, cot_a_ref.shape[1] :] = cot_b_ref[...]
    dno_ref[...] = dot(cot_ref[...], wo_ref[...], 1, 1)
    squares = jnp.zeros((length, lanes), f32)
    crosses = jnp.zeros((length, lanes), f32)
    for at in range(0, inner, lanes):
        here = slice(at, at + lanes)
        gate = gate_ref[:, here]
        gated = y_ref[:, here] * (gate * sigmoid(gate))
        squares = squares + gated * gated
        crosses = crosses + gated * (small_ref[gain_row : gain_row + 1, here] * dno_ref[:, here])
    scale = lax.rsqrt(jnp.sum(squares, axis=1, keepdims=True) * (1.0 / inner) + norm_eps)
    cross = scale * scale * scale * (jnp.sum(crosses, axis=1, keepdims=True) * (1.0 / inner))
    scale_b = jnp.broadcast_to(scale, (length, lanes))
    cross_b = jnp.broadcast_to(cross, (length, lanes))
    for at in range(0, inner, lanes):
        here = slice(at, at + lanes)
        gate = gate_ref[:, here]
        mixed_out = y_ref[:, here]
        sig = sigmoid(gate)
        silu = gate * sig
        gated = mixed_out * silu
        scaled = gated * scale_b
        d_out = dno_ref[:, here]
        low_ref[:, here] = (scaled * small_ref[gain_row : gain_row + 1, here]).astype(bf16)
        dgain_ref[0:1, here] += jnp.sum(scaled * d_out, axis=0, keepdims=True)
        d_gated = scale_b * (small_ref[gain_row : gain_row + 1, here] * d_out) - gated * cross_b
        dy_ref[:, here] = (d_gated * silu).astype(bf16)
        dgate_ref[:, here] = (d_gated * mixed_out * (sig * (1.0 + gate * (1.0 - sig)))).astype(
            bf16
        )
    out_ref[...] = (x_ref[...].astype(f32) + dot(low_ref[...], wo_ref[...])).astype(bf16)
    add_product(out_sum, low_ref, cot_ref[...])
    add_product(gate_sum, normed_ref, dgate_ref[...])
    last = jnp.logical_and(
        pl.program_id(0) == pl.num_programs(0) - 1, pl.program_id(1) == pl.num_programs(1) - 1
    )

    @pl.when(last)
    def _():
        hand_out(core_ref[0], out_sum, out_send, out_keep)
        hand_out(core_ref[0], gate_sum, gate_send, gate_keep)


def mixer_backward_kernel(
    ext_ref,
    dtr_ref,
    cum_ref,
    y_ref,
    sin_ref,
    dy_ref,
    conv_ref,
    head_ref,
    skip_ref,
    sum_ref,
    start_ref,
    next_ref,
    small_in_ref,
    dgain_ref,
    _,
    dproj_ref,
    dconv_ref,
    end_ref,
    lead_ref,
    grad_ref,
    dsx_ref,
    dwv_ref,
    dye_ref,
    weighted_ref,
    zhigh_ref,
    zlow_ref,
    direct_ref,
    rows_ref,
    *,
    heads,
    inner,
    taps,
    fresh,
):
    step = pl.program_id(1)
    length = dy_ref.shape[0]
    half = length // 2
    conv_dim = conv_ref.shape[1]
    state_dim = (conv_dim - inner) // 2
    first = jnp.logical_and(pl.program_id(0) == 0, step == 0)

    @pl.when(first)
    def _():
        if small_in_ref.shape == dconv_ref.shape:
            dconv_ref[...] = small_in_ref[...]
        else:
            dconv_ref[...] = jnp.zeros_like(dconv_ref)
            dconv_ref[taps + 2 : taps + 3, :inner] = dgain_ref[0:1, :]
        rows_ref[...] = jnp.zeros_like(rows_ref)

    @pl.when(step == 0)
    def _():
        if fresh:
            grad_ref[...] = jnp.zeros_like(grad_ref)
            dsx_ref[:, length : length + 8, :] = jnp.zeros((conv_dim // lanes, 8, lanes), f32)
        else:
            grad_ref[...] = start_ref[...]
            dsx_ref[:, length : length + 8, :] = next_ref[...]

    @pl.when(step > 0)
    def _():
        dsx_ref[:, length : length + 8, :] = dsx_ref[:, 0:8, :]

    lane = lax.broadcasted_iota(jnp.int32, (length, lanes), 1)
    low_lane = lane < lanes // 2
    head_lane = lane < heads
    steps, shifted = step_sizes(dtr_ref[...], head_ref, head_lane)
    cum = cum_ref[...]
    cum_rows = cum.T

    def slope_chunk(at):
        summed = conv_chunk(ext_ref, conv_ref, at, length, taps)
        sig = sigmoid(summed)
        return summed * sig, sig * (1.0 + summed * (1.0 - sig))

    def put_grad(at, d_summed):
        here = slice(at, at + lanes)
        chunk = at // lanes
        dsx_ref[chunk, 0:length, :] = d_summed
        total = None
        for tap in range(taps):
            base = 8 - (taps - 1) + tap
            dconv_ref[tap : tap + 1, here] += jnp.sum(
                d_summed * ext_ref[chunk, base : base + length, :], axis=0, keepdims=True
            )
            back = taps - 1 - tap
            term = conv_ref[tap : tap + 1, here] * dsx_ref[chunk, back : back + length, :]
            total = term if total is None else total + term
        dconv_ref[taps : taps + 1, here] += jnp.sum(d_summed, axis=0, keepdims=True)
        dproj_ref[:, here] = total.astype(bf16)

    parts = [slope_chunk(inner + at) for at in range(0, 2 * state_dim, lanes)]
    count = state_dim // lanes
    keys = jnp.concatenate([part[0] for part in parts[:count]], axis=1).astype(bf16)
    queries = jnp.concatenate([part[0] for part in parts[count:]], axis=1).astype(bf16)
    grad_low = grad_ref[...].astype(bf16)
    dwv_ref[...] = dot(keys, grad_low)
    square = (half, half)
    diag = lax.broadcasted_iota(jnp.int32, square, 0) <= lax.broadcasted_iota(
        jnp.int32, square, 1
    )
    scores_00 = jnp.where(diag, dot(keys[:half], queries[:half], 1, 1), 0.0)
    scores_01 = dot(keys[:half], queries[half:], 1, 1)
    scores_11 = jnp.where(diag, dot(keys[half:], queries[half:], 1, 1), 0.0)
    ds_00 = jnp.zeros(square, f32)
    ds_01 = jnp.zeros(square, f32)
    ds_11 = jnp.zeros(square, f32)
    for pair in range(heads // 2):
        at = pair * lanes
        here = slice(at, at + lanes)
        values, slope = slope_chunk(at)
        cum_rep, cum_0, cum_1 = pair_columns(cum, pair, low_lane)
        dt_rep, _, _ = pair_columns(steps, pair, low_lane)
        stepped = (values * dt_rep).astype(bf16)
        stepped_f = stepped.astype(f32)
        last = cum_rep[length - 1 : length, :]
        tail = jnp.exp2(last - cum_rep)
        d_y = dy_ref[:, here]
        d_yf = d_y.astype(f32)
        d_y_t = d_yf.T.astype(bf16)
        dye_ref[:, here] = (d_yf * jnp.exp2(cum_rep)).astype(bf16)
        top = None
        bottom = None
        for which, cum_col in ((0, cum_0), (1, cum_1)):
            own_lane = low_lane if which == 0 else jnp.logical_not(low_lane)
            own_dy = jnp.where(own_lane, d_yf, 0.0).astype(bf16)
            own_x = jnp.where(own_lane, stepped_f, 0.0).astype(bf16)
            head = 2 * pair + which
            early = cum_rows[head : head + 1, :half]
            late = cum_rows[head : head + 1, half:]
            decay_00 = jnp.exp2(jnp.minimum(early - cum_col[:half], 0.0))
            decay_01 = jnp.exp2(late - cum_col[:half])
            decay_11 = jnp.exp2(jnp.minimum(late - cum_col[half:], 0.0))
            mix_0 = jnp.concatenate(
                [(decay_00 * scores_00).astype(bf16), (decay_01 * scores_01).astype(bf16)], axis=1
            )
            mix_1 = (decay_11 * scores_11).astype(bf16)
            part_top = dot(mix_0, own_dy)
            part_bottom = dot(mix_1, own_dy[half:])
            top = part_top if top is None else top + part_top
            bottom = part_bottom if bottom is None else bottom + part_bottom
            d_mix_0 = dot(own_x[:half], d_y_t)
            d_mix_1 = dot(own_x[half:], d_y_t[:, half:])
            ds_00 = ds_00 + decay_00 * d_mix_0[:, :half]
            ds_01 = ds_01 + decay_01 * d_mix_0[:, half:]
            ds_11 = ds_11 + decay_11 * d_mix_1
        d_diag = jnp.concatenate([top, bottom], axis=0)
        weighted = (stepped_f * tail).astype(bf16)
        weighted_ref[:, here] = weighted
        d_weighted = dwv_ref[:, here]
        through = weighted.astype(f32) * d_weighted
        d_stepped = d_diag + tail * d_weighted
        skip = skip_ref[0:1, here]
        z = d_yf * (y_ref[:, here] - skip * values) - stepped_f * d_diag - through
        z_high, z_low = halves(z)
        zhigh_ref[:, here] = z_high
        zlow_ref[:, here] = z_low
        direct_ref[:, here] = (d_stepped * values).astype(bf16)
        total_decay = jnp.exp2(last)
        rows_ref[0:1, here] = jnp.sum(through, axis=0, keepdims=True) + total_decay * jnp.sum(
            grad_ref[:, here] * sin_ref[:, here].astype(f32), axis=0, keepdims=True
        )
        rows_ref[1:2, here] = jnp.sum(d_yf * values, axis=0, keepdims=True)
        put_grad(at, (d_stepped * dt_rep + skip * d_yf) * slope)
        grad_ref[:, here] = total_decay * grad_ref[:, here]

    grad_ref[...] += dot(queries, dye_ref[...], 0, 0)
    ds_00 = jnp.where(diag, ds_00, 0.0).astype(bf16)
    ds_11 = jnp.where(diag, ds_11, 0.0).astype(bf16)
    ds_01 = ds_01.astype(bf16)
    d_queries = dot(dye_ref[...], sin_ref[...], 1, 1)
    d_keys = dot(weighted_ref[...], grad_low, 1, 1)
    d_queries = d_queries + jnp.concatenate(
        [
            dot(ds_00, keys[:half], 0, 0),
            dot(ds_01, keys[:half], 0, 0) + dot(ds_11, keys[half:], 0, 0),
        ],
        axis=0,
    )
    d_keys = d_keys + jnp.concatenate(
        [
            dot(ds_00, queries[:half]) + dot(ds_01, queries[half:]),
            dot(ds_11, queries[half:]),
        ],
        axis=0,
    )
    for at in range(0, state_dim, lanes):
        put_grad(inner + at, d_keys[:, at : at + lanes] * parts[at // lanes][1])
        put_grad(
            inner + state_dim + at,
            d_queries[:, at : at + lanes] * parts[count + at // lanes][1],
        )
    summing = sum_ref[...]
    rows_high, rows_low = halves(rows_ref[...])
    row_sums = dot(rows_high, summing) + dot(rows_low, summing)
    d_cum = dot(zhigh_ref[...], summing) + dot(zlow_ref[...], summing)
    at_last = lax.broadcasted_iota(jnp.int32, (length, lanes), 0) == length - 1
    d_cum = d_cum + jnp.where(at_last, row_sums[0:1, :], 0.0)
    row = lax.broadcasted_iota(jnp.int32, (length, length), 0)
    col = lax.broadcasted_iota(jnp.int32, (length, length), 1)
    d_log = tri_sum((row <= col).astype(bf16), d_cum, head_lane)
    rate = jnp.exp(head_ref[1:2, :])
    d_steps = dot(direct_ref[...], summing) - rate * d_log
    d_raw = jnp.where(head_lane, d_steps * sigmoid(shifted), 0.0)
    dproj_ref[:, conv_dim : conv_dim + lanes] = d_raw.astype(bf16)
    head_row = slice(taps + 3, taps + 4)
    dconv_ref[head_row, :lanes] += jnp.sum(d_raw, axis=0, keepdims=True)
    dconv_ref[head_row, lanes : 2 * lanes] += jnp.sum(d_log * steps, axis=0, keepdims=True) * (
        -rate
    )
    dconv_ref[head_row, 2 * lanes : 3 * lanes] += row_sums[1:2, :]

    @pl.when(step == pl.num_programs(1) - 1)
    def _():
        end_ref[...] = grad_ref[...]
        lead_ref[...] = dsx_ref[:, 0:8, :]


def input_grad_kernel(
    core_ref,
    x_ref,
    dgate_ref,
    dproj_ref,
    small_ref,
    dsmall_in_ref,
    wg_own,
    wg_other,
    wa_own,
    wa_other,
    wb_own,
    wb_other,
    dx_ref,
    dsmall_ref,
    a_send,
    a_keep,
    b_send,
    b_keep,
    normed_ref,
    a_sum,
    b_sum,
    wg_ref,
    wa_ref,
    wb_ref,
    wg_sems,
    wa_sems,
    wb_sems,
    *,
    gain_row,
):
    first = jnp.logical_and(pl.program_id(0) == 0, pl.program_id(1) == 0)
    width = x_ref.shape[1]

    @pl.when(first)
    def _():
        copies = fetch_weight(core_ref, wg_own, wg_other, wg_ref, wg_sems)
        copies += fetch_weight(core_ref, wa_own, wa_other, wa_ref, wa_sems)
        copies += fetch_weight(core_ref, wb_own, wb_other, wb_ref, wb_sems)
        dsmall_ref[...] = dsmall_in_ref[...]
        a_sum[...] = jnp.zeros_like(a_sum)
        b_sum[...] = jnp.zeros_like(b_sum)
        for copy in copies:
            copy.wait()

    wide_a = wa_ref.shape[1]
    d_normed = (
        dot(dgate_ref[...], wg_ref[...], 1, 1)
        + dot(dproj_ref[:, :wide_a], wa_ref[...], 1, 1)
        + dot(dproj_ref[:, wide_a:], wb_ref[...], 1, 1)
    )
    rows = x_ref[...].astype(f32)
    scale = lax.rsqrt(jnp.mean(rows * rows, axis=-1, keepdims=True) + norm_eps)
    scaled = rows * scale
    dsmall_ref[gain_row : gain_row + 1, :width] += jnp.sum(
        scaled * d_normed, axis=0, keepdims=True
    )
    gain = small_ref[gain_row : gain_row + 1, :width]
    normed_ref[...] = (scaled * gain).astype(bf16)
    add_product(a_sum, normed_ref, dproj_ref[:, :wide_a])
    add_product(b_sum, normed_ref, dproj_ref[:, wide_a:])
    inner_grad = gain * d_normed
    cross = jnp.mean(scaled * inner_grad, axis=-1, keepdims=True)
    dx_ref[...] = (scale * (inner_grad - scaled * cross)).astype(bf16)
    last = jnp.logical_and(
        pl.program_id(0) == pl.num_programs(0) - 1, pl.program_id(1) == pl.num_programs(1) - 1
    )

    @pl.when(last)
    def _():
        hand_out(core_ref[0], a_sum, a_send, a_keep)
        hand_out(core_ref[0], b_sum, b_send, b_keep)


def adam_kernel(
    rates_ref,
    *refs,
    heads,
    taps,
    at_refs,
    arrivals,
):
    sum_refs, refs = refs[:arrivals], refs[arrivals:]
    rest_refs, front_refs, refs = refs[:arrivals], refs[arrivals : 2 * arrivals], refs[2 * arrivals :]
    ins, outs = refs[:18], refs[18:]
    learn_rate, decay_rate = rates_ref[0], rates_ref[3]
    beta_one, beta_two = rates_ref[1], rates_ref[2]
    first_scale, second_scale = rates_ref[4], rates_ref[5]

    def update(which, grad, index):
        master, first, second = (ref[index] for ref in ins[3 * which : 3 * which + 3])
        new_first = beta_one * first + (1.0 - beta_one) * grad
        new_second = beta_two * second + (1.0 - beta_two) * grad * grad
        change = -learn_rate * (
            (new_first * first_scale) / (jnp.sqrt(new_second * second_scale) + adam_eps)
            + decay_rate * master
        )
        where = at_refs[which]
        outs[where][index] = master + change if which in (1, 4) else change
        outs[where + 1][index] = new_first
        outs[where + 2][index] = new_second
        if which in (1, 4):
            outs[-2 if which == 1 else -1][index] = (master + change).astype(bf16)

    everything = (slice(None), slice(None))
    rest, front = rest_refs[0][...], front_refs[0][...]
    inner = rest.shape[1] // 2
    for rest_ref, front_ref in zip(rest_refs[1:], front_refs[1:]):
        rest = rest + rest_ref[...].astype(f32)
        front = front + front_ref[...].astype(f32)
    proj = ins[3].shape[1]
    update(1, rest[:, :inner], (slice(None), slice(0, inner)))
    update(1, front[:, : proj - inner], (slice(None), slice(inner, proj)))
    rows = rest.shape[0]
    half = inner // 2
    update(4, rest[:, inner : inner + half], (slice(0, rows), slice(None)))
    update(4, rest[:, inner + half :], (slice(rows, 2 * rows), slice(None)))

    place = rates_ref[7].astype(jnp.int32)
    terms = [ref[...] for ref in sum_refs]
    sums = terms[0]
    for term in terms[1:]:
        sums = sums + term

    def own(at, count):
        wide = sums.shape[1]
        shift = lax.rem(wide - place * count, wide)
        return pltpu.roll(sums, shift, 1)[at, :count]

    update(0, own(slice(taps + 1, taps + 2), ins[0].shape[1]), everything)
    update(2, own(slice(0, taps + 1), ins[6].shape[1]), everything)
    update(3, own(slice(taps + 2, taps + 3), ins[9].shape[1]), everything)
    sums = jnp.zeros_like(sums)
    for source in range(arrivals):
        distance = lax.rem(place + arrivals - source, arrivals)
        term = terms[0]
        for which in range(1, arrivals):
            term = jnp.where(distance == which, terms[which], term)
        sums = sums + term
    head_row = slice(taps + 3, taps + 4)
    for row in range(3):
        grad = sums[head_row, row * lanes : row * lanes + heads]
        update(5, grad, (slice(row, row + 1), slice(None)))


def whole(shape):
    return pl.BlockSpec(shape, lambda p, b: (0,) * len(shape))


def by_block(shape, size, back=False):
    if back:
        return pl.BlockSpec(shape, lambda p, s: (p * size + (size - 1 - s), 0))
    return pl.BlockSpec(shape, lambda p, b: (p * size + b, 0))


def by_part(shape):
    return pl.BlockSpec(shape, lambda p, b: (p, 0))


def params():
    return pltpu.CompilerParams(
        dimension_semantics=("arbitrary", "arbitrary"), vmem_limit_bytes=vmem_bytes
    )


def cost(flops, moved, powers):
    return pl.CostEstimate(flops=flops, bytes_accessed=moved, transcendentals=powers)


ANY = pl.BlockSpec(memory_space=pl.ANY)
SMEM = pl.BlockSpec(memory_space=pltpu.SMEM)


def weight_scratch(*weights):
    wholes = [
        pltpu.VMEM((2 * own.shape[0] * own.shape[1], own.shape[2]), bf16) for own, _ in weights
    ]
    return wholes + [pltpu.SemaphoreType.DMA((2 * own.shape[0],)) for own, _ in weights]


def handed_out(rows, columns, blocks):
    shape = (blocks, rows // (2 * blocks), columns)
    return [jax.ShapeDtypeStruct(shape, bf16), jax.ShapeDtypeStruct(shape, f32)]


def mixer_forward(dims, core, tokens, wa, wb, small, head, skip, edge, start, grouped, kept, blocks):
    part, size, piece, width, inner, heads, taps = dims
    first, count = blocks
    conv_dim = small.shape[1]
    state_dim = (conv_dim - inner) // 2
    all_blocks = part * size
    rows = all_blocks * piece
    ext_rows = piece + 8
    chunks = conv_dim // lanes
    resumed = kept is not None

    def by_block(shape):
        return pl.BlockSpec(shape, lambda p, b: (p * size + first + b, 0))

    tail_block = pl.BlockSpec((chunks, 8, lanes), lambda p, b: (p, 0, 0))
    before = core
    if resumed:
        *arrays, start, before = kept
    else:
        arrays = []
    return pl.pallas_call(
        partial(
            mixer_forward_kernel,
            heads=heads,
            inner=inner,
            taps=taps,
            grouped=grouped,
            resumed=resumed,
        ),
        grid=(part, count),
        in_specs=[
            SMEM,
            by_block((piece, width)),
            by_part((8, width)) if grouped else ANY,
            ANY,
            ANY,
            ANY,
            ANY,
            whole(small.shape),
            whole(head.shape),
            whole(skip.shape),
            by_part((state_dim, inner)) if grouped or resumed else ANY,
            tail_block if resumed else ANY,
        ]
        + [ANY] * len(arrays),
        out_specs=[
            by_block((piece, width)),
            pl.BlockSpec((chunks, ext_rows, lanes), lambda p, b: (p * size + first + b, 0, 0)),
            by_block((piece, lanes)),
            by_block((piece, lanes)),
            by_block((piece, inner)),
            by_block((state_dim, inner)),
            by_part((state_dim, inner)),
            tail_block,
        ],
        out_shape=[
            jax.ShapeDtypeStruct((rows, width), bf16),
            jax.ShapeDtypeStruct((all_blocks * chunks, ext_rows, lanes), f32),
            jax.ShapeDtypeStruct((rows, lanes), f32),
            jax.ShapeDtypeStruct((rows, lanes), f32),
            jax.ShapeDtypeStruct((rows, inner), f32),
            jax.ShapeDtypeStruct((all_blocks * state_dim, inner), bf16),
            jax.ShapeDtypeStruct((part * state_dim, inner), f32),
            jax.ShapeDtypeStruct((part * chunks, 8, lanes), f32),
        ],
        scratch_shapes=[
            pltpu.VMEM((chunks, 8, lanes), f32),
            pltpu.VMEM((state_dim, inner), f32),
            pltpu.VMEM((piece, inner), f32),
            pltpu.VMEM((piece, inner), bf16),
        ]
        + weight_scratch(wa, wb),
        input_output_aliases={12 + at: at for at in range(len(arrays))},
        compiler_params=params(),
        cost_estimate=cost(1, 1, 0),
    )(core, tokens, edge, *wa, *wb, small, head, skip, start, before, *arrays)


def gate_step(dims, core, normed, tokens, cots_b, y, wg, wo, small):
    part, size, piece, width, inner, heads, taps = dims
    rows = part * size * piece
    blocks = wo[0].shape[0]
    handed = handed_out(inner, width, blocks) + handed_out(width, inner, blocks)
    wide_b = cots_b.shape[1]
    at_a = width // (width - wide_b)
    return pl.pallas_call(
        partial(gate_kernel, gain_row=taps + 2),
        grid=(part, size),
        in_specs=[
            SMEM,
            by_block((piece, width), size),
            by_block((piece, width), size),
            pl.BlockSpec((piece, width - wide_b), lambda p, b: (p * size + b, at_a)),
            by_block((piece, wide_b), size),
            by_block((piece, inner), size),
            ANY,
            ANY,
            ANY,
            ANY,
            whole(small.shape),
        ],
        out_specs=[
            by_block((piece, width), size),
            by_block((piece, inner), size),
            by_block((piece, inner), size),
            whole((8, inner)),
        ]
        + [whole(array.shape) for array in handed],
        out_shape=[
            jax.ShapeDtypeStruct((rows, width), bf16),
            jax.ShapeDtypeStruct((rows, inner), bf16),
            jax.ShapeDtypeStruct((rows, inner), bf16),
            jax.ShapeDtypeStruct((8, inner), f32),
        ]
        + handed,
        scratch_shapes=[
            pltpu.VMEM((piece, inner), f32),
            pltpu.VMEM((piece, inner), f32),
            pltpu.VMEM((piece, inner), bf16),
            pltpu.VMEM((piece, width), bf16),
            pltpu.VMEM((inner, width), f32),
            pltpu.VMEM((width, inner), f32),
        ]
        + weight_scratch(wg, wo),
        compiler_params=params(),
        cost_estimate=cost(1, 1, 0),
    )(core, normed, tokens, tokens, cots_b, y, *wg, *wo, small)


def mixer_backward(dims, saved, consts, carry, blocks, fresh):
    part, size, piece, width, inner, heads, taps = dims
    first, count = blocks
    small, head, skip, summing, dgain = consts
    conv_dim = small.shape[1]
    state_dim = (conv_dim - inner) // 2
    ext_rows = piece + 8
    chunks = conv_dim // lanes
    wide = conv_dim + lanes
    dproj, dsmall, state, lead = carry
    lead_block = pl.BlockSpec((chunks, 8, lanes), lambda p, s: (p, 0, 0))

    def by_block(shape):
        return pl.BlockSpec(shape, lambda p, s: (p * size + (first + count - 1 - s), 0))

    return pl.pallas_call(
        partial(mixer_backward_kernel, heads=heads, inner=inner, taps=taps, fresh=fresh),
        grid=(part, count),
        in_specs=[
            pl.BlockSpec(
                (chunks, ext_rows, lanes), lambda p, s: (p * size + (first + count - 1 - s), 0, 0)
            ),
            by_block((piece, lanes)),
            by_block((piece, lanes)),
            by_block((piece, inner)),
            by_block((state_dim, inner)),
            by_block((piece, inner)),
            whole(small.shape),
            whole(head.shape),
            whole(skip.shape),
            whole(summing.shape),
            ANY if fresh else by_part((state_dim, inner)),
            ANY if fresh else lead_block,
            whole(dsmall.shape),
            whole(dgain.shape),
            ANY,
        ],
        out_specs=[
            by_block((piece, wide)),
            whole((8, conv_dim)),
            by_part((state_dim, inner)),
            lead_block,
        ],
        out_shape=[
            jax.ShapeDtypeStruct((part * size * piece, wide), bf16),
            jax.ShapeDtypeStruct((8, conv_dim), f32),
            jax.ShapeDtypeStruct((part * state_dim, inner), f32),
            jax.ShapeDtypeStruct((part * chunks, 8, lanes), f32),
        ],
        scratch_shapes=[
            pltpu.VMEM((state_dim, inner), f32),
            pltpu.VMEM((chunks, ext_rows, lanes), f32),
            pltpu.VMEM((piece, inner), f32),
            pltpu.VMEM((piece, inner), bf16),
            pltpu.VMEM((piece, inner), bf16),
            pltpu.VMEM((piece, inner), bf16),
            pltpu.VMEM((piece, inner), bf16),
            pltpu.VMEM((piece, inner), bf16),
            pltpu.VMEM((8, inner), f32),
        ],
        input_output_aliases={14: 0} if dproj.shape[0] == part * size * piece else {},
        compiler_params=params(),
        cost_estimate=cost(1, 1, 0),
    )(*saved, small, head, skip, summing, state, lead, dsmall, dgain, dproj)


def input_grad(dims, core, tokens, dgate, dproj, small, dsmall, wg, wa, wb):
    part, size, piece, width, inner, heads, taps = dims
    rows = part * size * piece
    blocks = wa[0].shape[0]
    wide_a, wide_b = wa[0].shape[2], wb[0].shape[2]
    handed = handed_out(width, wide_a, blocks) + handed_out(width, wide_b, blocks)
    return pl.pallas_call(
        partial(input_grad_kernel, gain_row=taps + 1),
        grid=(part, size),
        in_specs=[
            SMEM,
            by_block((piece, width), size),
            by_block((piece, inner), size),
            by_block((piece, dproj.shape[1]), size),
            whole(small.shape),
            whole(dsmall.shape),
            ANY,
            ANY,
            ANY,
            ANY,
            ANY,
            ANY,
        ],
        out_specs=[by_block((piece, width), size), whole(dsmall.shape)]
        + [whole(array.shape) for array in handed],
        out_shape=[
            jax.ShapeDtypeStruct((rows, width), bf16),
            jax.ShapeDtypeStruct(dsmall.shape, f32),
        ]
        + handed,
        scratch_shapes=[
            pltpu.VMEM((piece, width), bf16),
            pltpu.VMEM((width, wide_a), f32),
            pltpu.VMEM((width, wide_b), f32),
        ]
        + weight_scratch(wg, wa, wb),
        compiler_params=params(),
        cost_estimate=cost(1, 1, 0),
    )(core, tokens, dgate, dproj, small, dsmall, *wg, *wa, *wb)


def adam(rates, sums, gate_grads, front_grads, states, heads, taps):
    outs = []
    at_refs = []
    for which, (master, first, second) in enumerate(states):
        at_refs.append(len(outs))
        outs += [jax.ShapeDtypeStruct(master.shape, f32)] * 3
    outs.append(jax.ShapeDtypeStruct(states[1][0].shape, bf16))
    outs.append(jax.ShapeDtypeStruct(states[4][0].shape, bf16))
    flat = [array for state in states for array in state]
    vmem = pl.BlockSpec(memory_space=pltpu.VMEM)
    return pl.pallas_call(
        partial(
            adam_kernel, heads=heads, taps=taps, at_refs=at_refs, arrivals=len(gate_grads)
        ),
        in_specs=[SMEM] + [vmem] * (3 * len(gate_grads) + len(flat)),
        out_specs=[vmem] * len(outs),
        out_shape=outs,
        compiler_params=pltpu.CompilerParams(vmem_limit_bytes=vmem_bytes),
        cost_estimate=cost(1, 1, 0),
    )(rates, *sums, *gate_grads, *front_grads, *flat)


def bit_count(extent):
    count = extent.bit_length() - 1
    if 1 << count != extent:
        raise ValueError(extent)
    return count


def swap(block, axis, bit):
    devices = range(lax.axis_size(axis))
    return lax.ppermute(block, axis, [(i, i ^ (1 << bit)) for i in devices])


def shifted_by(block, axis, distance):
    devices = range(lax.axis_size(axis))
    route = [(i, i + distance) for i in devices if i + distance in devices]
    return lax.ppermute(block, axis, route)


def pick(block, at, axis):
    return lax.dynamic_index_in_dim(block, at, axis, keepdims=False)


def gather_bit(block, axis, bit, at, *others):
    mine = (lax.axis_index(axis) >> bit) & 1
    other = swap(block, axis, bit)
    if others:
        other = after(other, *others)
    low = jnp.where(mine == 1, other, block)
    high = jnp.where(mine == 1, block, other)
    return jnp.stack([low, high], axis=at)


def gather_seq(shard, *others):
    block = shard
    for done, bit in enumerate(reversed(range(bit_count(lax.axis_size("seq"))))):
        block = gather_bit(block, "seq", bit, done, *(others if done == 0 else ()))
    return block.reshape((-1,) + shard.shape)


def dp_orders():
    bits = bit_count(lax.axis_size("dp"))
    return list(range(bits - 1, 0, -1)) + [0], list(range(1, bits)) + [0]


def gather_dp_bit(block, order, step, *others):
    at = sum(1 for b in order[:step] if b > order[step])
    return gather_bit(block, "dp", order[step], at, *others)


def give_half(block, axis, bit, at):
    mine = (lax.axis_index(axis) >> bit) & 1
    other = swap(pick(block, 1 - mine, at).astype(bf16), axis, bit)
    return pick(block, mine, at) + other.astype(f32)


def core_sums(send, keep):
    extent = lax.axis_size("seq")
    bits = bit_count(lax.axis_size("dp")) - 1
    shape = (2,) * bits + (extent, -1, send.shape[2])
    other = swap(send, "dp", 0)
    return keep.reshape(shape), other.reshape(shape)


def core_and_next(keep, other, order):
    bit = order[-2]
    at = sum(1 for b in order[:-2] if b > bit)
    mine = (lax.axis_index("dp") >> bit) & 1
    sent = pick(keep, 1 - mine, at) + pick(other, 1 - mine, at).astype(f32)
    arrived = swap(sent.astype(bf16), "dp", bit)
    return pick(keep, mine, at) + pick(other, mine, at).astype(f32), arrived


def scatter_dp_bit(block, order, step):
    bit = order[-1 - step]
    return give_half(block, "dp", bit, sum(1 for b in order[: len(order) - 1 - step] if b > bit))


def scatter_seq(block):
    extent = lax.axis_size("seq")
    place = lax.axis_index("seq")
    arrivals = [pick(block, place, 0)]
    for distance in range(1, extent):
        sent = pick(block, lax.rem(place + distance, extent), 0).astype(bf16)
        route = [(i, (i + distance) % extent) for i in range(extent)]
        arrivals.append(lax.ppermute(sent, "seq", route))
    return arrivals


def sum_bits(block, axis, bits):
    for bit in bits:
        block = block + swap(block, axis, bit)
    return block


def seq_groups(size):
    extent = lax.axis_size("seq")
    if size == extent:
        return None
    return [list(range(at, at + size)) for at in range(0, extent, size)]


def to_sequences(block, part, size):
    if size > 1:
        block = lax.all_to_all(
            block, "seq", 0, 0, axis_index_groups=seq_groups(size), tiled=True
        )
    piece, width = block.shape[1:]
    block = block.reshape(size, part, piece, width)
    if part > 1:
        block = block.transpose(1, 0, 2, 3)
    return block.reshape(-1, width)


def to_pieces(rows, part, size, piece):
    block = rows.reshape(part, size, piece, -1)
    if part > 1:
        block = block.transpose(1, 0, 2, 3)
    block = block.reshape(part * size, piece, -1)
    if size > 1:
        block = lax.all_to_all(
            block, "seq", 0, 0, axis_index_groups=seq_groups(size), tiled=True
        )
    return block


def after(value, *others):
    return lax.optimization_barrier((value,) + others)[0]


def padded(block, rows, columns):
    return jnp.pad(block, ((0, rows - block.shape[0]), (0, columns - block.shape[1])))


def summing_matrix(inner, heads):
    columns = np.zeros((inner, lanes), np.float32)
    columns[np.arange(inner), np.arange(inner) // (inner // heads)] = 1.0
    return jnp.asarray(columns, bf16)


def local(
    layer_in,
    out_grad,
    norm_gain,
    in_weight,
    conv_params,
    gate_gain,
    out_weight,
    head_params,
    norm_first,
    norm_second,
    in_first,
    in_second,
    conv_first,
    conv_second,
    gate_first,
    gate_second,
    out_first,
    out_second,
    head_first,
    head_second,
    step_count,
    hyper,
):
    seq_count, piece, width = layer_in.shape
    seq_extent = lax.axis_size("seq")
    me = lax.axis_index("dp") * seq_extent + lax.axis_index("seq")
    step_float = step_count[0].astype(f32)
    scales = 1.0 / (1.0 - hyper[1:3] ** step_float)
    place = lax.axis_index("seq")
    rates = jnp.concatenate([hyper, scales, jnp.stack([me.astype(f32), place.astype(f32)])])
    core = (lax.axis_index("dp") & 1).astype(jnp.int32)[None]
    owners = lax.axis_size("dp") * seq_extent
    size = math.gcd(seq_extent, seq_count)
    part = seq_count // size
    groups = seq_extent // size
    inner = out_weight.shape[0] * owners
    heads = head_params.shape[1]
    tap_rows, conv_own = conv_params.shape
    taps = tap_rows - 1
    conv_dim = conv_own * owners
    state_dim = (conv_dim - inner) // 2
    own_rows = in_weight.shape[0]
    gate_own = gate_gain.shape[0]
    wide_a = min(1024, inner)
    dims = (part, size, piece, width, inner, heads, taps)

    head = padded(head_params, 8, lanes)
    skip = jnp.repeat(head_params[2], inner // heads)[None, :]
    summing = summing_matrix(inner, heads)

    in_low = padded(in_weight.astype(bf16), own_rows, inner + conv_dim + lanes)
    out_low_own = out_weight.astype(bf16).reshape(2, own_rows, width)
    own_small = jnp.concatenate(
        [
            padded(conv_params.astype(bf16), tap_rows, lanes),
            padded(norm_gain.astype(bf16)[None, :], 1, lanes),
            padded(gate_gain.astype(bf16)[None, :], 1, lanes),
        ]
    )
    shard = jnp.concatenate([in_low, out_low_own[0], out_low_own[1]], axis=1)
    half = width // 6
    both = jnp.concatenate([layer_in, out_grad[:, :, :half]], axis=2)
    second = lax.optimization_barrier(out_grad[:, :, half:])
    if own_rows >= tap_rows + 2:
        shard = jnp.concatenate([shard, padded(own_small, own_rows, lanes)], axis=1)
        gathered = gather_seq(shard, both, second, head, skip)
        seq_small = gathered[:, : tap_rows + 2, -lanes:]
    else:
        gathered = gather_seq(shard)
        seq_small = gather_seq(padded(own_small, 8, lanes))[:, : tap_rows + 2]
    tokens = to_sequences(after(both, shard), part, size)
    small = jnp.zeros((8, conv_dim), bf16)
    group = lax.axis_index("dp")
    for at, rows, count in (
        (0, tap_rows, conv_own),
        (tap_rows, 1, own_rows),
        (tap_rows + 1, 1, gate_own),
    ):
        piece_rows = jnp.concatenate(
            [seq_small[z, at : at + rows, :count] for z in range(seq_extent)], axis=1
        )
        small = lax.dynamic_update_slice(small, piece_rows, (at, group * seq_extent * count))
    front_end = inner + conv_dim + lanes
    wg = gathered[:, :, :inner]
    wa = gathered[:, :, inner : inner + wide_a]
    wb = gathered[:, :, inner + wide_a : front_end]
    wo = jnp.stack(
        [
            gathered[:, :, front_end : front_end + width],
            gathered[:, :, front_end + width : front_end + 2 * width],
        ],
        axis=1,
    ).reshape(-1, 2 * own_rows, width)
    order_a, order_b = dp_orders()
    last = len(order_a) - 1
    for step in range(last):
        wa = gather_dp_bit(wa, order_a, step)
        wb = gather_dp_bit(wb, order_b, step)
    small = sum_bits(small, "dp", order_a[:-1])
    for step in range(last):
        if step == 1:
            wg, wo = after((wg, wo), wa, wb, small)
        if step < last - 1:
            wg = gather_dp_bit(wg, order_a, step)
            wo = gather_dp_bit(wo, order_b, step)

    def core_halves(block):
        block = block.reshape(owners // 2 // seq_extent, -1, block.shape[-1])
        return block, swap(block, "dp", 0)

    wb = core_halves(wb)
    wa = core_halves(wa)
    small = sum_bits(after(small, tokens, wa, wb, head, skip), "dp", [0]).astype(f32)
    cots_b = to_sequences(after(second, tokens), part, size)

    edge = core
    if groups > 1:
        edge = tokens.reshape(part, size * piece, -1)[:, size * piece - 8 :, :width]
        edge = shifted_by(edge, "seq", size).reshape(part * 8, width)

    def forward(start, kept, blocks):
        weights = (wa, wb, small, head, skip)
        grouped = groups > 1
        return mixer_forward(dims, core, tokens, *weights, edge, start, grouped, kept, blocks)

    start = core
    if groups > 1:
        first_out = forward(jnp.zeros((part * state_dim, inner), f32), None, (0, size))
        cum_last = first_out[3].reshape(part, size, piece, lanes)[:, :, piece - 1, :heads]
        decay = jnp.exp2(jnp.sum(cum_last, axis=1))
        decay = jnp.repeat(decay, inner // heads, axis=1)[:, None, :]

        def relay(ends, distance):
            ends = ends.reshape(part, state_dim, inner)
            carried = jnp.zeros_like(ends)
            for _ in range(groups - 1):
                sent = (decay * carried + ends).astype(bf16)
                carried = shifted_by(sent, "seq", distance).astype(f32)
            return carried.reshape(part * state_dim, inner)

        start = relay(first_out[6], size)
    normed, ext, dtr, cum, y, sin, _, _ = forward(start, None, (0, size))
    wg = core_halves(gather_dp_bit(wg, order_a, last - 1, normed))
    wo = core_halves(gather_dp_bit(wo, order_b, last - 1, normed))
    layer_rows, dy, dgate, dgain, *handed = gate_step(
        dims, core, normed, tokens, cots_b, y, wg, wo, small
    )
    layer_out = to_pieces(layer_rows, part, size, piece)
    consts = (small, head, skip, summing, dgain)
    saved = (ext, dtr, cum, y, sin, dy)

    def backward(carry, blocks, fresh=False):
        return list(mixer_backward(dims, saved, consts, carry, blocks, fresh))

    def fresh_carry():
        if groups == 1:
            return (core, head, core, core)
        lead = jnp.zeros((part * (conv_dim // lanes), 8, lanes), f32)
        first_out = (core, head, jnp.zeros((part * state_dim, inner), f32), lead)
        first_out = backward(first_out, (0, size))
        return (core, head, relay(first_out[2], -size), lead)

    calls = [(size - 1, 1), (size - 2, 1), (0, size - 2)]
    g_out = core_sums(*handed[:2])
    g_gate = core_sums(*handed[2:])
    carry = backward(fresh_carry(), calls[0], groups == 1)
    carry[2], g_out, g_gate = lax.optimization_barrier((carry[2], g_out, g_gate))
    g_out = core_and_next(*g_out, order_a)
    g_gate = core_and_next(*g_gate, order_b)
    carry = backward(carry, calls[1])
    carry[2], g_out, g_gate = lax.optimization_barrier((carry[2], g_out, g_gate))
    g_out = g_out[0] + g_out[1].astype(f32)
    g_gate = g_gate[0] + g_gate[1].astype(f32)
    for step in range(2, last + 1):
        g_out = scatter_dp_bit(g_out, order_a, step)
        g_gate = scatter_dp_bit(g_gate, order_b, step)
    carry = backward(carry, calls[2])
    carry[0], g_out, g_gate = lax.optimization_barrier((carry[0], g_out, g_gate))
    g_rest = scatter_seq(
        jnp.concatenate([g_gate, g_out[:, :own_rows], g_out[:, own_rows:]], axis=2)
    )
    dproj, dsmall, _, lead = carry
    if groups > 1:
        lead = shifted_by(lead.astype(bf16), "seq", -size).astype(f32)
        lead = lead.reshape(part, -1, 8, lanes).transpose(0, 2, 1, 3).reshape(part, 8, conv_dim)
        fixes = []
        for row in range(taps - 1):
            terms = [small[tap] * lead[:, row - tap] for tap in range(row + 1)]
            fixes.append(sum(terms[1:], terms[0]))
        fix = jnp.pad(jnp.stack(fixes, axis=1), ((0, 0), (0, 0), (0, lanes)))
        dproj = dproj.reshape(part, size * piece, conv_dim + lanes)
        ends = dproj[:, size * piece - (taps - 1) :].astype(f32) + fix
        dproj = dproj.at[:, size * piece - (taps - 1) :].set(ends.astype(bf16))
        dproj = dproj.reshape(-1, conv_dim + lanes)
    tokens = after(tokens, layer_out, dproj)
    dx, dsmall, *handed = input_grad(dims, core, tokens, dgate, dproj, small, dsmall, wg, wa, wb)
    dx, dsmall, handed, g_rest = lax.optimization_barrier((dx, dsmall, handed, g_rest))
    g_a = core_sums(*handed[:2])
    g_b = core_sums(*handed[2:])
    g_a = core_and_next(*g_a, order_a)
    g_b = core_and_next(*g_b, order_b)
    g_a = g_a[0] + g_a[1].astype(f32)
    g_b = g_b[0] + g_b[1].astype(f32)
    for step in range(2, last + 1):
        g_a = scatter_dp_bit(g_a, order_a, step)
        g_b = scatter_dp_bit(g_b, order_b, step)
    pieces = to_pieces(dx, part, size, piece)
    in_grad = out_grad.astype(f32) + pieces.astype(f32)
    g_front = scatter_seq(jnp.concatenate([g_a, g_b], axis=2))
    dsmall = sum_bits(dsmall, "dp", order_a[:0:-1])
    dsmall = sum_bits(after(dsmall, pieces), "dp", order_a[:1])
    slab_wide = -(-max(3 * lanes, seq_extent * max(conv_own, own_rows, gate_own)) // lanes) * lanes
    slab = [
        padded(
            lax.dynamic_slice(
                dsmall, (at, group * seq_extent * count), (rows, seq_extent * count)
            ),
            rows,
            slab_wide,
        )
        for at, rows, count in (
            (0, tap_rows, conv_own),
            (tap_rows, 1, own_rows),
            (tap_rows + 1, 1, gate_own),
        )
    ]
    dsmall = jnp.concatenate(slab + [dsmall[tap_rows + 2 :, :slab_wide]])
    sums = [dsmall]
    for distance in range(1, seq_extent):
        route = [(i, (i + distance) % seq_extent) for i in range(seq_extent)]
        sums.append(lax.ppermute(dsmall, "seq", route))

    states = (
        (norm_gain[None, :], norm_first[None, :], norm_second[None, :]),
        (in_weight, in_first, in_second),
        (conv_params, conv_first, conv_second),
        (gate_gain[None, :], gate_first[None, :], gate_second[None, :]),
        (out_weight, out_first, out_second),
        (head_params, head_first, head_second),
    )
    new = adam(rates, sums, g_rest, g_front, states, heads, taps)
    new = [array[0] if array.shape[0] == 1 else array for array in new]
    return (layer_out, in_grad, *new)


def solution(mesh):
    in_specs = (
        P("dp", "seq", None),
        P("dp", "seq", None),
        P(("dp", "seq")),
        P(("dp", "seq"), None),
        P(None, ("dp", "seq")),
        P(("dp", "seq")),
        P(("dp", "seq"), None),
        P(),
        P(("dp", "seq")),
        P(("dp", "seq")),
        P(("dp", "seq"), None),
        P(("dp", "seq"), None),
        P(None, ("dp", "seq")),
        P(None, ("dp", "seq")),
        P(("dp", "seq")),
        P(("dp", "seq")),
        P(("dp", "seq"), None),
        P(("dp", "seq"), None),
        P(),
        P(),
        P(),
        P(),
    )
    out_specs = (
        P("dp", "seq", None),
        P("dp", "seq", None),
        P(("dp", "seq")),
        P(("dp", "seq")),
        P(("dp", "seq")),
        P(("dp", "seq"), None),
        P(("dp", "seq"), None),
        P(("dp", "seq"), None),
        P(None, ("dp", "seq")),
        P(None, ("dp", "seq")),
        P(None, ("dp", "seq")),
        P(("dp", "seq")),
        P(("dp", "seq")),
        P(("dp", "seq")),
        P(("dp", "seq"), None),
        P(("dp", "seq"), None),
        P(("dp", "seq"), None),
        P(),
        P(),
        P(),
        P(("dp", "seq"), None),
        P(("dp", "seq"), None),
    )
    return jax.shard_map(local, mesh=mesh, in_specs=in_specs, out_specs=out_specs, check_vma=False)
```

```python
import math
from functools import partial

import jax
import jax.numpy as jnp
import numpy as np
from jax import lax
from jax.experimental import pallas as pl
from jax.experimental.pallas import tpu as pltpu
from jax.sharding import PartitionSpec as P

norm_eps = 1e-05
adam_eps = 1e-08
log2e = math.log2(math.e)
lanes = 128
vmem_bytes = 56 * 1024 * 1024
f32 = jnp.float32
bf16 = jnp.bfloat16


def dot(left, right, left_dim=1, right_dim=0):
    return lax.dot_general(
        left, right, (((left_dim,), (right_dim,)), ((), ())), preferred_element_type=f32
    )


def halves(value):
    high = value.astype(bf16)
    return high, (value - high.astype(f32)).astype(bf16)


def sigmoid(value):
    return 0.5 * jnp.tanh(0.5 * value) + 0.5


def column(ref_value, at, width):
    return jnp.broadcast_to(ref_value[:, at : at + 1], (ref_value.shape[0], width))


def pair_columns(value, pair, low_lane):
    rows = value.shape[0]
    first = column(value, 2 * pair, lanes)
    second = column(value, 2 * pair + 1, lanes)
    return jnp.where(low_lane, first, second), first, second


def tri_sum(mask, value, head_lane):
    high = value.astype(bf16).astype(f32)
    rest = value - high
    mid = rest.astype(bf16).astype(f32)
    low = rest - mid
    packed = high + pltpu.roll(mid, 32, 1) + pltpu.roll(low, 64, 1)
    summed = dot(mask, packed.astype(bf16))
    total = summed + pltpu.roll(summed, lanes - 32, 1) + pltpu.roll(summed, lanes - 64, 1)
    return jnp.where(head_lane, total, 0.0)


def conv_chunk(ext_ref, conv_ref, at, length, taps):
    summed = conv_ref[taps : taps + 1, at : at + lanes]
    base = 8 - (taps - 1)
    for tap in range(taps):
        summed = (
            summed
            + conv_ref[tap : tap + 1, at : at + lanes]
            * ext_ref[at // lanes, base + tap : base + tap + length, :]
        )
    return summed


def put_columns(ext_ref, rows, values, chunk):
    for at in range(0, values.shape[1], lanes):
        ext_ref[chunk + at // lanes, rows, :] = values[:, at : at + lanes]


def step_sizes(dt_raw, head_ref, head_lane):
    shifted = dt_raw + head_ref[0:1, :]
    steps = jnp.maximum(shifted, 0.0) + jnp.log1p(jnp.exp(-jnp.abs(shifted)))
    return jnp.where(head_lane, steps, 0.0), shifted


def fetch_weight(core_ref, own_ref, other_ref, whole_ref, sems):
    blocks, rows, _ = own_ref.shape
    core = core_ref[0]
    copies = []
    for block in range(blocks):
        for which, source in ((core, own_ref), (1 - core, other_ref)):
            at = pl.multiple_of((2 * block + which) * rows, rows)
            copies.append(
                pltpu.make_async_copy(
                    source.at[block], whole_ref.at[pl.ds(at, rows)], sems.at[len(copies)]
                )
            )
    for copy in copies:
        copy.start()
    return copies


def hand_out(core, total_ref, send_ref, keep_ref):
    blocks, rows, _ = send_ref.shape
    for block in range(blocks):
        at = pl.multiple_of((2 * block + 1 - core) * rows, rows)
        send_ref[block] = total_ref[pl.ds(at, rows), :].astype(bf16)
        at = pl.multiple_of((2 * block + core) * rows, rows)
        keep_ref[block] = total_ref[pl.ds(at, rows), :]


def add_product(total_ref, left_ref, right):
    for at in range(0, total_ref.shape[0], 2 * lanes):
        here = slice(at, at + 2 * lanes)
        total_ref[here, :] += dot(left_ref[:, here], right, 0, 0)


def mixer_forward_kernel(
    core_ref,
    x_ref,
    edge_ref,
    wa_own,
    wa_other,
    wb_own,
    wb_other,
    conv_ref,
    head_ref,
    skip_ref,
    start_ref,
    before_ref,
    *refs,
    heads,
    inner,
    taps,
    grouped,
    resumed,
):
    (
        normed_ref,
        ext_ref,
        dtr_ref,
        cum_ref,
        y_ref,
        sin_ref,
        end_ref,
        after_ref,
        tail_ref,
        state_ref,
        carried_ref,
        weighted_ref,
        wa_ref,
        wb_ref,
        wa_sems,
        wb_sems,
    ) = refs[6:] if resumed else refs
    block = pl.program_id(1)
    length, width = x_ref.shape

    @pl.when(jnp.logical_and(pl.program_id(0) == 0, block == 0))
    def _():
        copies = fetch_weight(core_ref, wa_own, wa_other, wa_ref, wa_sems)
        copies += fetch_weight(core_ref, wb_own, wb_other, wb_ref, wb_sems)
        for copy in copies:
            copy.wait()

    half = length // 2
    wide_a = wa_ref.shape[1]
    conv_dim = conv_ref.shape[1]
    state_dim = (conv_dim - inner) // 2

    def norm_of(rows):
        rows = rows.astype(f32)
        scale = lax.rsqrt(jnp.mean(rows * rows, axis=-1, keepdims=True) + norm_eps)
        return (rows * scale * conv_ref[taps + 1 : taps + 2, :width]).astype(bf16)

    @pl.when(block == 0)
    def _():
        if resumed:
            state_ref[...] = start_ref[...]
            tail_ref[...] = before_ref[...]
        elif grouped:
            state_ref[...] = start_ref[...]
            edge = norm_of(edge_ref[...])
            put_columns(tail_ref, slice(0, 8), dot(edge, wa_ref[...]), 0)
            edge_b = dot(edge, wb_ref[...])[:, : conv_dim - wide_a]
            put_columns(tail_ref, slice(0, 8), edge_b, wide_a // lanes)
        else:
            state_ref[...] = jnp.zeros_like(state_ref)
            tail_ref[...] = jnp.zeros_like(tail_ref)

    normed = norm_of(x_ref[...])
    normed_ref[...] = normed
    ext_ref[:, 0:8, :] = tail_ref[...]
    own_rows = slice(8, 8 + length)
    for at in range(0, wide_a, 2 * lanes):
        product = dot(normed, wa_ref[:, at : at + 2 * lanes])
        put_columns(ext_ref, own_rows, product, at // lanes)
    second = dot(normed, wb_ref[...])
    put_columns(ext_ref, own_rows, second[:, : conv_dim - wide_a], wide_a // lanes)
    dt_raw = second[:, conv_dim - wide_a :]
    tail_ref[...] = ext_ref[:, length : length + 8, :]

    lane = lax.broadcasted_iota(jnp.int32, (length, lanes), 1)
    low_lane = lane < lanes // 2
    head_lane = lane < heads
    dtr_ref[...] = dt_raw
    steps, _ = step_sizes(dt_raw, head_ref, head_lane)
    log_decay = steps * (-log2e * jnp.exp(head_ref[1:2, :]))
    row = lax.broadcasted_iota(jnp.int32, (length, length), 0)
    col = lax.broadcasted_iota(jnp.int32, (length, length), 1)
    cum = tri_sum((row >= col).astype(bf16), log_decay, head_lane)
    cum_ref[...] = cum
    cum_rows = cum.T

    def mixed_chunk(at):
        summed = conv_chunk(ext_ref, conv_ref, at, length, taps)
        return summed * sigmoid(summed)

    keys = jnp.concatenate(
        [mixed_chunk(inner + at) for at in range(0, state_dim, lanes)], axis=1
    ).astype(bf16)
    queries = jnp.concatenate(
        [mixed_chunk(inner + state_dim + at) for at in range(0, state_dim, lanes)], axis=1
    ).astype(bf16)
    state_low = state_ref[...].astype(bf16)
    sin_ref[...] = state_low
    carried_ref[...] = dot(queries, state_low)
    square = (half, half)
    diag = lax.broadcasted_iota(jnp.int32, square, 0) >= lax.broadcasted_iota(
        jnp.int32, square, 1
    )
    scores_00 = jnp.where(diag, dot(queries[:half], keys[:half], 1, 1), 0.0)
    scores_10 = dot(queries[half:], keys[:half], 1, 1)
    scores_11 = jnp.where(diag, dot(queries[half:], keys[half:], 1, 1), 0.0)
    for pair in range(heads // 2):
        at = pair * lanes
        values = mixed_chunk(at)
        cum_rep, cum_0, cum_1 = pair_columns(cum, pair, low_lane)
        dt_rep, _, _ = pair_columns(steps, pair, low_lane)
        stepped = values * dt_rep
        last = cum_rep[length - 1 : length, :]
        weighted_ref[:, at : at + lanes] = (stepped * jnp.exp2(last - cum_rep)).astype(bf16)
        top = None
        bottom = None
        for which, cum_col in ((0, cum_0), (1, cum_1)):
            own = jnp.where(low_lane if which == 0 else jnp.logical_not(low_lane), stepped, 0.0)
            own = own.astype(bf16)
            head = 2 * pair + which
            early = cum_rows[head : head + 1, :half]
            late = cum_rows[head : head + 1, half:]
            mix_00 = jnp.exp2(jnp.minimum(cum_col[:half] - early, 0.0)) * scores_00
            mix_10 = jnp.exp2(cum_col[half:] - early) * scores_10
            mix_11 = jnp.exp2(jnp.minimum(cum_col[half:] - late, 0.0)) * scores_11
            part_top = dot(mix_00.astype(bf16), own[:half])
            part_bottom = dot(
                jnp.concatenate([mix_10.astype(bf16), mix_11.astype(bf16)], axis=1), own
            )
            top = part_top if top is None else top + part_top
            bottom = part_bottom if bottom is None else bottom + part_bottom
        rest = (
            jnp.exp2(cum_rep) * carried_ref[:, at : at + lanes]
            + skip_ref[0:1, at : at + lanes] * values
        )
        y_ref[0:half, at : at + lanes] = top + rest[:half]
        y_ref[half:length, at : at + lanes] = bottom + rest[half:]
        state_ref[:, at : at + lanes] = jnp.exp2(last) * state_ref[:, at : at + lanes]

    state_ref[...] += dot(keys, weighted_ref[...], 0, 0)

    @pl.when(block == pl.num_programs(1) - 1)
    def _():
        end_ref[...] = state_ref[...]
        after_ref[...] = tail_ref[...]


def gate_kernel(
    core_ref,
    normed_ref,
    x_ref,
    cot_a_ref,
    cot_b_ref,
    y_ref,
    wg_own,
    wg_other,
    wo_own,
    wo_other,
    small_ref,
    out_ref,
    dy_ref,
    dgate_ref,
    dgain_ref,
    out_send,
    out_keep,
    gate_send,
    gate_keep,
    gate_ref,
    dno_ref,
    low_ref,
    cot_ref,
    out_sum,
    gate_sum,
    wg_ref,
    wo_ref,
    wg_sems,
    wo_sems,
    *,
    gain_row,
):
    length, inner = y_ref.shape
    first = jnp.logical_and(pl.program_id(0) == 0, pl.program_id(1) == 0)

    @pl.when(first)
    def _():
        copies = fetch_weight(core_ref, wg_own, wg_other, wg_ref, wg_sems)
        copies += fetch_weight(core_ref, wo_own, wo_other, wo_ref, wo_sems)
        dgain_ref[...] = jnp.zeros_like(dgain_ref)
        out_sum[...] = jnp.zeros_like(out_sum)
        gate_sum[...] = jnp.zeros_like(gate_sum)
        for copy in copies:
            copy.wait()

    gate_ref[...] = dot(normed_ref[...], wg_ref[...])
    cot_ref[:, : cot_a_ref.shape[1]] = cot_a_ref[...]
    cot_ref[:, cot_a_ref.shape[1] :] = cot_b_ref[...]
    dno_ref[...] = dot(cot_ref[...], wo_ref[...], 1, 1)
    squares = jnp.zeros((length, lanes), f32)
    crosses = jnp.zeros((length, lanes), f32)
    for at in range(0, inner, lanes):
        here = slice(at, at + lanes)
        gate = gate_ref[:, here]
        gated = y_ref[:, here] * (gate * sigmoid(gate))
        squares = squares + gated * gated
        crosses = crosses + gated * (small_ref[gain_row : gain_row + 1, here] * dno_ref[:, here])
    scale = lax.rsqrt(jnp.sum(squares, axis=1, keepdims=True) * (1.0 / inner) + norm_eps)
    cross = scale * scale * scale * (jnp.sum(crosses, axis=1, keepdims=True) * (1.0 / inner))
    scale_b = jnp.broadcast_to(scale, (length, lanes))
    cross_b = jnp.broadcast_to(cross, (length, lanes))
    for at in range(0, inner, lanes):
        here = slice(at, at + lanes)
        gate = gate_ref[:, here]
        mixed_out = y_ref[:, here]
        sig = sigmoid(gate)
        silu = gate * sig
        gated = mixed_out * silu
        scaled = gated * scale_b
        d_out = dno_ref[:, here]
        low_ref[:, here] = (scaled * small_ref[gain_row : gain_row + 1, here]).astype(bf16)
        dgain_ref[0:1, here] += jnp.sum(scaled * d_out, axis=0, keepdims=True)
        d_gated = scale_b * (small_ref[gain_row : gain_row + 1, here] * d_out) - gated * cross_b
        dy_ref[:, here] = (d_gated * silu).astype(bf16)
        dgate_ref[:, here] = (d_gated * mixed_out * (sig * (1.0 + gate * (1.0 - sig)))).astype(
            bf16
        )
    out_ref[...] = (x_ref[...].astype(f32) + dot(low_ref[...], wo_ref[...])).astype(bf16)
    add_product(out_sum, low_ref, cot_ref[...])
    add_product(gate_sum, normed_ref, dgate_ref[...])
    last = jnp.logical_and(
        pl.program_id(0) == pl.num_programs(0) - 1, pl.program_id(1) == pl.num_programs(1) - 1
    )

    @pl.when(last)
    def _():
        hand_out(core_ref[0], out_sum, out_send, out_keep)
        hand_out(core_ref[0], gate_sum, gate_send, gate_keep)


def mixer_backward_kernel(
    ext_ref,
    dtr_ref,
    cum_ref,
    y_ref,
    sin_ref,
    dy_ref,
    conv_ref,
    head_ref,
    skip_ref,
    sum_ref,
    start_ref,
    next_ref,
    small_in_ref,
    dgain_ref,
    _,
    dproj_ref,
    dconv_ref,
    end_ref,
    lead_ref,
    grad_ref,
    dsx_ref,
    dwv_ref,
    dye_ref,
    weighted_ref,
    zhigh_ref,
    zlow_ref,
    direct_ref,
    rows_ref,
    *,
    heads,
    inner,
    taps,
    fresh,
):
    step = pl.program_id(1)
    length = dy_ref.shape[0]
    half = length // 2
    conv_dim = conv_ref.shape[1]
    state_dim = (conv_dim - inner) // 2
    first = jnp.logical_and(pl.program_id(0) == 0, step == 0)

    @pl.when(first)
    def _():
        if small_in_ref.shape == dconv_ref.shape:
            dconv_ref[...] = small_in_ref[...]
        else:
            dconv_ref[...] = jnp.zeros_like(dconv_ref)
            dconv_ref[taps + 2 : taps + 3, :inner] = dgain_ref[0:1, :]
        rows_ref[...] = jnp.zeros_like(rows_ref)

    @pl.when(step == 0)
    def _():
        if fresh:
            grad_ref[...] = jnp.zeros_like(grad_ref)
            dsx_ref[:, length : length + 8, :] = jnp.zeros((conv_dim // lanes, 8, lanes), f32)
        else:
            grad_ref[...] = start_ref[...]
            dsx_ref[:, length : length + 8, :] = next_ref[...]

    @pl.when(step > 0)
    def _():
        dsx_ref[:, length : length + 8, :] = dsx_ref[:, 0:8, :]

    lane = lax.broadcasted_iota(jnp.int32, (length, lanes), 1)
    low_lane = lane < lanes // 2
    head_lane = lane < heads
    steps, shifted = step_sizes(dtr_ref[...], head_ref, head_lane)
    cum = cum_ref[...]
    cum_rows = cum.T

    def slope_chunk(at):
        summed = conv_chunk(ext_ref, conv_ref, at, length, taps)
        sig = sigmoid(summed)
        return summed * sig, sig * (1.0 + summed * (1.0 - sig))

    def put_grad(at, d_summed):
        here = slice(at, at + lanes)
        chunk = at // lanes
        dsx_ref[chunk, 0:length, :] = d_summed
        total = None
        for tap in range(taps):
            base = 8 - (taps - 1) + tap
            dconv_ref[tap : tap + 1, here] += jnp.sum(
                d_summed * ext_ref[chunk, base : base + length, :], axis=0, keepdims=True
            )
            back = taps - 1 - tap
            term = conv_ref[tap : tap + 1, here] * dsx_ref[chunk, back : back + length, :]
            total = term if total is None else total + term
        dconv_ref[taps : taps + 1, here] += jnp.sum(d_summed, axis=0, keepdims=True)
        dproj_ref[:, here] = total.astype(bf16)

    parts = [slope_chunk(inner + at) for at in range(0, 2 * state_dim, lanes)]
    count = state_dim // lanes
    keys = jnp.concatenate([part[0] for part in parts[:count]], axis=1).astype(bf16)
    queries = jnp.concatenate([part[0] for part in parts[count:]], axis=1).astype(bf16)
    grad_low = grad_ref[...].astype(bf16)
    dwv_ref[...] = dot(keys, grad_low)
    square = (half, half)
    diag = lax.broadcasted_iota(jnp.int32, square, 0) <= lax.broadcasted_iota(
        jnp.int32, square, 1
    )
    scores_00 = jnp.where(diag, dot(keys[:half], queries[:half], 1, 1), 0.0)
    scores_01 = dot(keys[:half], queries[half:], 1, 1)
    scores_11 = jnp.where(diag, dot(keys[half:], queries[half:], 1, 1), 0.0)
    ds_00 = jnp.zeros(square, f32)
    ds_01 = jnp.zeros(square, f32)
    ds_11 = jnp.zeros(square, f32)
    for pair in range(heads // 2):
        at = pair * lanes
        here = slice(at, at + lanes)
        values, slope = slope_chunk(at)
        cum_rep, cum_0, cum_1 = pair_columns(cum, pair, low_lane)
        dt_rep, _, _ = pair_columns(steps, pair, low_lane)
        stepped = (values * dt_rep).astype(bf16)
        stepped_f = stepped.astype(f32)
        last = cum_rep[length - 1 : length, :]
        tail = jnp.exp2(last - cum_rep)
        d_y = dy_ref[:, here]
        d_yf = d_y.astype(f32)
        d_y_t = d_yf.T.astype(bf16)
        dye_ref[:, here] = (d_yf * jnp.exp2(cum_rep)).astype(bf16)
        top = None
        bottom = None
        for which, cum_col in ((0, cum_0), (1, cum_1)):
            own_lane = low_lane if which == 0 else jnp.logical_not(low_lane)
            own_dy = jnp.where(own_lane, d_yf, 0.0).astype(bf16)
            own_x = jnp.where(own_lane, stepped_f, 0.0).astype(bf16)
            head = 2 * pair + which
            early = cum_rows[head : head + 1, :half]
            late = cum_rows[head : head + 1, half:]
            decay_00 = jnp.exp2(jnp.minimum(early - cum_col[:half], 0.0))
            decay_01 = jnp.exp2(late - cum_col[:half])
            decay_11 = jnp.exp2(jnp.minimum(late - cum_col[half:], 0.0))
            mix_0 = jnp.concatenate(
                [(decay_00 * scores_00).astype(bf16), (decay_01 * scores_01).astype(bf16)], axis=1
            )
            mix_1 = (decay_11 * scores_11).astype(bf16)
            part_top = dot(mix_0, own_dy)
            part_bottom = dot(mix_1, own_dy[half:])
            top = part_top if top is None else top + part_top
            bottom = part_bottom if bottom is None else bottom + part_bottom
            d_mix_0 = dot(own_x[:half], d_y_t)
            d_mix_1 = dot(own_x[half:], d_y_t[:, half:])
            ds_00 = ds_00 + decay_00 * d_mix_0[:, :half]
            ds_01 = ds_01 + decay_01 * d_mix_0[:, half:]
            ds_11 = ds_11 + decay_11 * d_mix_1
        d_diag = jnp.concatenate([top, bottom], axis=0)
        weighted = (stepped_f * tail).astype(bf16)
        weighted_ref[:, here] = weighted
        d_weighted = dwv_ref[:, here]
        through = weighted.astype(f32) * d_weighted
        d_stepped = d_diag + tail * d_weighted
        skip = skip_ref[0:1, here]
        z = d_yf * (y_ref[:, here] - skip * values) - stepped_f * d_diag - through
        z_high, z_low = halves(z)
        zhigh_ref[:, here] = z_high
        zlow_ref[:, here] = z_low
        direct_ref[:, here] = (d_stepped * values).astype(bf16)
        total_decay = jnp.exp2(last)
        rows_ref[0:1, here] = jnp.sum(through, axis=0, keepdims=True) + total_decay * jnp.sum(
            grad_ref[:, here] * sin_ref[:, here].astype(f32), axis=0, keepdims=True
        )
        rows_ref[1:2, here] = jnp.sum(d_yf * values, axis=0, keepdims=True)
        put_grad(at, (d_stepped * dt_rep + skip * d_yf) * slope)
        grad_ref[:, here] = total_decay * grad_ref[:, here]

    grad_ref[...] += dot(queries, dye_ref[...], 0, 0)
    ds_00 = jnp.where(diag, ds_00, 0.0).astype(bf16)
    ds_11 = jnp.where(diag, ds_11, 0.0).astype(bf16)
    ds_01 = ds_01.astype(bf16)
    d_queries = dot(dye_ref[...], sin_ref[...], 1, 1)
    d_keys = dot(weighted_ref[...], grad_low, 1, 1)
    d_queries = d_queries + jnp.concatenate(
        [
            dot(ds_00, keys[:half], 0, 0),
            dot(ds_01, keys[:half], 0, 0) + dot(ds_11, keys[half:], 0, 0),
        ],
        axis=0,
    )
    d_keys = d_keys + jnp.concatenate(
        [
            dot(ds_00, queries[:half]) + dot(ds_01, queries[half:]),
            dot(ds_11, queries[half:]),
        ],
        axis=0,
    )
    for at in range(0, state_dim, lanes):
        put_grad(inner + at, d_keys[:, at : at + lanes] * parts[at // lanes][1])
        put_grad(
            inner + state_dim + at,
            d_queries[:, at : at + lanes] * parts[count + at // lanes][1],
        )
    summing = sum_ref[...]
    rows_high, rows_low = halves(rows_ref[...])
    row_sums = dot(rows_high, summing) + dot(rows_low, summing)
    d_cum = dot(zhigh_ref[...], summing) + dot(zlow_ref[...], summing)
    at_last = lax.broadcasted_iota(jnp.int32, (length, lanes), 0) == length - 1
    d_cum = d_cum + jnp.where(at_last, row_sums[0:1, :], 0.0)
    row = lax.broadcasted_iota(jnp.int32, (length, length), 0)
    col = lax.broadcasted_iota(jnp.int32, (length, length), 1)
    d_log = tri_sum((row <= col).astype(bf16), d_cum, head_lane)
    rate = jnp.exp(head_ref[1:2, :])
    d_steps = dot(direct_ref[...], summing) - rate * d_log
    d_raw = jnp.where(head_lane, d_steps * sigmoid(shifted), 0.0)
    dproj_ref[:, conv_dim : conv_dim + lanes] = d_raw.astype(bf16)
    head_row = slice(taps + 3, taps + 4)
    dconv_ref[head_row, :lanes] += jnp.sum(d_raw, axis=0, keepdims=True)
    dconv_ref[head_row, lanes : 2 * lanes] += jnp.sum(d_log * steps, axis=0, keepdims=True) * (
        -rate
    )
    dconv_ref[head_row, 2 * lanes : 3 * lanes] += row_sums[1:2, :]

    @pl.when(step == pl.num_programs(1) - 1)
    def _():
        end_ref[...] = grad_ref[...]
        lead_ref[...] = dsx_ref[:, 0:8, :]


def input_grad_kernel(
    core_ref,
    x_ref,
    dgate_ref,
    dproj_ref,
    small_ref,
    dsmall_in_ref,
    wg_own,
    wg_other,
    wa_own,
    wa_other,
    wb_own,
    wb_other,
    dx_ref,
    dsmall_ref,
    a_send,
    a_keep,
    b_send,
    b_keep,
    normed_ref,
    a_sum,
    b_sum,
    wg_ref,
    wa_ref,
    wb_ref,
    wg_sems,
    wa_sems,
    wb_sems,
    *,
    gain_row,
):
    first = jnp.logical_and(pl.program_id(0) == 0, pl.program_id(1) == 0)
    width = x_ref.shape[1]

    @pl.when(first)
    def _():
        copies = fetch_weight(core_ref, wg_own, wg_other, wg_ref, wg_sems)
        copies += fetch_weight(core_ref, wa_own, wa_other, wa_ref, wa_sems)
        copies += fetch_weight(core_ref, wb_own, wb_other, wb_ref, wb_sems)
        dsmall_ref[...] = dsmall_in_ref[...]
        a_sum[...] = jnp.zeros_like(a_sum)
        b_sum[...] = jnp.zeros_like(b_sum)
        for copy in copies:
            copy.wait()

    wide_a = wa_ref.shape[1]
    d_normed = (
        dot(dgate_ref[...], wg_ref[...], 1, 1)
        + dot(dproj_ref[:, :wide_a], wa_ref[...], 1, 1)
        + dot(dproj_ref[:, wide_a:], wb_ref[...], 1, 1)
    )
    rows = x_ref[...].astype(f32)
    scale = lax.rsqrt(jnp.mean(rows * rows, axis=-1, keepdims=True) + norm_eps)
    scaled = rows * scale
    dsmall_ref[gain_row : gain_row + 1, :width] += jnp.sum(
        scaled * d_normed, axis=0, keepdims=True
    )
    gain = small_ref[gain_row : gain_row + 1, :width]
    normed_ref[...] = (scaled * gain).astype(bf16)
    add_product(a_sum, normed_ref, dproj_ref[:, :wide_a])
    add_product(b_sum, normed_ref, dproj_ref[:, wide_a:])
    inner_grad = gain * d_normed
    cross = jnp.mean(scaled * inner_grad, axis=-1, keepdims=True)
    dx_ref[...] = (scale * (inner_grad - scaled * cross)).astype(bf16)
    last = jnp.logical_and(
        pl.program_id(0) == pl.num_programs(0) - 1, pl.program_id(1) == pl.num_programs(1) - 1
    )

    @pl.when(last)
    def _():
        hand_out(core_ref[0], a_sum, a_send, a_keep)
        hand_out(core_ref[0], b_sum, b_send, b_keep)


def adam_kernel(
    rates_ref,
    *refs,
    heads,
    taps,
    at_refs,
    arrivals,
):
    sum_refs, refs = refs[:arrivals], refs[arrivals:]
    rest_refs, front_refs, refs = refs[:arrivals], refs[arrivals : 2 * arrivals], refs[2 * arrivals :]
    ins, outs = refs[:18], refs[18:]
    learn_rate, decay_rate = rates_ref[0], rates_ref[3]
    beta_one, beta_two = rates_ref[1], rates_ref[2]
    first_scale, second_scale = rates_ref[4], rates_ref[5]

    def update(which, grad, index):
        master, first, second = (ref[index] for ref in ins[3 * which : 3 * which + 3])
        new_first = beta_one * first + (1.0 - beta_one) * grad
        new_second = beta_two * second + (1.0 - beta_two) * grad * grad
        change = -learn_rate * (
            (new_first * first_scale) / (jnp.sqrt(new_second * second_scale) + adam_eps)
            + decay_rate * master
        )
        where = at_refs[which]
        outs[where][index] = master + change if which in (1, 4) else change
        outs[where + 1][index] = new_first
        outs[where + 2][index] = new_second
        if which in (1, 4):
            outs[-2 if which == 1 else -1][index] = (master + change).astype(bf16)

    everything = (slice(None), slice(None))
    rest, front = rest_refs[0][...], front_refs[0][...]
    inner = rest.shape[1] // 2
    for rest_ref, front_ref in zip(rest_refs[1:], front_refs[1:]):
        rest = rest + rest_ref[...].astype(f32)
        front = front + front_ref[...].astype(f32)
    proj = ins[3].shape[1]
    update(1, rest[:, :inner], (slice(None), slice(0, inner)))
    update(1, front[:, : proj - inner], (slice(None), slice(inner, proj)))
    rows = rest.shape[0]
    half = inner // 2
    update(4, rest[:, inner : inner + half], (slice(0, rows), slice(None)))
    update(4, rest[:, inner + half :], (slice(rows, 2 * rows), slice(None)))

    place = rates_ref[7].astype(jnp.int32)
    terms = [ref[...] for ref in sum_refs]
    sums = terms[0]
    for term in terms[1:]:
        sums = sums + term

    def own(at, count):
        wide = sums.shape[1]
        shift = lax.rem(wide - place * count, wide)
        return pltpu.roll(sums, shift, 1)[at, :count]

    update(0, own(slice(taps + 1, taps + 2), ins[0].shape[1]), everything)
    update(2, own(slice(0, taps + 1), ins[6].shape[1]), everything)
    update(3, own(slice(taps + 2, taps + 3), ins[9].shape[1]), everything)
    sums = jnp.zeros_like(sums)
    for source in range(arrivals):
        distance = lax.rem(place + arrivals - source, arrivals)
        term = terms[0]
        for which in range(1, arrivals):
            term = jnp.where(distance == which, terms[which], term)
        sums = sums + term
    head_row = slice(taps + 3, taps + 4)
    for row in range(3):
        grad = sums[head_row, row * lanes : row * lanes + heads]
        update(5, grad, (slice(row, row + 1), slice(None)))


def whole(shape):
    return pl.BlockSpec(shape, lambda p, b: (0,) * len(shape))


def by_block(shape, size, back=False):
    if back:
        return pl.BlockSpec(shape, lambda p, s: (p * size + (size - 1 - s), 0))
    return pl.BlockSpec(shape, lambda p, b: (p * size + b, 0))


def by_part(shape):
    return pl.BlockSpec(shape, lambda p, b: (p, 0))


def params():
    return pltpu.CompilerParams(
        dimension_semantics=("arbitrary", "arbitrary"), vmem_limit_bytes=vmem_bytes
    )


def cost(flops, moved, powers):
    return pl.CostEstimate(flops=flops, bytes_accessed=moved, transcendentals=powers)


ANY = pl.BlockSpec(memory_space=pl.ANY)
SMEM = pl.BlockSpec(memory_space=pltpu.SMEM)


def weight_scratch(*weights):
    wholes = [
        pltpu.VMEM((2 * own.shape[0] * own.shape[1], own.shape[2]), bf16) for own, _ in weights
    ]
    return wholes + [pltpu.SemaphoreType.DMA((2 * own.shape[0],)) for own, _ in weights]


def handed_out(rows, columns, blocks):
    shape = (blocks, rows // (2 * blocks), columns)
    return [jax.ShapeDtypeStruct(shape, bf16), jax.ShapeDtypeStruct(shape, f32)]


def mixer_forward(dims, core, tokens, wa, wb, small, head, skip, edge, start, grouped, kept, blocks):
    part, size, piece, width, inner, heads, taps = dims
    first, count = blocks
    conv_dim = small.shape[1]
    state_dim = (conv_dim - inner) // 2
    all_blocks = part * size
    rows = all_blocks * piece
    ext_rows = piece + 8
    chunks = conv_dim // lanes
    resumed = kept is not None

    def by_block(shape):
        return pl.BlockSpec(shape, lambda p, b: (p * size + first + b, 0))

    tail_block = pl.BlockSpec((chunks, 8, lanes), lambda p, b: (p, 0, 0))
    before = core
    if resumed:
        *arrays, start, before = kept
    else:
        arrays = []
    return pl.pallas_call(
        partial(
            mixer_forward_kernel,
            heads=heads,
            inner=inner,
            taps=taps,
            grouped=grouped,
            resumed=resumed,
        ),
        grid=(part, count),
        in_specs=[
            SMEM,
            by_block((piece, width)),
            by_part((8, width)) if grouped else ANY,
            ANY,
            ANY,
            ANY,
            ANY,
            whole(small.shape),
            whole(head.shape),
            whole(skip.shape),
            by_part((state_dim, inner)) if grouped or resumed else ANY,
            tail_block if resumed else ANY,
        ]
        + [ANY] * len(arrays),
        out_specs=[
            by_block((piece, width)),
            pl.BlockSpec((chunks, ext_rows, lanes), lambda p, b: (p * size + first + b, 0, 0)),
            by_block((piece, lanes)),
            by_block((piece, lanes)),
            by_block((piece, inner)),
            by_block((state_dim, inner)),
            by_part((state_dim, inner)),
            tail_block,
        ],
        out_shape=[
            jax.ShapeDtypeStruct((rows, width), bf16),
            jax.ShapeDtypeStruct((all_blocks * chunks, ext_rows, lanes), f32),
            jax.ShapeDtypeStruct((rows, lanes), f32),
            jax.ShapeDtypeStruct((rows, lanes), f32),
            jax.ShapeDtypeStruct((rows, inner), f32),
            jax.ShapeDtypeStruct((all_blocks * state_dim, inner), bf16),
            jax.ShapeDtypeStruct((part * state_dim, inner), f32),
            jax.ShapeDtypeStruct((part * chunks, 8, lanes), f32),
        ],
        scratch_shapes=[
            pltpu.VMEM((chunks, 8, lanes), f32),
            pltpu.VMEM((state_dim, inner), f32),
            pltpu.VMEM((piece, inner), f32),
            pltpu.VMEM((piece, inner), bf16),
        ]
        + weight_scratch(wa, wb),
        input_output_aliases={12 + at: at for at in range(len(arrays))},
        compiler_params=params(),
        cost_estimate=cost(1, 1, 0),
    )(core, tokens, edge, *wa, *wb, small, head, skip, start, before, *arrays)


def gate_step(dims, core, normed, tokens, cots_b, y, wg, wo, small):
    part, size, piece, width, inner, heads, taps = dims
    rows = part * size * piece
    blocks = wo[0].shape[0]
    handed = handed_out(inner, width, blocks) + handed_out(width, inner, blocks)
    wide_b = cots_b.shape[1]
    at_a = width // (width - wide_b)
    return pl.pallas_call(
        partial(gate_kernel, gain_row=taps + 2),
        grid=(part, size),
        in_specs=[
            SMEM,
            by_block((piece, width), size),
            by_block((piece, width), size),
            pl.BlockSpec((piece, width - wide_b), lambda p, b: (p * size + b, at_a)),
            by_block((piece, wide_b), size),
            by_block((piece, inner), size),
            ANY,
            ANY,
            ANY,
            ANY,
            whole(small.shape),
        ],
        out_specs=[
            by_block((piece, width), size),
            by_block((piece, inner), size),
            by_block((piece, inner), size),
            whole((8, inner)),
        ]
        + [whole(array.shape) for array in handed],
        out_shape=[
            jax.ShapeDtypeStruct((rows, width), bf16),
            jax.ShapeDtypeStruct((rows, inner), bf16),
            jax.ShapeDtypeStruct((rows, inner), bf16),
            jax.ShapeDtypeStruct((8, inner), f32),
        ]
        + handed,
        scratch_shapes=[
            pltpu.VMEM((piece, inner), f32),
            pltpu.VMEM((piece, inner), f32),
            pltpu.VMEM((piece, inner), bf16),
            pltpu.VMEM((piece, width), bf16),
            pltpu.VMEM((inner, width), f32),
            pltpu.VMEM((width, inner), f32),
        ]
        + weight_scratch(wg, wo),
        compiler_params=params(),
        cost_estimate=cost(1, 1, 0),
    )(core, normed, tokens, tokens, cots_b, y, *wg, *wo, small)


def mixer_backward(dims, saved, consts, carry, blocks, fresh):
    part, size, piece, width, inner, heads, taps = dims
    first, count = blocks
    small, head, skip, summing, dgain = consts
    conv_dim = small.shape[1]
    state_dim = (conv_dim - inner) // 2
    ext_rows = piece + 8
    chunks = conv_dim // lanes
    wide = conv_dim + lanes
    dproj, dsmall, state, lead = carry
    lead_block = pl.BlockSpec((chunks, 8, lanes), lambda p, s: (p, 0, 0))

    def by_block(shape):
        return pl.BlockSpec(shape, lambda p, s: (p * size + (first + count - 1 - s), 0))

    return pl.pallas_call(
        partial(mixer_backward_kernel, heads=heads, inner=inner, taps=taps, fresh=fresh),
        grid=(part, count),
        in_specs=[
            pl.BlockSpec(
                (chunks, ext_rows, lanes), lambda p, s: (p * size + (first + count - 1 - s), 0, 0)
            ),
            by_block((piece, lanes)),
            by_block((piece, lanes)),
            by_block((piece, inner)),
            by_block((state_dim, inner)),
            by_block((piece, inner)),
            whole(small.shape),
            whole(head.shape),
            whole(skip.shape),
            whole(summing.shape),
            ANY if fresh else by_part((state_dim, inner)),
            ANY if fresh else lead_block,
            whole(dsmall.shape),
            whole(dgain.shape),
            ANY,
        ],
        out_specs=[
            by_block((piece, wide)),
            whole((8, conv_dim)),
            by_part((state_dim, inner)),
            lead_block,
        ],
        out_shape=[
            jax.ShapeDtypeStruct((part * size * piece, wide), bf16),
            jax.ShapeDtypeStruct((8, conv_dim), f32),
            jax.ShapeDtypeStruct((part * state_dim, inner), f32),
            jax.ShapeDtypeStruct((part * chunks, 8, lanes), f32),
        ],
        scratch_shapes=[
            pltpu.VMEM((state_dim, inner), f32),
            pltpu.VMEM((chunks, ext_rows, lanes), f32),
            pltpu.VMEM((piece, inner), f32),
            pltpu.VMEM((piece, inner), bf16),
            pltpu.VMEM((piece, inner), bf16),
            pltpu.VMEM((piece, inner), bf16),
            pltpu.VMEM((piece, inner), bf16),
            pltpu.VMEM((piece, inner), bf16),
            pltpu.VMEM((8, inner), f32),
        ],
        input_output_aliases={14: 0} if dproj.shape[0] == part * size * piece else {},
        compiler_params=params(),
        cost_estimate=cost(1, 1, 0),
    )(*saved, small, head, skip, summing, state, lead, dsmall, dgain, dproj)


def input_grad(dims, core, tokens, dgate, dproj, small, dsmall, wg, wa, wb):
    part, size, piece, width, inner, heads, taps = dims
    rows = part * size * piece
    blocks = wa[0].shape[0]
    wide_a, wide_b = wa[0].shape[2], wb[0].shape[2]
    handed = handed_out(width, wide_a, blocks) + handed_out(width, wide_b, blocks)
    return pl.pallas_call(
        partial(input_grad_kernel, gain_row=taps + 1),
        grid=(part, size),
        in_specs=[
            SMEM,
            by_block((piece, width), size),
            by_block((piece, inner), size),
            by_block((piece, dproj.shape[1]), size),
            whole(small.shape),
            whole(dsmall.shape),
            ANY,
            ANY,
            ANY,
            ANY,
            ANY,
            ANY,
        ],
        out_specs=[by_block((piece, width), size), whole(dsmall.shape)]
        + [whole(array.shape) for array in handed],
        out_shape=[
            jax.ShapeDtypeStruct((rows, width), bf16),
            jax.ShapeDtypeStruct(dsmall.shape, f32),
        ]
        + handed,
        scratch_shapes=[
            pltpu.VMEM((piece, width), bf16),
            pltpu.VMEM((width, wide_a), f32),
            pltpu.VMEM((width, wide_b), f32),
        ]
        + weight_scratch(wg, wa, wb),
        compiler_params=params(),
        cost_estimate=cost(1, 1, 0),
    )(core, tokens, dgate, dproj, small, dsmall, *wg, *wa, *wb)


def adam(rates, sums, gate_grads, front_grads, states, heads, taps):
    outs = []
    at_refs = []
    for which, (master, first, second) in enumerate(states):
        at_refs.append(len(outs))
        outs += [jax.ShapeDtypeStruct(master.shape, f32)] * 3
    outs.append(jax.ShapeDtypeStruct(states[1][0].shape, bf16))
    outs.append(jax.ShapeDtypeStruct(states[4][0].shape, bf16))
    flat = [array for state in states for array in state]
    vmem = pl.BlockSpec(memory_space=pltpu.VMEM)
    return pl.pallas_call(
        partial(
            adam_kernel, heads=heads, taps=taps, at_refs=at_refs, arrivals=len(gate_grads)
        ),
        in_specs=[SMEM] + [vmem] * (3 * len(gate_grads) + len(flat)),
        out_specs=[vmem] * len(outs),
        out_shape=outs,
        compiler_params=pltpu.CompilerParams(vmem_limit_bytes=vmem_bytes),
        cost_estimate=cost(1, 1, 0),
    )(rates, *sums, *gate_grads, *front_grads, *flat)


def bit_count(extent):
    count = extent.bit_length() - 1
    if 1 << count != extent:
        raise ValueError(extent)
    return count


def swap(block, axis, bit):
    devices = range(lax.axis_size(axis))
    return lax.ppermute(block, axis, [(i, i ^ (1 << bit)) for i in devices])


def shifted_by(block, axis, distance):
    devices = range(lax.axis_size(axis))
    route = [(i, i + distance) for i in devices if i + distance in devices]
    return lax.ppermute(block, axis, route)


def pick(block, at, axis):
    return lax.dynamic_index_in_dim(block, at, axis, keepdims=False)


def gather_bit(block, axis, bit, at, *others):
    mine = (lax.axis_index(axis) >> bit) & 1
    other = swap(block, axis, bit)
    if others:
        other = after(other, *others)
    low = jnp.where(mine == 1, other, block)
    high = jnp.where(mine == 1, block, other)
    return jnp.stack([low, high], axis=at)


def gather_seq(shard, *others):
    block = shard
    for done, bit in enumerate(reversed(range(bit_count(lax.axis_size("seq"))))):
        block = gather_bit(block, "seq", bit, done, *(others if done == 0 else ()))
    return block.reshape((-1,) + shard.shape)


def dp_orders():
    bits = bit_count(lax.axis_size("dp"))
    return list(range(bits - 1, 0, -1)) + [0], list(range(1, bits)) + [0]


def gather_dp_bit(block, order, step, *others):
    at = sum(1 for b in order[:step] if b > order[step])
    return gather_bit(block, "dp", order[step], at, *others)


def give_half(block, axis, bit, at):
    mine = (lax.axis_index(axis) >> bit) & 1
    other = swap(pick(block, 1 - mine, at).astype(bf16), axis, bit)
    return pick(block, mine, at) + other.astype(f32)


def core_sums(send, keep):
    extent = lax.axis_size("seq")
    bits = bit_count(lax.axis_size("dp")) - 1
    shape = (2,) * bits + (extent, -1, send.shape[2])
    other = swap(send, "dp", 0)
    return keep.reshape(shape), other.reshape(shape)


def core_and_next(keep, other, order):
    bit = order[-2]
    at = sum(1 for b in order[:-2] if b > bit)
    mine = (lax.axis_index("dp") >> bit) & 1
    sent = pick(keep, 1 - mine, at) + pick(other, 1 - mine, at).astype(f32)
    arrived = swap(sent.astype(bf16), "dp", bit)
    return pick(keep, mine, at) + pick(other, mine, at).astype(f32), arrived


def scatter_dp_bit(block, order, step):
    bit = order[-1 - step]
    return give_half(block, "dp", bit, sum(1 for b in order[: len(order) - 1 - step] if b > bit))


def scatter_seq(block, *others):
    extent = lax.axis_size("seq")
    place = lax.axis_index("seq")
    arrivals = [pick(block, place, 0)]
    for distance in range(1, extent):
        sent = pick(block, lax.rem(place + distance, extent), 0).astype(bf16)
        if others and distance == extent - 1:
            sent = after(sent, *others)
        route = [(i, (i + distance) % extent) for i in range(extent)]
        arrivals.append(lax.ppermute(sent, "seq", route))
    return arrivals


def sum_bits(block, axis, bits):
    for bit in bits:
        block = block + swap(block, axis, bit)
    return block


def seq_groups(size):
    extent = lax.axis_size("seq")
    if size == extent:
        return None
    return [list(range(at, at + size)) for at in range(0, extent, size)]


def to_sequences(block, part, size):
    if size > 1:
        block = lax.all_to_all(
            block, "seq", 0, 0, axis_index_groups=seq_groups(size), tiled=True
        )
    piece, width = block.shape[1:]
    block = block.reshape(size, part, piece, width)
    if part > 1:
        block = block.transpose(1, 0, 2, 3)
    return block.reshape(-1, width)


def to_pieces(rows, part, size, piece):
    block = rows.reshape(part, size, piece, -1)
    if part > 1:
        block = block.transpose(1, 0, 2, 3)
    block = block.reshape(part * size, piece, -1)
    if size > 1:
        block = lax.all_to_all(
            block, "seq", 0, 0, axis_index_groups=seq_groups(size), tiled=True
        )
    return block


def after(value, *others):
    return lax.optimization_barrier((value,) + others)[0]


def padded(block, rows, columns):
    return jnp.pad(block, ((0, rows - block.shape[0]), (0, columns - block.shape[1])))


def summing_matrix(inner, heads):
    columns = np.zeros((inner, lanes), np.float32)
    columns[np.arange(inner), np.arange(inner) // (inner // heads)] = 1.0
    return jnp.asarray(columns, bf16)


def local(
    layer_in,
    out_grad,
    norm_gain,
    in_weight,
    conv_params,
    gate_gain,
    out_weight,
    head_params,
    norm_first,
    norm_second,
    in_first,
    in_second,
    conv_first,
    conv_second,
    gate_first,
    gate_second,
    out_first,
    out_second,
    head_first,
    head_second,
    step_count,
    hyper,
):
    seq_count, piece, width = layer_in.shape
    seq_extent = lax.axis_size("seq")
    me = lax.axis_index("dp") * seq_extent + lax.axis_index("seq")
    step_float = step_count[0].astype(f32)
    scales = 1.0 / (1.0 - hyper[1:3] ** step_float)
    place = lax.axis_index("seq")
    rates = jnp.concatenate([hyper, scales, jnp.stack([me.astype(f32), place.astype(f32)])])
    core = (lax.axis_index("dp") & 1).astype(jnp.int32)[None]
    owners = lax.axis_size("dp") * seq_extent
    size = math.gcd(seq_extent, seq_count)
    part = seq_count // size
    groups = seq_extent // size
    inner = out_weight.shape[0] * owners
    heads = head_params.shape[1]
    tap_rows, conv_own = conv_params.shape
    taps = tap_rows - 1
    conv_dim = conv_own * owners
    state_dim = (conv_dim - inner) // 2
    own_rows = in_weight.shape[0]
    gate_own = gate_gain.shape[0]
    wide_a = min(1024, inner)
    dims = (part, size, piece, width, inner, heads, taps)

    head = padded(head_params, 8, lanes)
    skip = jnp.repeat(head_params[2], inner // heads)[None, :]
    summing = summing_matrix(inner, heads)

    in_low = padded(in_weight.astype(bf16), own_rows, inner + conv_dim + lanes)
    out_low_own = out_weight.astype(bf16).reshape(2, own_rows, width)
    own_small = jnp.concatenate(
        [
            padded(conv_params.astype(bf16), tap_rows, lanes),
            padded(norm_gain.astype(bf16)[None, :], 1, lanes),
            padded(gate_gain.astype(bf16)[None, :], 1, lanes),
        ]
    )
    shard = jnp.concatenate([in_low, out_low_own[0], out_low_own[1]], axis=1)
    half = width // 6
    both = jnp.concatenate([layer_in, out_grad[:, :, :half]], axis=2)
    second = lax.optimization_barrier(out_grad[:, :, half:])
    if own_rows >= tap_rows + 2:
        shard = jnp.concatenate([shard, padded(own_small, own_rows, lanes)], axis=1)
        gathered = gather_seq(shard, both, second, head, skip)
        seq_small = gathered[:, : tap_rows + 2, -lanes:]
    else:
        gathered = gather_seq(shard)
        seq_small = gather_seq(padded(own_small, 8, lanes))[:, : tap_rows + 2]
    tokens = to_sequences(after(both, shard), part, size)
    small = jnp.zeros((8, conv_dim), bf16)
    group = lax.axis_index("dp")
    for at, rows, count in (
        (0, tap_rows, conv_own),
        (tap_rows, 1, own_rows),
        (tap_rows + 1, 1, gate_own),
    ):
        piece_rows = jnp.concatenate(
            [seq_small[z, at : at + rows, :count] for z in range(seq_extent)], axis=1
        )
        small = lax.dynamic_update_slice(small, piece_rows, (at, group * seq_extent * count))
    front_end = inner + conv_dim + lanes
    wg = gathered[:, :, :inner]
    wa = gathered[:, :, inner : inner + wide_a]
    wb = gathered[:, :, inner + wide_a : front_end]
    wo = jnp.stack(
        [
            gathered[:, :, front_end : front_end + width],
            gathered[:, :, front_end + width : front_end + 2 * width],
        ],
        axis=1,
    ).reshape(-1, 2 * own_rows, width)
    order_a, order_b = dp_orders()
    last = len(order_a) - 1
    for step in range(last):
        wa = gather_dp_bit(wa, order_a, step)
        wb = gather_dp_bit(wb, order_b, step)
    small = sum_bits(small, "dp", order_a[:-1])
    for step in range(last):
        if step == 1:
            wg, wo = after((wg, wo), wa, wb, small)
        if step < last - 1:
            wg = gather_dp_bit(wg, order_a, step)
            wo = gather_dp_bit(wo, order_b, step)

    def core_halves(block):
        block = block.reshape(owners // 2 // seq_extent, -1, block.shape[-1])
        return block, swap(block, "dp", 0)

    wb = core_halves(wb)
    wa = core_halves(wa)
    small = sum_bits(after(small, tokens, wa, wb, head, skip), "dp", [0]).astype(f32)
    cots_b = to_sequences(after(second, tokens), part, size)

    edge = core
    if groups > 1:
        edge = tokens.reshape(part, size * piece, -1)[:, size * piece - 8 :, :width]
        edge = shifted_by(edge, "seq", size).reshape(part * 8, width)

    def forward(start, kept, blocks):
        weights = (wa, wb, small, head, skip)
        grouped = groups > 1
        return mixer_forward(dims, core, tokens, *weights, edge, start, grouped, kept, blocks)

    start = core
    if groups > 1:
        first_out = forward(jnp.zeros((part * state_dim, inner), f32), None, (0, size))
        cum_last = first_out[3].reshape(part, size, piece, lanes)[:, :, piece - 1, :heads]
        decay = jnp.exp2(jnp.sum(cum_last, axis=1))
        decay = jnp.repeat(decay, inner // heads, axis=1)[:, None, :]

        def relay(ends, distance):
            ends = ends.reshape(part, state_dim, inner)
            carried = jnp.zeros_like(ends)
            for _ in range(groups - 1):
                sent = (decay * carried + ends).astype(bf16)
                carried = shifted_by(sent, "seq", distance).astype(f32)
            return carried.reshape(part * state_dim, inner)

        start = relay(first_out[6], size)
    normed, ext, dtr, cum, y, sin, _, _ = forward(start, None, (0, size))
    wg = core_halves(gather_dp_bit(wg, order_a, last - 1, normed))
    wo = core_halves(gather_dp_bit(wo, order_b, last - 1, normed))
    layer_rows, dy, dgate, dgain, *handed = gate_step(
        dims, core, normed, tokens, cots_b, y, wg, wo, small
    )
    layer_out = to_pieces(layer_rows, part, size, piece)
    consts = (small, head, skip, summing, dgain)
    saved = (ext, dtr, cum, y, sin, dy)

    def backward(carry, blocks, fresh=False):
        return list(mixer_backward(dims, saved, consts, carry, blocks, fresh))

    def fresh_carry():
        if groups == 1:
            return (core, head, core, core)
        lead = jnp.zeros((part * (conv_dim // lanes), 8, lanes), f32)
        first_out = (core, head, jnp.zeros((part * state_dim, inner), f32), lead)
        first_out = backward(first_out, (0, size))
        return (core, head, relay(first_out[2], -size), lead)

    calls = [(size - 1, 1), (size - 2, 1), (0, size - 2)]
    g_out = core_sums(*handed[:2])
    g_gate = core_sums(*handed[2:])
    carry = backward(fresh_carry(), calls[0], groups == 1)
    carry[2], g_out, g_gate = lax.optimization_barrier((carry[2], g_out, g_gate))
    g_out = core_and_next(*g_out, order_a)
    g_gate = core_and_next(*g_gate, order_b)
    carry = backward(carry, calls[1])
    carry[2], g_out, g_gate = lax.optimization_barrier((carry[2], g_out, g_gate))
    g_out = g_out[0] + g_out[1].astype(f32)
    g_gate = g_gate[0] + g_gate[1].astype(f32)
    for step in range(2, last + 1):
        g_out = scatter_dp_bit(g_out, order_a, step)
        g_gate = scatter_dp_bit(g_gate, order_b, step)
    carry = backward(carry, calls[2])
    carry[0], g_out, g_gate = lax.optimization_barrier((carry[0], g_out, g_gate))
    g_rest = scatter_seq(
        jnp.concatenate([g_gate, g_out[:, :own_rows], g_out[:, own_rows:]], axis=2)
    )
    dproj, dsmall, _, lead = carry
    if groups > 1:
        lead = shifted_by(lead.astype(bf16), "seq", -size).astype(f32)
        lead = lead.reshape(part, -1, 8, lanes).transpose(0, 2, 1, 3).reshape(part, 8, conv_dim)
        fixes = []
        for row in range(taps - 1):
            terms = [small[tap] * lead[:, row - tap] for tap in range(row + 1)]
            fixes.append(sum(terms[1:], terms[0]))
        fix = jnp.pad(jnp.stack(fixes, axis=1), ((0, 0), (0, 0), (0, lanes)))
        dproj = dproj.reshape(part, size * piece, conv_dim + lanes)
        ends = dproj[:, size * piece - (taps - 1) :].astype(f32) + fix
        dproj = dproj.at[:, size * piece - (taps - 1) :].set(ends.astype(bf16))
        dproj = dproj.reshape(-1, conv_dim + lanes)
    tokens = after(tokens, layer_out, dproj)
    dx, dsmall, *handed = input_grad(dims, core, tokens, dgate, dproj, small, dsmall, wg, wa, wb)
    dx, dsmall, handed, g_rest = lax.optimization_barrier((dx, dsmall, handed, g_rest))
    g_a = core_sums(*handed[:2])
    g_b = core_sums(*handed[2:])
    g_a = core_and_next(*g_a, order_a)
    g_b = core_and_next(*g_b, order_b)
    dsmall = after(dsmall, g_a[0], g_b[0])
    g_a = g_a[0] + g_a[1].astype(f32)
    g_b = g_b[0] + g_b[1].astype(f32)
    for step in range(2, last + 1):
        g_a = scatter_dp_bit(g_a, order_a, step)
        g_b = scatter_dp_bit(g_b, order_b, step)
    pieces = to_pieces(dx, part, size, piece)
    in_grad = out_grad.astype(f32) + pieces.astype(f32)
    g_front = scatter_seq(jnp.concatenate([g_a, g_b], axis=2), pieces)
    dsmall = sum_bits(dsmall, "dp", order_a[::-1])
    slab_wide = -(-max(3 * lanes, seq_extent * max(conv_own, own_rows, gate_own)) // lanes) * lanes
    slab = [
        padded(
            lax.dynamic_slice(
                dsmall, (at, group * seq_extent * count), (rows, seq_extent * count)
            ),
            rows,
            slab_wide,
        )
        for at, rows, count in (
            (0, tap_rows, conv_own),
            (tap_rows, 1, own_rows),
            (tap_rows + 1, 1, gate_own),
        )
    ]
    dsmall = jnp.concatenate(slab + [dsmall[tap_rows + 2 :, :slab_wide]])
    sums = [dsmall]
    for distance in range(1, seq_extent):
        route = [(i, (i + distance) % seq_extent) for i in range(seq_extent)]
        sums.append(lax.ppermute(dsmall, "seq", route))

    states = (
        (norm_gain[None, :], norm_first[None, :], norm_second[None, :]),
        (in_weight, in_first, in_second),
        (conv_params, conv_first, conv_second),
        (gate_gain[None, :], gate_first[None, :], gate_second[None, :]),
        (out_weight, out_first, out_second),
        (head_params, head_first, head_second),
    )
    new = adam(rates, sums, g_rest, g_front, states, heads, taps)
    new = [array[0] if array.shape[0] == 1 else array for array in new]
    return (layer_out, in_grad, *new)


def solution(mesh):
    in_specs = (
        P("dp", "seq", None),
        P("dp", "seq", None),
        P(("dp", "seq")),
        P(("dp", "seq"), None),
        P(None, ("dp", "seq")),
        P(("dp", "seq")),
        P(("dp", "seq"), None),
        P(),
        P(("dp", "seq")),
        P(("dp", "seq")),
        P(("dp", "seq"), None),
        P(("dp", "seq"), None),
        P(None, ("dp", "seq")),
        P(None, ("dp", "seq")),
        P(("dp", "seq")),
        P(("dp", "seq")),
        P(("dp", "seq"), None),
        P(("dp", "seq"), None),
        P(),
        P(),
        P(),
        P(),
    )
    out_specs = (
        P("dp", "seq", None),
        P("dp", "seq", None),
        P(("dp", "seq")),
        P(("dp", "seq")),
        P(("dp", "seq")),
        P(("dp", "seq"), None),
        P(("dp", "seq"), None),
        P(("dp", "seq"), None),
        P(None, ("dp", "seq")),
        P(None, ("dp", "seq")),
        P(None, ("dp", "seq")),
        P(("dp", "seq")),
        P(("dp", "seq")),
        P(("dp", "seq")),
        P(("dp", "seq"), None),
        P(("dp", "seq"), None),
        P(("dp", "seq"), None),
        P(),
        P(),
        P(),
        P(("dp", "seq"), None),
        P(("dp", "seq"), None),
    )
    return jax.shard_map(local, mesh=mesh, in_specs=in_specs, out_specs=out_specs, check_vma=False)
```

```python
import math
from functools import partial

import jax
import jax.numpy as jnp
import numpy as np
from jax import lax
from jax.experimental import pallas as pl
from jax.experimental.pallas import tpu as pltpu
from jax.sharding import PartitionSpec as P

norm_eps = 1e-05
adam_eps = 1e-08
log2e = math.log2(math.e)
lanes = 128
vmem_bytes = 56 * 1024 * 1024
f32 = jnp.float32
bf16 = jnp.bfloat16


def dot(left, right, left_dim=1, right_dim=0):
    return lax.dot_general(
        left, right, (((left_dim,), (right_dim,)), ((), ())), preferred_element_type=f32
    )


def halves(value):
    high = value.astype(bf16)
    return high, (value - high.astype(f32)).astype(bf16)


def sigmoid(value):
    return 0.5 * jnp.tanh(0.5 * value) + 0.5


def column(ref_value, at, width):
    return jnp.broadcast_to(ref_value[:, at : at + 1], (ref_value.shape[0], width))


def pair_columns(value, pair, low_lane):
    rows = value.shape[0]
    first = column(value, 2 * pair, lanes)
    second = column(value, 2 * pair + 1, lanes)
    return jnp.where(low_lane, first, second), first, second


def tri_sum(mask, value, head_lane):
    high = value.astype(bf16).astype(f32)
    rest = value - high
    mid = rest.astype(bf16).astype(f32)
    low = rest - mid
    packed = high + pltpu.roll(mid, 32, 1) + pltpu.roll(low, 64, 1)
    summed = dot(mask, packed.astype(bf16))
    total = summed + pltpu.roll(summed, lanes - 32, 1) + pltpu.roll(summed, lanes - 64, 1)
    return jnp.where(head_lane, total, 0.0)


def conv_chunk(ext_ref, conv_ref, at, length, taps):
    summed = conv_ref[taps : taps + 1, at : at + lanes]
    base = 8 - (taps - 1)
    for tap in range(taps):
        summed = (
            summed
            + conv_ref[tap : tap + 1, at : at + lanes]
            * ext_ref[at // lanes, base + tap : base + tap + length, :]
        )
    return summed


def put_columns(ext_ref, rows, values, chunk):
    for at in range(0, values.shape[1], lanes):
        ext_ref[chunk + at // lanes, rows, :] = values[:, at : at + lanes]


def step_sizes(dt_raw, head_ref, head_lane):
    shifted = dt_raw + head_ref[0:1, :]
    steps = jnp.maximum(shifted, 0.0) + jnp.log1p(jnp.exp(-jnp.abs(shifted)))
    return jnp.where(head_lane, steps, 0.0), shifted


def fetch_weight(core_ref, own_ref, other_ref, whole_ref, sems):
    blocks, rows, _ = own_ref.shape
    core = core_ref[0]
    copies = []
    for block in range(blocks):
        for which, source in ((core, own_ref), (1 - core, other_ref)):
            at = pl.multiple_of((2 * block + which) * rows, rows)
            copies.append(
                pltpu.make_async_copy(
                    source.at[block], whole_ref.at[pl.ds(at, rows)], sems.at[len(copies)]
                )
            )
    for copy in copies:
        copy.start()
    return copies


def hand_out(core, total_ref, send_ref, keep_ref):
    blocks, rows, _ = send_ref.shape
    for block in range(blocks):
        at = pl.multiple_of((2 * block + 1 - core) * rows, rows)
        send_ref[block] = total_ref[pl.ds(at, rows), :].astype(bf16)
        at = pl.multiple_of((2 * block + core) * rows, rows)
        keep_ref[block] = total_ref[pl.ds(at, rows), :]


def add_product(total_ref, left_ref, right):
    for at in range(0, total_ref.shape[0], 2 * lanes):
        here = slice(at, at + 2 * lanes)
        total_ref[here, :] += dot(left_ref[:, here], right, 0, 0)


def mixer_forward_kernel(
    core_ref,
    x_ref,
    edge_ref,
    wa_own,
    wa_other,
    wb_own,
    wb_other,
    conv_ref,
    head_ref,
    skip_ref,
    start_ref,
    before_ref,
    *refs,
    heads,
    inner,
    taps,
    grouped,
    resumed,
):
    (
        normed_ref,
        ext_ref,
        dtr_ref,
        cum_ref,
        y_ref,
        sin_ref,
        end_ref,
        after_ref,
        tail_ref,
        state_ref,
        carried_ref,
        weighted_ref,
        wa_ref,
        wb_ref,
        wa_sems,
        wb_sems,
    ) = refs[6:] if resumed else refs
    block = pl.program_id(1)
    length, width = x_ref.shape

    @pl.when(jnp.logical_and(pl.program_id(0) == 0, block == 0))
    def _():
        copies = fetch_weight(core_ref, wa_own, wa_other, wa_ref, wa_sems)
        copies += fetch_weight(core_ref, wb_own, wb_other, wb_ref, wb_sems)
        for copy in copies:
            copy.wait()

    half = length // 2
    wide_a = wa_ref.shape[1]
    conv_dim = conv_ref.shape[1]
    state_dim = (conv_dim - inner) // 2

    def norm_of(rows):
        rows = rows.astype(f32)
        scale = lax.rsqrt(jnp.mean(rows * rows, axis=-1, keepdims=True) + norm_eps)
        return (rows * scale * conv_ref[taps + 1 : taps + 2, :width]).astype(bf16)

    @pl.when(block == 0)
    def _():
        if resumed:
            state_ref[...] = start_ref[...]
            tail_ref[...] = before_ref[...]
        elif grouped:
            state_ref[...] = start_ref[...]
            edge = norm_of(edge_ref[...])
            put_columns(tail_ref, slice(0, 8), dot(edge, wa_ref[...]), 0)
            edge_b = dot(edge, wb_ref[...])[:, : conv_dim - wide_a]
            put_columns(tail_ref, slice(0, 8), edge_b, wide_a // lanes)
        else:
            state_ref[...] = jnp.zeros_like(state_ref)
            tail_ref[...] = jnp.zeros_like(tail_ref)

    normed = norm_of(x_ref[...])
    normed_ref[...] = normed
    ext_ref[:, 0:8, :] = tail_ref[...]
    own_rows = slice(8, 8 + length)
    for at in range(0, wide_a, 2 * lanes):
        product = dot(normed, wa_ref[:, at : at + 2 * lanes])
        put_columns(ext_ref, own_rows, product, at // lanes)
    second = dot(normed, wb_ref[...])
    put_columns(ext_ref, own_rows, second[:, : conv_dim - wide_a], wide_a // lanes)
    dt_raw = second[:, conv_dim - wide_a :]
    tail_ref[...] = ext_ref[:, length : length + 8, :]

    lane = lax.broadcasted_iota(jnp.int32, (length, lanes), 1)
    low_lane = lane < lanes // 2
    head_lane = lane < heads
    dtr_ref[...] = dt_raw
    steps, _ = step_sizes(dt_raw, head_ref, head_lane)
    log_decay = steps * (-log2e * jnp.exp(head_ref[1:2, :]))
    row = lax.broadcasted_iota(jnp.int32, (length, length), 0)
    col = lax.broadcasted_iota(jnp.int32, (length, length), 1)
    cum = tri_sum((row >= col).astype(bf16), log_decay, head_lane)
    cum_ref[...] = cum
    cum_rows = cum.T

    def mixed_chunk(at):
        summed = conv_chunk(ext_ref, conv_ref, at, length, taps)
        return summed * sigmoid(summed)

    keys = jnp.concatenate(
        [mixed_chunk(inner + at) for at in range(0, state_dim, lanes)], axis=1
    ).astype(bf16)
    queries = jnp.concatenate(
        [mixed_chunk(inner + state_dim + at) for at in range(0, state_dim, lanes)], axis=1
    ).astype(bf16)
    state_low = state_ref[...].astype(bf16)
    sin_ref[...] = state_low
    carried_ref[...] = dot(queries, state_low)
    square = (half, half)
    diag = lax.broadcasted_iota(jnp.int32, square, 0) >= lax.broadcasted_iota(
        jnp.int32, square, 1
    )
    scores_00 = jnp.where(diag, dot(queries[:half], keys[:half], 1, 1), 0.0)
    scores_10 = dot(queries[half:], keys[:half], 1, 1)
    scores_11 = jnp.where(diag, dot(queries[half:], keys[half:], 1, 1), 0.0)
    for pair in range(heads // 2):
        at = pair * lanes
        values = mixed_chunk(at)
        cum_rep, cum_0, cum_1 = pair_columns(cum, pair, low_lane)
        dt_rep, _, _ = pair_columns(steps, pair, low_lane)
        stepped = values * dt_rep
        last = cum_rep[length - 1 : length, :]
        weighted_ref[:, at : at + lanes] = (stepped * jnp.exp2(last - cum_rep)).astype(bf16)
        top = None
        bottom = None
        for which, cum_col in ((0, cum_0), (1, cum_1)):
            own = jnp.where(low_lane if which == 0 else jnp.logical_not(low_lane), stepped, 0.0)
            own = own.astype(bf16)
            head = 2 * pair + which
            early = cum_rows[head : head + 1, :half]
            late = cum_rows[head : head + 1, half:]
            mix_00 = jnp.exp2(jnp.minimum(cum_col[:half] - early, 0.0)) * scores_00
            mix_10 = jnp.exp2(cum_col[half:] - early) * scores_10
            mix_11 = jnp.exp2(jnp.minimum(cum_col[half:] - late, 0.0)) * scores_11
            part_top = dot(mix_00.astype(bf16), own[:half])
            part_bottom = dot(
                jnp.concatenate([mix_10.astype(bf16), mix_11.astype(bf16)], axis=1), own
            )
            top = part_top if top is None else top + part_top
            bottom = part_bottom if bottom is None else bottom + part_bottom
        rest = (
            jnp.exp2(cum_rep) * carried_ref[:, at : at + lanes]
            + skip_ref[0:1, at : at + lanes] * values
        )
        y_ref[0:half, at : at + lanes] = top + rest[:half]
        y_ref[half:length, at : at + lanes] = bottom + rest[half:]
        state_ref[:, at : at + lanes] = jnp.exp2(last) * state_ref[:, at : at + lanes]

    state_ref[...] += dot(keys, weighted_ref[...], 0, 0)

    @pl.when(block == pl.num_programs(1) - 1)
    def _():
        end_ref[...] = state_ref[...]
        after_ref[...] = tail_ref[...]


def gate_kernel(
    core_ref,
    normed_ref,
    x_ref,
    cot_a_ref,
    cot_b_ref,
    y_ref,
    wg_own,
    wg_other,
    wo_own,
    wo_other,
    small_ref,
    out_ref,
    dy_ref,
    dgate_ref,
    dgain_ref,
    out_send,
    out_keep,
    gate_send,
    gate_keep,
    gate_ref,
    dno_ref,
    low_ref,
    cot_ref,
    out_sum,
    gate_sum,
    wg_ref,
    wo_ref,
    wg_sems,
    wo_sems,
    *,
    gain_row,
):
    length, inner = y_ref.shape
    first = jnp.logical_and(pl.program_id(0) == 0, pl.program_id(1) == 0)

    @pl.when(first)
    def _():
        copies = fetch_weight(core_ref, wg_own, wg_other, wg_ref, wg_sems)
        copies += fetch_weight(core_ref, wo_own, wo_other, wo_ref, wo_sems)
        dgain_ref[...] = jnp.zeros_like(dgain_ref)
        out_sum[...] = jnp.zeros_like(out_sum)
        gate_sum[...] = jnp.zeros_like(gate_sum)
        for copy in copies:
            copy.wait()

    gate_ref[...] = dot(normed_ref[...], wg_ref[...])
    cot_ref[:, : cot_a_ref.shape[1]] = cot_a_ref[...]
    cot_ref[:, cot_a_ref.shape[1] :] = cot_b_ref[...]
    dno_ref[...] = dot(cot_ref[...], wo_ref[...], 1, 1)
    squares = jnp.zeros((length, lanes), f32)
    crosses = jnp.zeros((length, lanes), f32)
    for at in range(0, inner, lanes):
        here = slice(at, at + lanes)
        gate = gate_ref[:, here]
        gated = y_ref[:, here] * (gate * sigmoid(gate))
        squares = squares + gated * gated
        crosses = crosses + gated * (small_ref[gain_row : gain_row + 1, here] * dno_ref[:, here])
    scale = lax.rsqrt(jnp.sum(squares, axis=1, keepdims=True) * (1.0 / inner) + norm_eps)
    cross = scale * scale * scale * (jnp.sum(crosses, axis=1, keepdims=True) * (1.0 / inner))
    scale_b = jnp.broadcast_to(scale, (length, lanes))
    cross_b = jnp.broadcast_to(cross, (length, lanes))
    for at in range(0, inner, lanes):
        here = slice(at, at + lanes)
        gate = gate_ref[:, here]
        mixed_out = y_ref[:, here]
        sig = sigmoid(gate)
        silu = gate * sig
        gated = mixed_out * silu
        scaled = gated * scale_b
        d_out = dno_ref[:, here]
        low_ref[:, here] = (scaled * small_ref[gain_row : gain_row + 1, here]).astype(bf16)
        dgain_ref[0:1, here] += jnp.sum(scaled * d_out, axis=0, keepdims=True)
        d_gated = scale_b * (small_ref[gain_row : gain_row + 1, here] * d_out) - gated * cross_b
        dy_ref[:, here] = (d_gated * silu).astype(bf16)
        dgate_ref[:, here] = (d_gated * mixed_out * (sig * (1.0 + gate * (1.0 - sig)))).astype(
            bf16
        )
    out_ref[...] = (x_ref[...].astype(f32) + dot(low_ref[...], wo_ref[...])).astype(bf16)
    add_product(out_sum, low_ref, cot_ref[...])
    add_product(gate_sum, normed_ref, dgate_ref[...])
    last = jnp.logical_and(
        pl.program_id(0) == pl.num_programs(0) - 1, pl.program_id(1) == pl.num_programs(1) - 1
    )

    @pl.when(last)
    def _():
        hand_out(core_ref[0], out_sum, out_send, out_keep)
        hand_out(core_ref[0], gate_sum, gate_send, gate_keep)


def mixer_backward_kernel(
    ext_ref,
    dtr_ref,
    cum_ref,
    y_ref,
    sin_ref,
    dy_ref,
    conv_ref,
    head_ref,
    skip_ref,
    sum_ref,
    start_ref,
    next_ref,
    small_in_ref,
    dgain_ref,
    _,
    dproj_ref,
    dconv_ref,
    end_ref,
    lead_ref,
    grad_ref,
    dsx_ref,
    dwv_ref,
    dye_ref,
    weighted_ref,
    zhigh_ref,
    zlow_ref,
    direct_ref,
    rows_ref,
    *,
    heads,
    inner,
    taps,
    fresh,
):
    step = pl.program_id(1)
    length = dy_ref.shape[0]
    half = length // 2
    conv_dim = conv_ref.shape[1]
    state_dim = (conv_dim - inner) // 2
    first = jnp.logical_and(pl.program_id(0) == 0, step == 0)

    @pl.when(first)
    def _():
        if small_in_ref.shape == dconv_ref.shape:
            dconv_ref[...] = small_in_ref[...]
        else:
            dconv_ref[...] = jnp.zeros_like(dconv_ref)
            dconv_ref[taps + 2 : taps + 3, :inner] = dgain_ref[0:1, :]
        rows_ref[...] = jnp.zeros_like(rows_ref)

    @pl.when(step == 0)
    def _():
        if fresh:
            grad_ref[...] = jnp.zeros_like(grad_ref)
            dsx_ref[:, length : length + 8, :] = jnp.zeros((conv_dim // lanes, 8, lanes), f32)
        else:
            grad_ref[...] = start_ref[...]
            dsx_ref[:, length : length + 8, :] = next_ref[...]

    @pl.when(step > 0)
    def _():
        dsx_ref[:, length : length + 8, :] = dsx_ref[:, 0:8, :]

    lane = lax.broadcasted_iota(jnp.int32, (length, lanes), 1)
    low_lane = lane < lanes // 2
    head_lane = lane < heads
    steps, shifted = step_sizes(dtr_ref[...], head_ref, head_lane)
    cum = cum_ref[...]
    cum_rows = cum.T

    def slope_chunk(at):
        summed = conv_chunk(ext_ref, conv_ref, at, length, taps)
        sig = sigmoid(summed)
        return summed * sig, sig * (1.0 + summed * (1.0 - sig))

    def put_grad(at, d_summed):
        here = slice(at, at + lanes)
        chunk = at // lanes
        dsx_ref[chunk, 0:length, :] = d_summed
        total = None
        for tap in range(taps):
            base = 8 - (taps - 1) + tap
            dconv_ref[tap : tap + 1, here] += jnp.sum(
                d_summed * ext_ref[chunk, base : base + length, :], axis=0, keepdims=True
            )
            back = taps - 1 - tap
            term = conv_ref[tap : tap + 1, here] * dsx_ref[chunk, back : back + length, :]
            total = term if total is None else total + term
        dconv_ref[taps : taps + 1, here] += jnp.sum(d_summed, axis=0, keepdims=True)
        dproj_ref[:, here] = total.astype(bf16)

    parts = [slope_chunk(inner + at) for at in range(0, 2 * state_dim, lanes)]
    count = state_dim // lanes
    keys = jnp.concatenate([part[0] for part in parts[:count]], axis=1).astype(bf16)
    queries = jnp.concatenate([part[0] for part in parts[count:]], axis=1).astype(bf16)
    grad_low = grad_ref[...].astype(bf16)
    dwv_ref[...] = dot(keys, grad_low)
    square = (half, half)
    diag = lax.broadcasted_iota(jnp.int32, square, 0) <= lax.broadcasted_iota(
        jnp.int32, square, 1
    )
    scores_00 = jnp.where(diag, dot(keys[:half], queries[:half], 1, 1), 0.0)
    scores_01 = dot(keys[:half], queries[half:], 1, 1)
    scores_11 = jnp.where(diag, dot(keys[half:], queries[half:], 1, 1), 0.0)
    ds_00 = jnp.zeros(square, f32)
    ds_01 = jnp.zeros(square, f32)
    ds_11 = jnp.zeros(square, f32)
    for pair in range(heads // 2):
        at = pair * lanes
        here = slice(at, at + lanes)
        values, slope = slope_chunk(at)
        cum_rep, cum_0, cum_1 = pair_columns(cum, pair, low_lane)
        dt_rep, _, _ = pair_columns(steps, pair, low_lane)
        stepped = (values * dt_rep).astype(bf16)
        stepped_f = stepped.astype(f32)
        last = cum_rep[length - 1 : length, :]
        tail = jnp.exp2(last - cum_rep)
        d_y = dy_ref[:, here]
        d_yf = d_y.astype(f32)
        d_y_t = d_yf.T.astype(bf16)
        dye_ref[:, here] = (d_yf * jnp.exp2(cum_rep)).astype(bf16)
        top = None
        bottom = None
        for which, cum_col in ((0, cum_0), (1, cum_1)):
            own_lane = low_lane if which == 0 else jnp.logical_not(low_lane)
            own_dy = jnp.where(own_lane, d_yf, 0.0).astype(bf16)
            own_x = jnp.where(own_lane, stepped_f, 0.0).astype(bf16)
            head = 2 * pair + which
            early = cum_rows[head : head + 1, :half]
            late = cum_rows[head : head + 1, half:]
            decay_00 = jnp.exp2(jnp.minimum(early - cum_col[:half], 0.0))
            decay_01 = jnp.exp2(late - cum_col[:half])
            decay_11 = jnp.exp2(jnp.minimum(late - cum_col[half:], 0.0))
            mix_0 = jnp.concatenate(
                [(decay_00 * scores_00).astype(bf16), (decay_01 * scores_01).astype(bf16)], axis=1
            )
            mix_1 = (decay_11 * scores_11).astype(bf16)
            part_top = dot(mix_0, own_dy)
            part_bottom = dot(mix_1, own_dy[half:])
            top = part_top if top is None else top + part_top
            bottom = part_bottom if bottom is None else bottom + part_bottom
            d_mix_0 = dot(own_x[:half], d_y_t)
            d_mix_1 = dot(own_x[half:], d_y_t[:, half:])
            ds_00 = ds_00 + decay_00 * d_mix_0[:, :half]
            ds_01 = ds_01 + decay_01 * d_mix_0[:, half:]
            ds_11 = ds_11 + decay_11 * d_mix_1
        d_diag = jnp.concatenate([top, bottom], axis=0)
        weighted = (stepped_f * tail).astype(bf16)
        weighted_ref[:, here] = weighted
        d_weighted = dwv_ref[:, here]
        through = weighted.astype(f32) * d_weighted
        d_stepped = d_diag + tail * d_weighted
        skip = skip_ref[0:1, here]
        z = d_yf * (y_ref[:, here] - skip * values) - stepped_f * d_diag - through
        z_high, z_low = halves(z)
        zhigh_ref[:, here] = z_high
        zlow_ref[:, here] = z_low
        direct_ref[:, here] = (d_stepped * values).astype(bf16)
        total_decay = jnp.exp2(last)
        rows_ref[0:1, here] = jnp.sum(through, axis=0, keepdims=True) + total_decay * jnp.sum(
            grad_ref[:, here] * sin_ref[:, here].astype(f32), axis=0, keepdims=True
        )
        rows_ref[1:2, here] = jnp.sum(d_yf * values, axis=0, keepdims=True)
        put_grad(at, (d_stepped * dt_rep + skip * d_yf) * slope)
        grad_ref[:, here] = total_decay * grad_ref[:, here]

    grad_ref[...] += dot(queries, dye_ref[...], 0, 0)
    ds_00 = jnp.where(diag, ds_00, 0.0).astype(bf16)
    ds_11 = jnp.where(diag, ds_11, 0.0).astype(bf16)
    ds_01 = ds_01.astype(bf16)
    d_queries = dot(dye_ref[...], sin_ref[...], 1, 1)
    d_keys = dot(weighted_ref[...], grad_low, 1, 1)
    d_queries = d_queries + jnp.concatenate(
        [
            dot(ds_00, keys[:half], 0, 0),
            dot(ds_01, keys[:half], 0, 0) + dot(ds_11, keys[half:], 0, 0),
        ],
        axis=0,
    )
    d_keys = d_keys + jnp.concatenate(
        [
            dot(ds_00, queries[:half]) + dot(ds_01, queries[half:]),
            dot(ds_11, queries[half:]),
        ],
        axis=0,
    )
    for at in range(0, state_dim, lanes):
        put_grad(inner + at, d_keys[:, at : at + lanes] * parts[at // lanes][1])
        put_grad(
            inner + state_dim + at,
            d_queries[:, at : at + lanes] * parts[count + at // lanes][1],
        )
    summing = sum_ref[...]
    rows_high, rows_low = halves(rows_ref[...])
    row_sums = dot(rows_high, summing) + dot(rows_low, summing)
    d_cum = dot(zhigh_ref[...], summing) + dot(zlow_ref[...], summing)
    at_last = lax.broadcasted_iota(jnp.int32, (length, lanes), 0) == length - 1
    d_cum = d_cum + jnp.where(at_last, row_sums[0:1, :], 0.0)
    row = lax.broadcasted_iota(jnp.int32, (length, length), 0)
    col = lax.broadcasted_iota(jnp.int32, (length, length), 1)
    d_log = tri_sum((row <= col).astype(bf16), d_cum, head_lane)
    rate = jnp.exp(head_ref[1:2, :])
    d_steps = dot(direct_ref[...], summing) - rate * d_log
    d_raw = jnp.where(head_lane, d_steps * sigmoid(shifted), 0.0)
    dproj_ref[:, conv_dim : conv_dim + lanes] = d_raw.astype(bf16)
    head_row = slice(taps + 3, taps + 4)
    dconv_ref[head_row, :lanes] += jnp.sum(d_raw, axis=0, keepdims=True)
    dconv_ref[head_row, lanes : 2 * lanes] += jnp.sum(d_log * steps, axis=0, keepdims=True) * (
        -rate
    )
    dconv_ref[head_row, 2 * lanes : 3 * lanes] += row_sums[1:2, :]

    @pl.when(step == pl.num_programs(1) - 1)
    def _():
        end_ref[...] = grad_ref[...]
        lead_ref[...] = dsx_ref[:, 0:8, :]


def input_grad_kernel(
    core_ref,
    x_ref,
    dgate_ref,
    dproj_ref,
    small_ref,
    dsmall_in_ref,
    wg_own,
    wg_other,
    wa_own,
    wa_other,
    wb_own,
    wb_other,
    dx_ref,
    dsmall_ref,
    a_send,
    a_keep,
    b_send,
    b_keep,
    normed_ref,
    a_sum,
    b_sum,
    wg_ref,
    wa_ref,
    wb_ref,
    wg_sems,
    wa_sems,
    wb_sems,
    *,
    gain_row,
):
    first = jnp.logical_and(pl.program_id(0) == 0, pl.program_id(1) == 0)
    width = x_ref.shape[1]

    @pl.when(first)
    def _():
        copies = fetch_weight(core_ref, wg_own, wg_other, wg_ref, wg_sems)
        copies += fetch_weight(core_ref, wa_own, wa_other, wa_ref, wa_sems)
        copies += fetch_weight(core_ref, wb_own, wb_other, wb_ref, wb_sems)
        dsmall_ref[...] = dsmall_in_ref[...]
        a_sum[...] = jnp.zeros_like(a_sum)
        b_sum[...] = jnp.zeros_like(b_sum)
        for copy in copies:
            copy.wait()

    wide_a = wa_ref.shape[1]
    d_normed = (
        dot(dgate_ref[...], wg_ref[...], 1, 1)
        + dot(dproj_ref[:, :wide_a], wa_ref[...], 1, 1)
        + dot(dproj_ref[:, wide_a:], wb_ref[...], 1, 1)
    )
    rows = x_ref[...].astype(f32)
    scale = lax.rsqrt(jnp.mean(rows * rows, axis=-1, keepdims=True) + norm_eps)
    scaled = rows * scale
    dsmall_ref[gain_row : gain_row + 1, :width] += jnp.sum(
        scaled * d_normed, axis=0, keepdims=True
    )
    gain = small_ref[gain_row : gain_row + 1, :width]
    normed_ref[...] = (scaled * gain).astype(bf16)
    add_product(a_sum, normed_ref, dproj_ref[:, :wide_a])
    add_product(b_sum, normed_ref, dproj_ref[:, wide_a:])
    inner_grad = gain * d_normed
    cross = jnp.mean(scaled * inner_grad, axis=-1, keepdims=True)
    dx_ref[...] = (scale * (inner_grad - scaled * cross)).astype(bf16)
    last = jnp.logical_and(
        pl.program_id(0) == pl.num_programs(0) - 1, pl.program_id(1) == pl.num_programs(1) - 1
    )

    @pl.when(last)
    def _():
        hand_out(core_ref[0], a_sum, a_send, a_keep)
        hand_out(core_ref[0], b_sum, b_send, b_keep)


def adam_kernel(
    rates_ref,
    *refs,
    heads,
    taps,
    at_refs,
    arrivals,
):
    sum_refs, refs = refs[:arrivals], refs[arrivals:]
    rest_refs, front_refs, refs = refs[:arrivals], refs[arrivals : 2 * arrivals], refs[2 * arrivals :]
    ins, outs = refs[:18], refs[18:]
    learn_rate, decay_rate = rates_ref[0], rates_ref[3]
    beta_one, beta_two = rates_ref[1], rates_ref[2]
    first_scale, second_scale = rates_ref[4], rates_ref[5]

    def update(which, grad, index):
        master, first, second = (ref[index] for ref in ins[3 * which : 3 * which + 3])
        new_first = beta_one * first + (1.0 - beta_one) * grad
        new_second = beta_two * second + (1.0 - beta_two) * grad * grad
        change = -learn_rate * (
            (new_first * first_scale) / (jnp.sqrt(new_second * second_scale) + adam_eps)
            + decay_rate * master
        )
        where = at_refs[which]
        outs[where][index] = master + change if which in (1, 4) else change
        outs[where + 1][index] = new_first
        outs[where + 2][index] = new_second
        if which in (1, 4):
            outs[-2 if which == 1 else -1][index] = (master + change).astype(bf16)

    everything = (slice(None), slice(None))
    rest, front = rest_refs[0][...], front_refs[0][...]
    inner = rest.shape[1] // 2
    for rest_ref, front_ref in zip(rest_refs[1:], front_refs[1:]):
        rest = rest + rest_ref[...].astype(f32)
        front = front + front_ref[...].astype(f32)
    proj = ins[3].shape[1]
    update(1, rest[:, :inner], (slice(None), slice(0, inner)))
    update(1, front[:, : proj - inner], (slice(None), slice(inner, proj)))
    rows = rest.shape[0]
    half = inner // 2
    update(4, rest[:, inner : inner + half], (slice(0, rows), slice(None)))
    update(4, rest[:, inner + half :], (slice(rows, 2 * rows), slice(None)))

    place = rates_ref[7].astype(jnp.int32)
    terms = [ref[...] for ref in sum_refs]
    sums = terms[0]
    for term in terms[1:]:
        sums = sums + term

    def own(at, count):
        wide = sums.shape[1]
        shift = lax.rem(wide - place * count, wide)
        return pltpu.roll(sums, shift, 1)[at, :count]

    update(0, own(slice(taps + 1, taps + 2), ins[0].shape[1]), everything)
    update(2, own(slice(0, taps + 1), ins[6].shape[1]), everything)
    update(3, own(slice(taps + 2, taps + 3), ins[9].shape[1]), everything)
    sums = jnp.zeros_like(sums)
    for source in range(arrivals):
        distance = lax.rem(place + arrivals - source, arrivals)
        term = terms[0]
        for which in range(1, arrivals):
            term = jnp.where(distance == which, terms[which], term)
        sums = sums + term
    head_row = slice(taps + 3, taps + 4)
    for row in range(3):
        grad = sums[head_row, row * lanes : row * lanes + heads]
        update(5, grad, (slice(row, row + 1), slice(None)))


def whole(shape):
    return pl.BlockSpec(shape, lambda p, b: (0,) * len(shape))


def by_block(shape, size, back=False):
    if back:
        return pl.BlockSpec(shape, lambda p, s: (p * size + (size - 1 - s), 0))
    return pl.BlockSpec(shape, lambda p, b: (p * size + b, 0))


def by_part(shape):
    return pl.BlockSpec(shape, lambda p, b: (p, 0))


def params():
    return pltpu.CompilerParams(
        dimension_semantics=("arbitrary", "arbitrary"), vmem_limit_bytes=vmem_bytes
    )


def cost(flops, moved, powers):
    return pl.CostEstimate(flops=flops, bytes_accessed=moved, transcendentals=powers)


ANY = pl.BlockSpec(memory_space=pl.ANY)
SMEM = pl.BlockSpec(memory_space=pltpu.SMEM)


def weight_scratch(*weights):
    wholes = [
        pltpu.VMEM((2 * own.shape[0] * own.shape[1], own.shape[2]), bf16) for own, _ in weights
    ]
    return wholes + [pltpu.SemaphoreType.DMA((2 * own.shape[0],)) for own, _ in weights]


def handed_out(rows, columns, blocks):
    shape = (blocks, rows // (2 * blocks), columns)
    return [jax.ShapeDtypeStruct(shape, bf16), jax.ShapeDtypeStruct(shape, f32)]


def mixer_forward(dims, core, tokens, wa, wb, small, head, skip, edge, start, grouped, kept, blocks):
    part, size, piece, width, inner, heads, taps = dims
    first, count = blocks
    conv_dim = small.shape[1]
    state_dim = (conv_dim - inner) // 2
    all_blocks = part * size
    rows = all_blocks * piece
    ext_rows = piece + 8
    chunks = conv_dim // lanes
    resumed = kept is not None

    def by_block(shape):
        return pl.BlockSpec(shape, lambda p, b: (p * size + first + b, 0))

    tail_block = pl.BlockSpec((chunks, 8, lanes), lambda p, b: (p, 0, 0))
    before = core
    if resumed:
        *arrays, start, before = kept
    else:
        arrays = []
    return pl.pallas_call(
        partial(
            mixer_forward_kernel,
            heads=heads,
            inner=inner,
            taps=taps,
            grouped=grouped,
            resumed=resumed,
        ),
        grid=(part, count),
        in_specs=[
            SMEM,
            by_block((piece, width)),
            by_part((8, width)) if grouped else ANY,
            ANY,
            ANY,
            ANY,
            ANY,
            whole(small.shape),
            whole(head.shape),
            whole(skip.shape),
            by_part((state_dim, inner)) if grouped or resumed else ANY,
            tail_block if resumed else ANY,
        ]
        + [ANY] * len(arrays),
        out_specs=[
            by_block((piece, width)),
            pl.BlockSpec((chunks, ext_rows, lanes), lambda p, b: (p * size + first + b, 0, 0)),
            by_block((piece, lanes)),
            by_block((piece, lanes)),
            by_block((piece, inner)),
            by_block((state_dim, inner)),
            by_part((state_dim, inner)),
            tail_block,
        ],
        out_shape=[
            jax.ShapeDtypeStruct((rows, width), bf16),
            jax.ShapeDtypeStruct((all_blocks * chunks, ext_rows, lanes), f32),
            jax.ShapeDtypeStruct((rows, lanes), f32),
            jax.ShapeDtypeStruct((rows, lanes), f32),
            jax.ShapeDtypeStruct((rows, inner), f32),
            jax.ShapeDtypeStruct((all_blocks * state_dim, inner), bf16),
            jax.ShapeDtypeStruct((part * state_dim, inner), f32),
            jax.ShapeDtypeStruct((part * chunks, 8, lanes), f32),
        ],
        scratch_shapes=[
            pltpu.VMEM((chunks, 8, lanes), f32),
            pltpu.VMEM((state_dim, inner), f32),
            pltpu.VMEM((piece, inner), f32),
            pltpu.VMEM((piece, inner), bf16),
        ]
        + weight_scratch(wa, wb),
        input_output_aliases={12 + at: at for at in range(len(arrays))},
        compiler_params=params(),
        cost_estimate=cost(1, 1, 0),
    )(core, tokens, edge, *wa, *wb, small, head, skip, start, before, *arrays)


def gate_step(dims, core, normed, tokens, cots_b, y, wg, wo, small):
    part, size, piece, width, inner, heads, taps = dims
    rows = part * size * piece
    blocks = wo[0].shape[0]
    handed = handed_out(inner, width, blocks) + handed_out(width, inner, blocks)
    wide_b = cots_b.shape[1]
    at_a = width // (width - wide_b)
    return pl.pallas_call(
        partial(gate_kernel, gain_row=taps + 2),
        grid=(part, size),
        in_specs=[
            SMEM,
            by_block((piece, width), size),
            by_block((piece, width), size),
            pl.BlockSpec((piece, width - wide_b), lambda p, b: (p * size + b, at_a)),
            by_block((piece, wide_b), size),
            by_block((piece, inner), size),
            ANY,
            ANY,
            ANY,
            ANY,
            whole(small.shape),
        ],
        out_specs=[
            by_block((piece, width), size),
            by_block((piece, inner), size),
            by_block((piece, inner), size),
            whole((8, inner)),
        ]
        + [whole(array.shape) for array in handed],
        out_shape=[
            jax.ShapeDtypeStruct((rows, width), bf16),
            jax.ShapeDtypeStruct((rows, inner), bf16),
            jax.ShapeDtypeStruct((rows, inner), bf16),
            jax.ShapeDtypeStruct((8, inner), f32),
        ]
        + handed,
        scratch_shapes=[
            pltpu.VMEM((piece, inner), f32),
            pltpu.VMEM((piece, inner), f32),
            pltpu.VMEM((piece, inner), bf16),
            pltpu.VMEM((piece, width), bf16),
            pltpu.VMEM((inner, width), f32),
            pltpu.VMEM((width, inner), f32),
        ]
        + weight_scratch(wg, wo),
        compiler_params=params(),
        cost_estimate=cost(1, 1, 0),
    )(core, normed, tokens, tokens, cots_b, y, *wg, *wo, small)


def mixer_backward(dims, saved, consts, carry, blocks, fresh):
    part, size, piece, width, inner, heads, taps = dims
    first, count = blocks
    small, head, skip, summing, dgain = consts
    conv_dim = small.shape[1]
    state_dim = (conv_dim - inner) // 2
    ext_rows = piece + 8
    chunks = conv_dim // lanes
    wide = conv_dim + lanes
    dproj, dsmall, state, lead = carry
    lead_block = pl.BlockSpec((chunks, 8, lanes), lambda p, s: (p, 0, 0))

    def by_block(shape):
        return pl.BlockSpec(shape, lambda p, s: (p * size + (first + count - 1 - s), 0))

    return pl.pallas_call(
        partial(mixer_backward_kernel, heads=heads, inner=inner, taps=taps, fresh=fresh),
        grid=(part, count),
        in_specs=[
            pl.BlockSpec(
                (chunks, ext_rows, lanes), lambda p, s: (p * size + (first + count - 1 - s), 0, 0)
            ),
            by_block((piece, lanes)),
            by_block((piece, lanes)),
            by_block((piece, inner)),
            by_block((state_dim, inner)),
            by_block((piece, inner)),
            whole(small.shape),
            whole(head.shape),
            whole(skip.shape),
            whole(summing.shape),
            ANY if fresh else by_part((state_dim, inner)),
            ANY if fresh else lead_block,
            whole(dsmall.shape),
            whole(dgain.shape),
            ANY,
        ],
        out_specs=[
            by_block((piece, wide)),
            whole((8, conv_dim)),
            by_part((state_dim, inner)),
            lead_block,
        ],
        out_shape=[
            jax.ShapeDtypeStruct((part * size * piece, wide), bf16),
            jax.ShapeDtypeStruct((8, conv_dim), f32),
            jax.ShapeDtypeStruct((part * state_dim, inner), f32),
            jax.ShapeDtypeStruct((part * chunks, 8, lanes), f32),
        ],
        scratch_shapes=[
            pltpu.VMEM((state_dim, inner), f32),
            pltpu.VMEM((chunks, ext_rows, lanes), f32),
            pltpu.VMEM((piece, inner), f32),
            pltpu.VMEM((piece, inner), bf16),
            pltpu.VMEM((piece, inner), bf16),
            pltpu.VMEM((piece, inner), bf16),
            pltpu.VMEM((piece, inner), bf16),
            pltpu.VMEM((piece, inner), bf16),
            pltpu.VMEM((8, inner), f32),
        ],
        input_output_aliases={14: 0} if dproj.shape[0] == part * size * piece else {},
        compiler_params=params(),
        cost_estimate=cost(1, 1, 0),
    )(*saved, small, head, skip, summing, state, lead, dsmall, dgain, dproj)


def input_grad(dims, core, tokens, dgate, dproj, small, dsmall, wg, wa, wb):
    part, size, piece, width, inner, heads, taps = dims
    rows = part * size * piece
    blocks = wa[0].shape[0]
    wide_a, wide_b = wa[0].shape[2], wb[0].shape[2]
    handed = handed_out(width, wide_a, blocks) + handed_out(width, wide_b, blocks)
    return pl.pallas_call(
        partial(input_grad_kernel, gain_row=taps + 1),
        grid=(part, size),
        in_specs=[
            SMEM,
            by_block((piece, width), size),
            by_block((piece, inner), size),
            by_block((piece, dproj.shape[1]), size),
            whole(small.shape),
            whole(dsmall.shape),
            ANY,
            ANY,
            ANY,
            ANY,
            ANY,
            ANY,
        ],
        out_specs=[by_block((piece, width), size), whole(dsmall.shape)]
        + [whole(array.shape) for array in handed],
        out_shape=[
            jax.ShapeDtypeStruct((rows, width), bf16),
            jax.ShapeDtypeStruct(dsmall.shape, f32),
        ]
        + handed,
        scratch_shapes=[
            pltpu.VMEM((piece, width), bf16),
            pltpu.VMEM((width, wide_a), f32),
            pltpu.VMEM((width, wide_b), f32),
        ]
        + weight_scratch(wg, wa, wb),
        compiler_params=params(),
        cost_estimate=cost(1, 1, 0),
    )(core, tokens, dgate, dproj, small, dsmall, *wg, *wa, *wb)


def adam(rates, sums, gate_grads, front_grads, states, heads, taps):
    outs = []
    at_refs = []
    for which, (master, first, second) in enumerate(states):
        at_refs.append(len(outs))
        outs += [jax.ShapeDtypeStruct(master.shape, f32)] * 3
    outs.append(jax.ShapeDtypeStruct(states[1][0].shape, bf16))
    outs.append(jax.ShapeDtypeStruct(states[4][0].shape, bf16))
    flat = [array for state in states for array in state]
    vmem = pl.BlockSpec(memory_space=pltpu.VMEM)
    return pl.pallas_call(
        partial(
            adam_kernel, heads=heads, taps=taps, at_refs=at_refs, arrivals=len(gate_grads)
        ),
        in_specs=[SMEM] + [vmem] * (3 * len(gate_grads) + len(flat)),
        out_specs=[vmem] * len(outs),
        out_shape=outs,
        compiler_params=pltpu.CompilerParams(vmem_limit_bytes=vmem_bytes),
        cost_estimate=cost(1, 1, 0),
    )(rates, *sums, *gate_grads, *front_grads, *flat)


def bit_count(extent):
    count = extent.bit_length() - 1
    if 1 << count != extent:
        raise ValueError(extent)
    return count


def swap(block, axis, bit):
    devices = range(lax.axis_size(axis))
    return lax.ppermute(block, axis, [(i, i ^ (1 << bit)) for i in devices])


def shifted_by(block, axis, distance):
    devices = range(lax.axis_size(axis))
    route = [(i, i + distance) for i in devices if i + distance in devices]
    return lax.ppermute(block, axis, route)


def pick(block, at, axis):
    return lax.dynamic_index_in_dim(block, at, axis, keepdims=False)


def gather_bit(block, axis, bit, at, *others):
    mine = (lax.axis_index(axis) >> bit) & 1
    other = swap(block, axis, bit)
    if others:
        other = after(other, *others)
    low = jnp.where(mine == 1, other, block)
    high = jnp.where(mine == 1, block, other)
    return jnp.stack([low, high], axis=at)


def gather_seq(shard, *others):
    block = shard
    for done, bit in enumerate(reversed(range(bit_count(lax.axis_size("seq"))))):
        block = gather_bit(block, "seq", bit, done, *(others if done == 0 else ()))
    return block.reshape((-1,) + shard.shape)


def dp_orders():
    bits = bit_count(lax.axis_size("dp"))
    return list(range(bits - 1, 0, -1)) + [0], list(range(1, bits)) + [0]


def gather_dp_bit(block, order, step, *others):
    at = sum(1 for b in order[:step] if b > order[step])
    return gather_bit(block, "dp", order[step], at, *others)


def give_half(block, axis, bit, at):
    mine = (lax.axis_index(axis) >> bit) & 1
    other = swap(pick(block, 1 - mine, at).astype(bf16), axis, bit)
    return pick(block, mine, at) + other.astype(f32)


def core_sums(send, keep):
    extent = lax.axis_size("seq")
    bits = bit_count(lax.axis_size("dp")) - 1
    shape = (2,) * bits + (extent, -1, send.shape[2])
    other = swap(send, "dp", 0)
    return keep.reshape(shape), other.reshape(shape)


def core_and_next(keep, other, order):
    bit = order[-2]
    at = sum(1 for b in order[:-2] if b > bit)
    mine = (lax.axis_index("dp") >> bit) & 1
    sent = pick(keep, 1 - mine, at) + pick(other, 1 - mine, at).astype(f32)
    arrived = swap(sent.astype(bf16), "dp", bit)
    return pick(keep, mine, at) + pick(other, mine, at).astype(f32), arrived


def scatter_dp_bit(block, order, step):
    bit = order[-1 - step]
    return give_half(block, "dp", bit, sum(1 for b in order[: len(order) - 1 - step] if b > bit))


def scatter_seq(block, *others):
    extent = lax.axis_size("seq")
    place = lax.axis_index("seq")
    arrivals = [pick(block, place, 0)]
    for distance in range(1, extent):
        sent = pick(block, lax.rem(place + distance, extent), 0).astype(bf16)
        if others and distance == extent - 1:
            sent = after(sent, *others)
        route = [(i, (i + distance) % extent) for i in range(extent)]
        arrivals.append(lax.ppermute(sent, "seq", route))
    return arrivals


def sum_bits(block, axis, bits):
    for bit in bits:
        block = block + swap(block, axis, bit)
    return block


def seq_groups(size):
    extent = lax.axis_size("seq")
    if size == extent:
        return None
    return [list(range(at, at + size)) for at in range(0, extent, size)]


def to_sequences(block, part, size):
    if size > 1:
        block = lax.all_to_all(
            block, "seq", 0, 0, axis_index_groups=seq_groups(size), tiled=True
        )
    piece, width = block.shape[1:]
    block = block.reshape(size, part, piece, width)
    if part > 1:
        block = block.transpose(1, 0, 2, 3)
    return block.reshape(-1, width)


def to_pieces(rows, part, size, piece):
    block = rows.reshape(part, size, piece, -1)
    if part > 1:
        block = block.transpose(1, 0, 2, 3)
    block = block.reshape(part * size, piece, -1)
    if size > 1:
        block = lax.all_to_all(
            block, "seq", 0, 0, axis_index_groups=seq_groups(size), tiled=True
        )
    return block


def after(value, *others):
    return lax.optimization_barrier((value,) + others)[0]


def padded(block, rows, columns):
    return jnp.pad(block, ((0, rows - block.shape[0]), (0, columns - block.shape[1])))


def summing_matrix(inner, heads):
    columns = np.zeros((inner, lanes), np.float32)
    columns[np.arange(inner), np.arange(inner) // (inner // heads)] = 1.0
    return jnp.asarray(columns, bf16)


def local(
    layer_in,
    out_grad,
    norm_gain,
    in_weight,
    conv_params,
    gate_gain,
    out_weight,
    head_params,
    norm_first,
    norm_second,
    in_first,
    in_second,
    conv_first,
    conv_second,
    gate_first,
    gate_second,
    out_first,
    out_second,
    head_first,
    head_second,
    step_count,
    hyper,
):
    seq_count, piece, width = layer_in.shape
    seq_extent = lax.axis_size("seq")
    me = lax.axis_index("dp") * seq_extent + lax.axis_index("seq")
    step_float = step_count[0].astype(f32)
    scales = 1.0 / (1.0 - hyper[1:3] ** step_float)
    place = lax.axis_index("seq")
    rates = jnp.concatenate([hyper, scales, jnp.stack([me.astype(f32), place.astype(f32)])])
    core = (lax.axis_index("dp") & 1).astype(jnp.int32)[None]
    owners = lax.axis_size("dp") * seq_extent
    size = math.gcd(seq_extent, seq_count)
    part = seq_count // size
    groups = seq_extent // size
    inner = out_weight.shape[0] * owners
    heads = head_params.shape[1]
    tap_rows, conv_own = conv_params.shape
    taps = tap_rows - 1
    conv_dim = conv_own * owners
    state_dim = (conv_dim - inner) // 2
    own_rows = in_weight.shape[0]
    gate_own = gate_gain.shape[0]
    wide_a = min(1024, inner)
    dims = (part, size, piece, width, inner, heads, taps)

    head = padded(head_params, 8, lanes)
    skip = jnp.repeat(head_params[2], inner // heads)[None, :]
    summing = summing_matrix(inner, heads)

    in_own = padded(in_weight, own_rows, inner + conv_dim + lanes)
    out_own = out_weight.reshape(2, own_rows, width)
    own_small = jnp.concatenate(
        [
            padded(conv_params, tap_rows, lanes),
            padded(norm_gain[None, :], 1, lanes),
            padded(gate_gain[None, :], 1, lanes),
        ]
    )
    shard = [in_own, out_own[0], out_own[1]]
    half = width // 6
    both = jnp.concatenate([layer_in, out_grad[:, :, :half]], axis=2)
    second = lax.optimization_barrier(out_grad[:, :, half:])
    if own_rows >= tap_rows + 2:
        shard = shard + [padded(own_small, own_rows, lanes)]
        shard = lax.optimization_barrier(jnp.concatenate(shard, axis=1)).astype(bf16)
        gathered = gather_seq(shard, both, second, head, skip)
        seq_small = gathered[:, : tap_rows + 2, -lanes:]
    else:
        shard = lax.optimization_barrier(jnp.concatenate(shard, axis=1)).astype(bf16)
        gathered = gather_seq(shard)
        seq_small = gather_seq(padded(own_small, 8, lanes).astype(bf16))[:, : tap_rows + 2]
    tokens = to_sequences(after(both, shard), part, size)
    small = jnp.zeros((8, conv_dim), bf16)
    group = lax.axis_index("dp")
    for at, rows, count in (
        (0, tap_rows, conv_own),
        (tap_rows, 1, own_rows),
        (tap_rows + 1, 1, gate_own),
    ):
        piece_rows = jnp.concatenate(
            [seq_small[z, at : at + rows, :count] for z in range(seq_extent)], axis=1
        )
        small = lax.dynamic_update_slice(small, piece_rows, (at, group * seq_extent * count))
    front_end = inner + conv_dim + lanes
    wg = gathered[:, :, :inner]
    wa = gathered[:, :, inner : inner + wide_a]
    wb = gathered[:, :, inner + wide_a : front_end]
    wo = jnp.stack(
        [
            gathered[:, :, front_end : front_end + width],
            gathered[:, :, front_end + width : front_end + 2 * width],
        ],
        axis=1,
    ).reshape(-1, 2 * own_rows, width)
    order_a, order_b = dp_orders()
    last = len(order_a) - 1
    for step in range(last):
        wa = gather_dp_bit(wa, order_a, step)
        wb = gather_dp_bit(wb, order_b, step)
    small = sum_bits(small, "dp", order_a[:-1])
    for step in range(last):
        if step == 1:
            wg, wo = after((wg, wo), wa, wb, small)
        if step < last - 1:
            wg = gather_dp_bit(wg, order_a, step)
            wo = gather_dp_bit(wo, order_b, step)

    def core_halves(block):
        block = block.reshape(owners // 2 // seq_extent, -1, block.shape[-1])
        return block, swap(block, "dp", 0)

    wb = core_halves(wb)
    wa = core_halves(wa)
    small = sum_bits(after(small, tokens, wa, wb, head, skip), "dp", [0]).astype(f32)
    cots_b = to_sequences(after(second, tokens), part, size)

    edge = core
    if groups > 1:
        edge = tokens.reshape(part, size * piece, -1)[:, size * piece - 8 :, :width]
        edge = shifted_by(edge, "seq", size).reshape(part * 8, width)

    def forward(start, kept, blocks):
        weights = (wa, wb, small, head, skip)
        grouped = groups > 1
        return mixer_forward(dims, core, tokens, *weights, edge, start, grouped, kept, blocks)

    start = core
    if groups > 1:
        first_out = forward(jnp.zeros((part * state_dim, inner), f32), None, (0, size))
        cum_last = first_out[3].reshape(part, size, piece, lanes)[:, :, piece - 1, :heads]
        decay = jnp.exp2(jnp.sum(cum_last, axis=1))
        decay = jnp.repeat(decay, inner // heads, axis=1)[:, None, :]

        def relay(ends, distance):
            ends = ends.reshape(part, state_dim, inner)
            carried = jnp.zeros_like(ends)
            for _ in range(groups - 1):
                sent = (decay * carried + ends).astype(bf16)
                carried = shifted_by(sent, "seq", distance).astype(f32)
            return carried.reshape(part * state_dim, inner)

        start = relay(first_out[6], size)
    normed, ext, dtr, cum, y, sin, _, _ = forward(start, None, (0, size))
    wg = core_halves(gather_dp_bit(wg, order_a, last - 1, normed))
    wo = core_halves(gather_dp_bit(wo, order_b, last - 1, normed))
    layer_rows, dy, dgate, dgain, *handed = gate_step(
        dims, core, normed, tokens, cots_b, y, wg, wo, small
    )
    layer_out = to_pieces(layer_rows, part, size, piece)
    consts = (small, head, skip, summing, dgain)
    saved = (ext, dtr, cum, y, sin, dy)

    def backward(carry, blocks, fresh=False):
        return list(mixer_backward(dims, saved, consts, carry, blocks, fresh))

    def fresh_carry():
        if groups == 1:
            return (core, head, core, core)
        lead = jnp.zeros((part * (conv_dim // lanes), 8, lanes), f32)
        first_out = (core, head, jnp.zeros((part * state_dim, inner), f32), lead)
        first_out = backward(first_out, (0, size))
        return (core, head, relay(first_out[2], -size), lead)

    calls = [(size - 1, 1), (size - 2, 1), (0, size - 2)]
    g_out = core_sums(*handed[:2])
    g_gate = core_sums(*handed[2:])
    carry = backward(fresh_carry(), calls[0], groups == 1)
    carry[2], g_out, g_gate = lax.optimization_barrier((carry[2], g_out, g_gate))
    g_out = core_and_next(*g_out, order_a)
    g_gate = core_and_next(*g_gate, order_b)
    carry = backward(carry, calls[1])
    carry[2], g_out, g_gate = lax.optimization_barrier((carry[2], g_out, g_gate))
    g_out = g_out[0] + g_out[1].astype(f32)
    g_gate = g_gate[0] + g_gate[1].astype(f32)
    for step in range(2, last + 1):
        g_out = scatter_dp_bit(g_out, order_a, step)
        g_gate = scatter_dp_bit(g_gate, order_b, step)
    carry = backward(carry, calls[2])
    carry[0], g_out, g_gate = lax.optimization_barrier((carry[0], g_out, g_gate))
    g_rest = scatter_seq(
        jnp.concatenate([g_gate, g_out[:, :own_rows], g_out[:, own_rows:]], axis=2)
    )
    dproj, dsmall, _, lead = carry
    if groups > 1:
        lead = shifted_by(lead.astype(bf16), "seq", -size).astype(f32)
        lead = lead.reshape(part, -1, 8, lanes).transpose(0, 2, 1, 3).reshape(part, 8, conv_dim)
        fixes = []
        for row in range(taps - 1):
            terms = [small[tap] * lead[:, row - tap] for tap in range(row + 1)]
            fixes.append(sum(terms[1:], terms[0]))
        fix = jnp.pad(jnp.stack(fixes, axis=1), ((0, 0), (0, 0), (0, lanes)))
        dproj = dproj.reshape(part, size * piece, conv_dim + lanes)
        ends = dproj[:, size * piece - (taps - 1) :].astype(f32) + fix
        dproj = dproj.at[:, size * piece - (taps - 1) :].set(ends.astype(bf16))
        dproj = dproj.reshape(-1, conv_dim + lanes)
    tokens = after(tokens, layer_out, dproj)
    dx, dsmall, *handed = input_grad(dims, core, tokens, dgate, dproj, small, dsmall, wg, wa, wb)
    dx, dsmall, handed, g_rest = lax.optimization_barrier((dx, dsmall, handed, g_rest))
    g_a = core_sums(*handed[:2])
    g_b = core_sums(*handed[2:])
    g_a = core_and_next(*g_a, order_a)
    g_b = core_and_next(*g_b, order_b)
    dsmall = after(dsmall, g_a[0], g_b[0])
    g_a = g_a[0] + g_a[1].astype(f32)
    g_b = g_b[0] + g_b[1].astype(f32)
    for step in range(2, last + 1):
        g_a = scatter_dp_bit(g_a, order_a, step)
        g_b = scatter_dp_bit(g_b, order_b, step)
    pieces = to_pieces(dx, part, size, piece)
    in_grad = out_grad.astype(f32) + pieces.astype(f32)
    g_front = scatter_seq(jnp.concatenate([g_a, g_b], axis=2), pieces)
    dsmall = sum_bits(dsmall, "dp", order_a[::-1])
    slab_wide = -(-max(3 * lanes, seq_extent * max(conv_own, own_rows, gate_own)) // lanes) * lanes
    slab = [
        padded(
            lax.dynamic_slice(
                dsmall, (at, group * seq_extent * count), (rows, seq_extent * count)
            ),
            rows,
            slab_wide,
        )
        for at, rows, count in (
            (0, tap_rows, conv_own),
            (tap_rows, 1, own_rows),
            (tap_rows + 1, 1, gate_own),
        )
    ]
    dsmall = jnp.concatenate(slab + [dsmall[tap_rows + 2 :, :slab_wide]])
    sums = [dsmall]
    for distance in range(1, seq_extent):
        route = [(i, (i + distance) % seq_extent) for i in range(seq_extent)]
        sums.append(lax.ppermute(dsmall, "seq", route))

    states = (
        (norm_gain[None, :], norm_first[None, :], norm_second[None, :]),
        (in_weight, in_first, in_second),
        (conv_params, conv_first, conv_second),
        (gate_gain[None, :], gate_first[None, :], gate_second[None, :]),
        (out_weight, out_first, out_second),
        (head_params, head_first, head_second),
    )
    new = adam(rates, sums, g_rest, g_front, states, heads, taps)
    new = [array[0] if array.shape[0] == 1 else array for array in new]
    return (layer_out, in_grad, *new)


def solution(mesh):
    in_specs = (
        P("dp", "seq", None),
        P("dp", "seq", None),
        P(("dp", "seq")),
        P(("dp", "seq"), None),
        P(None, ("dp", "seq")),
        P(("dp", "seq")),
        P(("dp", "seq"), None),
        P(),
        P(("dp", "seq")),
        P(("dp", "seq")),
        P(("dp", "seq"), None),
        P(("dp", "seq"), None),
        P(None, ("dp", "seq")),
        P(None, ("dp", "seq")),
        P(("dp", "seq")),
        P(("dp", "seq")),
        P(("dp", "seq"), None),
        P(("dp", "seq"), None),
        P(),
        P(),
        P(),
        P(),
    )
    out_specs = (
        P("dp", "seq", None),
        P("dp", "seq", None),
        P(("dp", "seq")),
        P(("dp", "seq")),
        P(("dp", "seq")),
        P(("dp", "seq"), None),
        P(("dp", "seq"), None),
        P(("dp", "seq"), None),
        P(None, ("dp", "seq")),
        P(None, ("dp", "seq")),
        P(None, ("dp", "seq")),
        P(("dp", "seq")),
        P(("dp", "seq")),
        P(("dp", "seq")),
        P(("dp", "seq"), None),
        P(("dp", "seq"), None),
        P(("dp", "seq"), None),
        P(),
        P(),
        P(),
        P(("dp", "seq"), None),
        P(("dp", "seq"), None),
    )
    return jax.shard_map(local, mesh=mesh, in_specs=in_specs, out_specs=out_specs, check_vma=False)
```
